32 devices in a mesh: fsdp: 32 (over z, y, x, core).
Axes of the slice: x: 2, y: 2, z: 4, core: 2. Of those that a mesh axis runs over, the one named last changes fastest.
Arguments:
- hidden: bfloat16 [32768, 768], P('fsdp'), may hold values from -6 to 6
- query_weight: bfloat16 [768, 768], P('fsdp'), may hold values from -0.21875 to 0.21875
- key_weight: bfloat16 [768, 768], P('fsdp'), may hold values from -0.21875 to 0.21875
- value_weight: bfloat16 [768, 768], P('fsdp'), may hold values from -0.21875 to 0.21875
- output_weight: bfloat16 [768, 768], P('fsdp'), may hold values from -0.875 to 0.875
- relative_table: bfloat16 [512, 768], P('fsdp'), may hold values from -6 to 6
- first_gain: bfloat16 [768], P('fsdp'), may hold values from 0.099609375 to 1.8984375
- first_shift: bfloat16 [768], P('fsdp'), may hold values from -2 to 2
- expand_weight: bfloat16 [768, 3072], P('fsdp'), may hold values from -0.21875 to 0.21875
- contract_weight: bfloat16 [3072, 768], P('fsdp'), may hold values from -0.21875 to 0.21875
- second_gain: bfloat16 [768], P('fsdp'), may hold values from 0.099609375 to 1.8984375
- second_shift: bfloat16 [768], P('fsdp'), may hold values from -2 to 2
- segment_ids: int32 [32768], P('fsdp'), may hold values from 0 to 1024, as said below
- valid: int32 [32768], P('fsdp'), may hold values from 0 to 1, as said below
- cotangent: bfloat16 [32768, 768], P('fsdp'), may hold values from -6 to 6
Outputs:
- output: bfloat16 [32768, 768], P('fsdp')
- input_grad: bfloat16 [32768, 768], P('fsdp')
- grad_query: float32 [768, 768], P('fsdp')
- grad_key: float32 [768, 768], P('fsdp')
- grad_value: float32 [768, 768], P('fsdp')
- grad_output: float32 [768, 768], P('fsdp')
- grad_table: float32 [512, 768], P('fsdp')
- grad_first_gain: float32 [768], P('fsdp')
- grad_first_shift: float32 [768], P('fsdp')
- grad_expand: float32 [768, 3072], P('fsdp')
- grad_contract: float32 [3072, 768], P('fsdp')
- grad_second_gain: float32 [768], P('fsdp')
- grad_second_shift: float32 [768], P('fsdp')
- rms_residual: float32 [], replicated
- rms_sublayer: float32 [], replicated
The draws below stay inside these ranges and needn't reach their ends.
Inputs may be any that keep to these rules, and one draw needn't show every extreme that they name: `segment_ids`: within each packed row of 1024 tokens the ids never fall and start at 0; the real tokens of a row come first and padding tokens carry the id 1024; documents are 1 to 1024 tokens long. `valid`: each packed row of 1024 tokens has its 1 entries on a prefix of 341 tokens or more.
All inputs are finite; a program needn't handle non-finite values.
Results may differ from the reference program's by a relative error of at most 0.015.
Values may be sent and summed in bfloat16 or wider, within the bound.
No kernel may reach another device: no remote copies, remote signals or barrier semaphores. Data moves between devices by JAX's collectives and lax.ppermute only.
A program may use at most 192 MiB of HBM per device.

```python
import math
import jax
import jax.numpy as jnp
import numpy as np
from jax import lax

D = 768
HEADS = 12
HEAD_DIM = 64
FF = 3072
BUCKETS = 256
LEN = 1024
TOK_DEV = 1024
TOKENS = 32768


def packing(key):
    rows = TOKENS // LEN
    base = jax.random.fold_in(key, 11)
    first, second, third = jax.random.split(base, 3)
    spread = jax.random.randint(first, (rows, 1), 2, 10)
    noise = jax.random.randint(second, (rows, LEN), 0, 1 << 20)
    position = jnp.arange(LEN, dtype=jnp.int32)[None, :]
    starts = jnp.bitwise_and(noise, jnp.left_shift(jnp.int32(1), spread) - 1) == 0
    starts = jnp.logical_or(starts, position == 0)
    segment = jnp.cumsum(starts.astype(jnp.int32), axis=1) - 1
    row_index = jnp.arange(rows, dtype=jnp.int32)[:, None]
    rising = LEN // 3 + (LEN - LEN // 3) * row_index // max(rows - 1, 1)
    jitter = jax.random.randint(third, (rows, 1), 0, LEN // 8 + 1)
    kept = jnp.clip(rising - jitter, LEN // 3, LEN)
    kept = jnp.where(row_index == 0, LEN // 3, kept)
    inside = position < kept
    segment = jnp.where(inside, segment, LEN)
    return (segment.reshape(-1).astype(jnp.int32), inside.astype(jnp.int32).reshape(-1))


def draw_segment_ids(key, part):
    return packing(key)[0]


def draw_valid(key, part):
    return packing(key)[1]


def with_spikes(values, stream_key, source, target, blocks, factor):
    owner, partner = [(jnp.arange(values.shape[dim]) // (values.shape[dim] // blocks)).reshape([-1 if axis == dim else 1 for axis in range(values.ndim)]) for dim in (source, target)]
    chosen = jax.random.permutation(stream_key, blocks)[partner]
    strong = (owner == chosen) | (owner == (partner + blocks // 2) % blocks)
    return jnp.where(strong, factor * values, values)


def steps_of(rng, dims, cuts, low, largest):
    factor_of = 1.0
    for dim, parts in cuts:
        steps = jax.random.uniform(jax.random.fold_in(jax.random.fold_in(rng, 6), dim), (parts,), jnp.float32, low / len(cuts), largest / len(cuts))
        factor_of = factor_of * jnp.repeat(jnp.exp(steps), dims[dim] // parts).reshape((-1,) + (1,) * (len(dims) - 1 - dim))
    return factor_of


def normal_values(key, shape, scale, bound, shards=(), held_as=jnp.bfloat16):
    entries = jax.random.normal(key, shape, jnp.float32) * scale
    if len(shards) > 0:
        entries = steps_of(key, shape, shards, -0.22, 0.18) * entries
    return jnp.clip(entries, min=-bound, max=bound).astype(held_as)


def gaussian_with(rng, dims, scale, reach, cuts, heavy, held_as=jnp.bfloat16):
    drawn = scale * jax.random.normal(rng, dims, jnp.float32)
    if cuts:
        drawn = drawn * steps_of(rng, dims, cuts, -0.22, 0.18)
    return jnp.clip(with_spikes(drawn, jax.random.fold_in(rng, 3), *heavy), -reach, reach).astype(held_as)


def setup_inputs(seed: int = 0) -> dict:
    streams_of = jax.random.split(jax.random.key(seed), 16)
    return {
        "hidden": gaussian_with(streams_of[0], (TOKENS, D), 1.0, 6.0, ((0, 32),), (0, 1, 32, 2.75)),
        "query_weight": normal_values(streams_of[1], (D, D), D ** -0.5, 0.21875, ((0, 32),)),
        "key_weight": normal_values(streams_of[2], (D, D), D ** -0.5, 0.21875, ((0, 32),)),
        "value_weight": normal_values(streams_of[3], (D, D), D ** -0.5, 0.21875, ((0, 32),)),
        "output_weight": normal_values(streams_of[4], (D, D), (D // 16) ** -0.5, 0.875, ((0, 32),)),
        "relative_table": normal_values(streams_of[5], (2 * BUCKETS, D), 1.0, 6.0, ((0, 32),)),
        "first_gain": jnp.clip(1.0 + 0.18 * jax.random.normal(streams_of[6], (D,), jnp.float32), 0.099609375, 1.8984375).astype(jnp.bfloat16),
        "first_shift": normal_values(streams_of[7], (D,), 0.4, 2.0, ((0, 32),)),
        "expand_weight": normal_values(streams_of[8], (D, FF), D ** -0.5, 0.21875, ((0, 32),)),
        "contract_weight": normal_values(streams_of[9], (FF, D), (FF // 4) ** -0.5, 0.21875, ((0, 32),)),
        "second_gain": jnp.clip(1.0 + 0.18 * jax.random.normal(streams_of[10], (D,), jnp.float32), 0.099609375, 1.8984375).astype(jnp.bfloat16),
        "second_shift": normal_values(streams_of[11], (D,), 0.4, 2.0, ((0, 32),)),
        "segment_ids": draw_segment_ids(jax.random.fold_in(streams_of[15], 71), 0),
        "valid": draw_valid(jax.random.fold_in(streams_of[15], 71), 0),
        "cotangent": normal_values(streams_of[14], (TOKENS, D), 1.0, 6.0, ((0, 32),)),
    }


NORM_EPS = 1e-07
MASKED = -1e+30

@jax.custom_vjp
def low(v):
    return lax.optimization_barrier(v.astype(jnp.bfloat16)).astype(jnp.float32)

@jax.custom_vjp
def low_back(v):
    return v

def low_keep(v):
    return (low(v), None)

def low_pass(kept, grad):
    return (grad,)

def back_keep(v):
    return (v, None)

def back_low(kept, grad):
    return (low(grad),)
low.defvjp(low_keep, low_pass)
low_back.defvjp(back_keep, back_low)

def bucket_index(offsets, buckets):
    middle = buckets // 2
    limit = 2 * buckets
    magnitude = np.abs(offsets)
    inside = (offsets < middle) & (offsets > -middle)
    clipped = np.where(inside, middle - 1, magnitude)
    logged = np.ceil(np.log(clipped / middle) / np.log((limit - 1) / middle) * (middle - 1)) + middle
    bucket = np.where(magnitude <= middle, offsets, (logged * np.sign(offsets)).astype(np.int32))
    return np.clip(bucket + buckets, 0, 2 * buckets - 1).astype(np.int32)

def layer_norm(values, gain, shift):
    centered = values - lax.optimization_barrier(jnp.mean(values, axis=-1, keepdims=True))
    variance = lax.optimization_barrier(jnp.mean(centered * centered, axis=-1, keepdims=True))
    return centered * lax.rsqrt(variance + NORM_EPS) * gain + shift

def matmul(left, right):
    return jnp.dot(left, right, precision=lax.Precision.HIGHEST)

def separate_heads(values):
    return values.reshape(values.shape[0], HEADS, HEAD_DIM).transpose(1, 0, 2)

def attend(query, key_rows, value_rows, position_key, pos_query, segment, index):
    scale = 1.0 / math.sqrt(3 * HEAD_DIM)
    query_per_head = separate_heads(query)
    key_heads = separate_heads(key_rows)
    value_heads = separate_heads(value_rows)
    content = jnp.einsum('hid,hjd->hij', query_per_head, key_heads, precision=lax.Precision.HIGHEST)
    gathered_along = low_back(jnp.einsum('qys,qls->qyl', query_per_head, separate_heads(position_key), precision=lax.Precision.HIGHEST))
    against = low_back(jnp.einsum('hjd,hbd->hjb', key_heads, separate_heads(pos_query), precision=lax.Precision.HIGHEST))
    spread_index = jnp.broadcast_to(index, (HEADS, LEN, LEN))
    picked_along = jnp.take_along_axis(gathered_along, spread_index, axis=2)
    picked_against = jnp.swapaxes(jnp.take_along_axis(against, spread_index, axis=2), 1, 2)
    allowed = segment[:, None] == segment[None, :]
    scores = low_back(jnp.where(allowed[None], (content + picked_along + picked_against) * scale, MASKED))
    probs = jax.nn.softmax(scores, axis=-1)
    mixed = jnp.einsum('hij,hjd->ihd', low(probs), value_heads, precision=lax.Precision.HIGHEST)
    return mixed.reshape(LEN, HEADS * HEAD_DIM)

def layer_forward(params, inputs, segment):
    query_weight, key_weight, value_weight, output_weight, relative_table, first_gain, first_shift, expand_weight, contract_weight, second_gain, second_shift = params
    query = low(low_back(matmul(inputs, query_weight)))
    key_rows = low(low_back(matmul(inputs, key_weight)))
    value_rows = low(low_back(matmul(inputs, value_weight)))
    position_key = low(low_back(matmul(relative_table, key_weight)))
    pos_query = low(low_back(matmul(relative_table, query_weight)))
    offsets = np.arange(LEN)[:, None] - np.arange(LEN)[None, :]
    index = jnp.asarray(bucket_index(offsets, BUCKETS), dtype=jnp.int32)
    count = inputs.shape[0] // LEN
    width = inputs.shape[1]

    def one_row(query_row, key_row, value_row, segment_row):
        return attend(query_row, key_row, value_row, position_key, pos_query, segment_row, index)
    mixed = jax.vmap(one_row)(query.reshape(count, LEN, width), key_rows.reshape(count, LEN, width), value_rows.reshape(count, LEN, width), segment.reshape(count, LEN))
    attended = low(low_back(mixed.reshape(inputs.shape[0], width)))
    branch = low_back(matmul(attended, output_weight))
    first_sum = inputs + branch
    normed = layer_norm(first_sum, first_gain, first_shift)
    expanded = low_back(matmul(low(normed), expand_weight))
    activated = low(jax.nn.gelu(expanded, approximate=False))
    branch_two = low_back(matmul(activated, contract_weight))
    second_sum = normed + branch_two
    return (layer_norm(second_sum, second_gain, second_shift), (second_sum, branch_two))

def reference(hidden, query_weight, key_weight, value_weight, output_weight, relative_table, first_gain, first_shift, expand_weight, contract_weight, second_gain, second_shift, segment_ids, valid, cotangent):
    params = tuple((weight_arg.astype(jnp.float32) for weight_arg in (query_weight, key_weight, value_weight, output_weight, relative_table, first_gain, first_shift, expand_weight, contract_weight, second_gain, second_shift)))
    width = hidden.shape[1]
    groups = hidden.shape[0] // TOK_DEV
    inputs = hidden.astype(jnp.float32).reshape(groups, TOK_DEV, width)
    segments = segment_ids.reshape(groups, TOK_DEV)
    masks = valid.reshape(groups, TOK_DEV)
    upstreams = cotangent.astype(jnp.float32).reshape(groups, TOK_DEV, width)

    def one_group(carry, item):
        block_in, block_segment, block_mask, block_upstream = item

        def forward(weights, values):
            return layer_forward(weights, values, block_segment)
        result, back, extra = jax.vjp(forward, params, block_in, has_aux=True)
        mask = block_mask.astype(jnp.float32)[:, None]
        grads, d_input = back(block_upstream * mask)
        second_sum, branch_two = extra
        stats = jnp.stack([jnp.sum(mask * second_sum * second_sum), jnp.sum(mask * branch_two * branch_two)])
        carry = jax.tree.map(lambda left, right: left + right, carry, (grads, stats))
        return (carry, (result.astype(jnp.bfloat16), d_input.astype(jnp.bfloat16)))
    init = (jax.tree.map(jnp.zeros_like, params), jnp.zeros((2,), jnp.float32))
    (grads, stats), (results, d_inputs) = lax.scan(one_group, init, (inputs, segments, masks, upstreams))
    whole = jnp.float32(hidden.shape[0] * width)
    rms_residual = jnp.sqrt(stats[0] / whole)
    rms_sublayer = jnp.sqrt(stats[1] / whole)
    return (results.reshape(hidden.shape), d_inputs.reshape(hidden.shape), grads[0], grads[1], grads[2], grads[3], grads[4], grads[5], grads[6], grads[7], grads[8], grads[9], grads[10], rms_residual, rms_sublayer)
```

```python
from functools import partial
import math

import jax
import jax.numpy as jnp
import numpy as np
from jax import lax
from jax.experimental import pallas as pl
from jax.experimental.pallas import tpu as pltpu
from jax.sharding import PartitionSpec as P

bf = jnp.bfloat16
f4 = jnp.float32
HEADS = 12
BUCKETS = 256
LEN = 1024
TILE = 128
CH = 256
NCH = LEN // CH
SCALE = 1.0 / math.sqrt(192.0)
NORM_EPS = 1e-07
MASKED = -1e30
ROWS_FIRST = (((0,), (0,)), ((), ()))
ROWS_LAST = (((1,), (1,)), ((), ()))
NT = ROWS_LAST
NN = (((1,), (0,)), ((), ()))


def bucket_index(offsets, buckets):
    middle = buckets // 2
    limit = 2 * buckets
    magnitude = np.abs(offsets)
    inside = (offsets < middle) & (offsets > -middle)
    clipped = np.where(inside, middle - 1, magnitude)
    logged = (
        np.ceil(np.log(clipped / middle) / np.log((limit - 1) / middle) * (middle - 1)) + middle
    )
    bucket = np.where(magnitude <= middle, offsets, (logged * np.sign(offsets)).astype(np.int32))
    return np.clip(bucket + buckets, 0, 2 * buckets - 1).astype(np.int32)


def layer_norm(values, gain, shift):
    centered = values - jnp.mean(values, axis=-1, keepdims=True)
    variance = jnp.mean(centered * centered, axis=-1, keepdims=True)
    return centered * lax.rsqrt(variance + NORM_EPS) * gain + shift


def gelu_exact(values):
    return jax.nn.gelu(values, approximate=False)


def dot(a,b,dims=NN): return lax.dot_general(a,b,dims,preferred_element_type=f4)
def al(x,m): return pl.multiple_of(x,m)
def iotas():
    r=lax.broadcasted_iota(jnp.int32,(TILE,TILE),0); c=lax.broadcasted_iota(jnp.int32,(TILE,TILE),1)
    return r,c
def fwd_kernel(b_ref,q_ref,k_ref,v_ref,rk_ref,rq_ref,segb_ref,segr_ref,
               att_ref,inv_ref,p_ref, qm,km,vj,xs,ys,sc,mx,sm,acc):
    r,c=iotas()
    eye=(r==c).astype(f4).astype(bf); rev=(r+c==TILE-1).astype(f4).astype(bf)
    early=(r+c)<TILE
    half=lax.broadcasted_iota(jnp.int32,(LEN,TILE),1)<64
    zero=jnp.zeros((LEN,TILE),bf)
    q=q_ref[...]; k=k_ref[...]; v=v_ref[...]
    for h in range(2):
        m=half if h==0 else jnp.logical_not(half)
        qm[h]=jnp.where(m,q,zero); km[h]=jnp.where(m,k,zero)
        vj[h,:,:TILE]=jnp.where(m,v,zero)
        for t in range(LEN//TILE): vj[h,t*TILE:(t+1)*TILE,TILE:]=rev
    halft=lax.broadcasted_iota(jnp.int32,(CH,TILE),1)<64
    def prod(ic,_):
        lo=b_ref[ic]; hi=b_ref[NCH+ic]
        rows=pl.ds(al(ic*CH,CH),CH)
        def one(d,_):
            w=pl.ds(al((d+4)*CH,CH),CH)
            for h in range(2):
                xs[h,rows,w]=dot(qm[h,rows,:],rk_ref[w,:],NT).astype(bf)
                ys[h,rows,w]=dot(km[h,rows,:],rq_ref[w,:],NT).astype(bf)
            return 0
        lax.fori_loop(lo-ic-1,hi-ic,one,0)
        return 0
    lax.fori_loop(0,NCH,prod,0)
    def skewed(ref,h,row,kk):
        rr=pl.ds(al(row*TILE,TILE),TILE)
        a=ref[h,rr,pl.ds(al((kk+8)*TILE,TILE),TILE)]
        b=ref[h,rr,pl.ds(al((kk+7)*TILE,TILE),TILE)]
        return pltpu.roll(jnp.where(early,a,b),0,1,stride=1,stride_axis=0)
    def chunk(ic,_):
        lo=b_ref[ic]; hi=b_ref[NCH+ic]
        rows=pl.ds(al(ic*CH,CH),CH)
        for h in range(2):
            mx[h]=jnp.full((CH,TILE),MASKED,f4)
            sm[h]=jnp.zeros((CH,TILE),f4)
        acc[...]=jnp.zeros((CH,TILE),f4)
        def score(jc,_):
            cols=pl.ds(al(jc*CH,CH),CH)
            segc=segr_ref[:,cols]
            for s in range(2):
                i=2*ic+s
                srow=segb_ref[pl.ds(al(i*TILE,TILE),TILE),:]
                for h in range(2):
                    aks=[]
                    for t in range(2):
                        aks.append(skewed(ys,h,2*jc+t,i-(2*jc+t)))
                    lhs=jnp.concatenate([qm[h,pl.ds(al(i*TILE,TILE),TILE),:],eye],axis=1)
                    rhs=jnp.concatenate([k_ref[cols,:],jnp.concatenate(aks,axis=0)],axis=1)
                    content=dot(lhs,rhs,NT)
                    best=mx[h,s*TILE:(s+1)*TILE,:]
                    for t in range(2):
                        along=skewed(xs,h,i,2*jc+t-i).astype(f4)
                        ok=srow==segc[:,t*TILE:(t+1)*TILE]
                        val=jnp.where(ok,content[:,t*TILE:(t+1)*TILE]+along,MASKED)
                        sc[h,s*TILE:(s+1)*TILE,pl.ds(al(jc*CH+t*TILE,TILE),TILE)]=val
                        best=jnp.maximum(best,val)
                    mx[h,s*TILE:(s+1)*TILE,:]=best
            return 0
        lax.fori_loop(lo,hi,score,0)
        for h in range(2):
            mx[h]=jnp.broadcast_to(jnp.max(mx[h],axis=1,keepdims=True),(CH,TILE))
        fac=SCALE*math.log2(math.e)
        def mix(jc,_):
            for h in range(2):
                top=mx[h]; tot=sm[h]
                for t in range(2):
                    cols=pl.ds(al(jc*CH+t*TILE,TILE),TILE)
                    e=jnp.exp2((sc[h,:,cols]-top)*fac)
                    tot=tot+e
                    res=dot(e.astype(bf),vj[h,cols,:])
                    acc[...]+=res[:,:TILE]
                    p_ref[h,rows,cols]=res[:,TILE:].astype(bf)
                sm[h]=tot
            return 0
        lax.fori_loop(lo,hi,mix,0)
        inv=[1.0/jnp.sum(sm[h],axis=1,keepdims=True) for h in range(2)]
        invp=jnp.where(halft,jnp.broadcast_to(inv[0],(CH,TILE)),jnp.broadcast_to(inv[1],(CH,TILE)))
        inv_ref[rows,:]=invp
        att_ref[rows,:]=acc[...]*invp
        return 0
    lax.fori_loop(0,NCH,chunk,0)
def attend_forward(bounds,q,k,v,rk,rq,segb,segr):
    D=q.shape[1]; np_=D//TILE
    col=lambda n: pl.BlockSpec((n,TILE),lambda p,*_:(0,p))
    return pl.pallas_call(fwd_kernel,
        grid_spec=pltpu.PrefetchScalarGridSpec(num_scalar_prefetch=1,grid=(np_,),
            in_specs=[col(LEN),col(LEN),col(LEN),col(2*LEN),col(2*LEN),
                      pl.BlockSpec((LEN,TILE),lambda p,*_:(0,0)),pl.BlockSpec((1,LEN),lambda p,*_:(0,0))],
            out_specs=[col(LEN),col(LEN),pl.BlockSpec((2,LEN,LEN),lambda p,*_:(p,0,0))],
            scratch_shapes=[pltpu.VMEM((2,LEN,TILE),bf),pltpu.VMEM((2,LEN,TILE),bf),pltpu.VMEM((2,LEN,2*TILE),bf),
                pltpu.VMEM((2,LEN,2*LEN),bf),pltpu.VMEM((2,LEN,2*LEN),bf),
                pltpu.VMEM((2,CH,LEN),f4),pltpu.VMEM((2,CH,TILE),f4),pltpu.VMEM((2,CH,TILE),f4),pltpu.VMEM((CH,TILE),f4)]),
        out_shape=[jax.ShapeDtypeStruct((LEN,D),f4),jax.ShapeDtypeStruct((LEN,D),f4),jax.ShapeDtypeStruct((2*np_,LEN,LEN),bf)],
        compiler_params=pltpu.CompilerParams(vmem_limit_bytes=58<<20),
        name="attend_forward",
    )(bounds,q,k,v,rk,rq,segb,segr)


def bwd_kernel(b_ref,q_ref,k_ref,v_ref,da_ref,att_ref,inv_ref,rk_ref,rq_ref,p_ref,
               dq_ref,dk_ref,dv_ref,gk_ref,gq_ref,
               dah,vr,krc,rkc,rqc,bdq,bda,bdk,ws,wt,gk,gq,dkt,dvt,dq,dk2,ds_,iv_):
    r,c=iotas()
    eye=(r==c).astype(f4).astype(bf); rev=(r+c==TILE-1).astype(f4).astype(bf)
    late=c>=r; early=c<=r
    half=lax.broadcasted_iota(jnp.int32,(LEN,TILE),1)<64
    zero=jnp.zeros((LEN,TILE),bf)
    low=lax.broadcasted_iota(jnp.int32,(TILE,LEN),0)<64
    zerot=jnp.zeros((TILE,LEN),bf)
    da=da_ref[...]
    dah[0]=jnp.where(half,da,zero); dah[1]=jnp.where(half,zero,da)
    das=(da.astype(f4)*inv_ref[...]).astype(bf)
    kr=[]
    for t in range(LEN//TILE):
        rows=slice(t*TILE,(t+1)*TILE)
        vr[rows,:]=dot(rev,v_ref[rows,:]).astype(bf)
        kr.append(dot(rev,k_ref[rows,:]).astype(bf))
    kr=jnp.concatenate(kr,axis=0)
    k0=jnp.where(half,kr,zero); k1=jnp.where(half,zero,kr)
    for t in range(NCH):
        krc[t,:CH,:]=k0[t*CH:(t+1)*CH]; krc[t,CH:,:]=k1[t*CH:(t+1)*CH]
    halfc=lax.broadcasted_iota(jnp.int32,(CH,TILE),1)<64
    zeroc=jnp.zeros((CH,TILE),bf)
    for t in range(2*NCH):
        rows=slice(t*CH,(t+1)*CH)
        a=rk_ref[rows,:]; b=rq_ref[rows,:]
        rkc[t,:CH,:]=jnp.where(halfc,a,zeroc); rkc[t,CH:,:]=jnp.where(halfc,zeroc,a)
        rqc[t,:CH,:]=jnp.where(halfc,b,zeroc); rqc[t,CH:,:]=jnp.where(halfc,zeroc,b)
    for ref,val in ((bdq,q_ref[...]),(bda,das),(bdk,kr)):
        vt=val.T
        v0=jnp.where(low,vt,zerot); v1=jnp.where(low,zerot,vt)
        for t in range(NCH):
            ref[t,:,:CH]=v0[:,t*CH:(t+1)*CH]; ref[t,:,CH:]=v1[:,t*CH:(t+1)*CH]
    gk[...]=jnp.zeros(gk.shape,f4); gq[...]=jnp.zeros(gq.shape,f4)
    dkt[...]=jnp.zeros(dkt.shape,f4); dvt[...]=jnp.zeros(dvt.shape,f4)
    dq[...]=jnp.zeros(dq.shape,f4); dk2[...]=jnp.zeros(dk2.shape,f4)
    def chunk(ic,_):
        lo=b_ref[2*NCH+ic]; hi=b_ref[3*NCH+ic]
        rows=pl.ds(al(ic*CH,CH),CH)
        @pl.when(hi>lo)
        def _():
            x=att_ref[rows,:]*da_ref[rows,:].astype(f4)
            ivp=inv_ref[rows,:]
            zf=jnp.zeros((CH,TILE),f4)
            ivr=pltpu.roll(ivp,64,1)
            for h in range(2):
                xm=jnp.where(halfc,x,zf) if h==0 else jnp.where(halfc,zf,x)
                ds_[h]=jnp.broadcast_to(jnp.sum(xm,axis=1,keepdims=True),(CH,TILE))
                iv_[h]=jnp.where(halfc,ivp,ivr) if h==0 else jnp.where(halfc,ivr,ivp)
            zz=jnp.zeros((CH,CH),bf)
            for h in range(2):
                for ref in (ws,wt):
                    ref[h,rows,pl.ds(al(lo*CH,CH),CH)]=zz
                    ref[h,rows,pl.ds(al((hi+1)*CH,CH),CH)]=zz
        def grad(jc,_):
            cols=pl.ds(al(jc*CH,CH),CH)
            dss=[];ps=[]
            for h in range(2):
                dp=dot(dah[h,rows,:],vr[cols,:],NT)
                pt=p_ref[h,rows,cols]
                d=ds_[h]; iv=iv_[h]
                parts=[]
                for t in range(2):
                    sl=slice(t*TILE,(t+1)*TILE)
                    parts.append((pt[:,sl].astype(f4)*((dp[:,sl]-d)*iv)).astype(bf))
                for t in range(2):
                    tt=dot(eye,parts[t],NT).astype(bf)
                    for s in range(2):
                        sr=slice(s*TILE,(s+1)*TILE)
                        ws[h,pl.ds(al(ic*CH+s*TILE,TILE),TILE),pl.ds(al((jc+1)*CH+t*TILE,TILE),TILE)]=pltpu.roll(parts[t][sr],0,1,stride=1,stride_axis=0)
                        wt[h,pl.ds(al(jc*CH+t*TILE,TILE),TILE),pl.ds(al((ic+1)*CH+s*TILE,TILE),TILE)]=pltpu.roll(tt[:,sr],1,1,stride=1,stride_axis=0)
                dss.append(jnp.concatenate(parts,axis=1)); ps.append(pt)
            dq[rows,:]+=dot(jnp.concatenate(dss,axis=1),krc[jc])
            dkt[:,cols]+=dot(bdq[ic],jnp.concatenate(dss,axis=0))
            dvt[:,cols]+=dot(bda[ic],jnp.concatenate(ps,axis=0))
            return 0
        lax.fori_loop(lo,hi,grad,0)
        return 0
    lax.fori_loop(0,NCH,chunk,0)
    def fold(ic,_):
        lo=b_ref[2*NCH+ic]; hi=b_ref[3*NCH+ic]
        rows=pl.ds(al(ic*CH,CH),CH)
        def one(d,_):
            w=pl.ds(al((d+4)*CH,CH),CH)
            for ref,mask,left,rc,outr,bd,g in ((ws,late,None,rkc,dq,bdq,gk),(wt,early,None,rqc,dk2,bdk,gq)):
                us=[]
                for h in range(2):
                    rr=[]
                    for s in range(2):
                        i=2*ic+s
                        rs=pl.ds(al(i*TILE,TILE),TILE)
                        cc=[]
                        for b in range(2):
                            j=i+2*d+b
                            x=ref[h,rs,pl.ds(al((j+2)*TILE,TILE),TILE)]
                            y=ref[h,rs,pl.ds(al((j+3)*TILE,TILE),TILE)]
                            cc.append(jnp.where(mask,x,y))
                        rr.append(jnp.concatenate(cc,axis=1))
                    us.append(jnp.concatenate(rr,axis=0))
                outr[rows,:]+=dot(jnp.concatenate(us,axis=1),rc[d+4])
                g[:,w]+=dot(bd[ic],jnp.concatenate(us,axis=0))
            return 0
        lax.fori_loop(lo-ic-1,jnp.where(hi>lo,hi-ic,lo-ic-1),one,0)
        return 0
    lax.fori_loop(0,NCH,fold,0)
    dq_ref[...]=(dq[...]*SCALE).astype(bf)
    for t in range(LEN//TILE):
        rows=slice(t*TILE,(t+1)*TILE)
        x=((dkt[:,rows].T+dk2[rows,:])*SCALE).astype(bf)
        dk_ref[rows,:]=dot(rev,x).astype(bf)
        dv_ref[rows,:]=dot(rev,dvt[:,rows].T.astype(bf)).astype(bf)
    gk_ref[...]=(gk[...]*SCALE).astype(bf)
    gq_ref[...]=(gq[...]*SCALE).astype(bf)
def attend_backward(bounds,q,k,v,da,att,inv,rkr,rq,p):
    D=q.shape[1]; np_=D//TILE
    col=lambda n: pl.BlockSpec((n,TILE),lambda p,*_:(0,p))
    colr=pl.BlockSpec((TILE,2*LEN),lambda p,*_:(p,0))
    return pl.pallas_call(bwd_kernel,
        grid_spec=pltpu.PrefetchScalarGridSpec(num_scalar_prefetch=1,grid=(np_,),
            in_specs=[col(LEN)]*6+[col(2*LEN)]*2+[pl.BlockSpec((2,LEN,LEN),lambda p,*_:(p,0,0))],
            out_specs=[col(LEN)]*3+[colr]*2,
            scratch_shapes=[pltpu.VMEM((2,LEN,TILE),bf),pltpu.VMEM((LEN,TILE),bf),pltpu.VMEM((NCH,2*CH,TILE),bf),
              pltpu.VMEM((2*NCH,2*CH,TILE),bf),pltpu.VMEM((2*NCH,2*CH,TILE),bf)]+[pltpu.VMEM((NCH,TILE,2*CH),bf)]*3+
              [pltpu.VMEM((2,LEN,LEN+2*CH),bf)]*2+[pltpu.VMEM((TILE,2*LEN),f4)]*2+[pltpu.VMEM((TILE,LEN),f4)]*2+
              [pltpu.VMEM((LEN,TILE),f4)]*2+[pltpu.VMEM((2,CH,TILE),f4)]*2),
        out_shape=[jax.ShapeDtypeStruct((LEN,D),bf)]*3+[jax.ShapeDtypeStruct((D,2*LEN),bf)]*2,
        compiler_params=pltpu.CompilerParams(vmem_limit_bytes=58<<20),
        name="attend_backward",
    )(bounds,q,k,v,da,att,inv,rkr,rq,p)


def offsets_onehot():
    index = bucket_index(LEN - np.arange(2 * LEN), BUCKETS)
    back = index.reshape(-1, TILE)[:, ::-1].reshape(-1)
    both = np.concatenate([index, back])
    table = (both[:, None] == np.arange(2 * BUCKETS)[None, :]).astype(np.float32)
    return jnp.asarray(table, dtype=bf)


def active_chunks(segment, valid):
    rows = segment.reshape(NCH, CH)
    ok = valid.reshape(NCH, CH) > 0
    first = rows[:, 0]
    last = rows[:, -1]
    over = (first[None, :] <= last[:, None]) & (last[None, :] >= first[:, None])
    real = jnp.max(jnp.where(ok, rows, -1), axis=1)
    back = (first[None, :] <= real[:, None]) & (last[None, :] >= first[:, None])
    back = back | back.T
    place = jnp.arange(NCH)[None, :]

    def limits(mask):
        lo = jnp.min(jnp.where(mask, place, NCH), axis=1)
        hi = jnp.max(jnp.where(mask, place + 1, 0), axis=1)
        return jnp.where(hi > 0, lo, 0), hi

    return jnp.concatenate(limits(over) + limits(back)).astype(jnp.int32)


def shards(
    hidden,
    query_weight,
    key_weight,
    value_weight,
    output_weight,
    relative_table,
    first_gain,
    first_shift,
    expand_weight,
    contract_weight,
    second_gain,
    second_shift,
    segment_ids,
    valid,
    cotangent,
):
    count = lax.axis_size("fsdp")
    width = hidden.shape[1]
    wide = expand_weight.shape[1]
    per = query_weight.shape[0]
    per_t = relative_table.shape[0]
    per_c = contract_weight.shape[0]
    small = jnp.concatenate([first_gain, first_shift, second_gain, second_shift])
    small = jnp.pad(small, (0, width - 4 * per))[None, :]
    pack = jnp.concatenate(
        [query_weight, key_weight, value_weight, output_weight, relative_table, small], axis=0
    )
    whole = lax.all_gather(pack, "fsdp", axis=0, tiled=False)
    part = lambda at, n: whole[:, at : at + n].reshape(count * n, width)
    query_full = part(0, per)
    key_full = part(per, per)
    value_full = part(2 * per, per)
    output_full = part(3 * per, per)
    table_full = part(4 * per, per_t)
    vectors = whole[:, 4 * per + per_t, : 4 * per].reshape(count, 4, per).transpose(1, 0, 2)
    vectors = vectors.reshape(4, count * per).astype(f4)
    gain_one, shift_one, gain_two, shift_two = vectors[0], vectors[1], vectors[2], vectors[3]
    expand_full = lax.all_gather(expand_weight, "fsdp", axis=0, tiled=True)
    contract_full = lax.all_gather(contract_weight, "fsdp", axis=0, tiled=True)

    bounds = active_chunks(segment_ids, valid)
    onehot = offsets_onehot()
    query = jnp.dot(hidden, query_full, preferred_element_type=f4).astype(bf)
    key_rows = jnp.dot(hidden, key_full, preferred_element_type=f4).astype(bf)
    value_rows = jnp.dot(hidden, value_full, preferred_element_type=f4).astype(bf)
    position_key = jnp.dot(table_full, key_full, preferred_element_type=f4).astype(bf)
    pos_query = jnp.dot(table_full, query_full, preferred_element_type=f4).astype(bf)
    along_rows = jnp.dot(onehot, position_key, preferred_element_type=f4).astype(bf)
    against_rows = jnp.dot(onehot[: 2 * LEN], pos_query, preferred_element_type=f4).astype(bf)
    along_back = along_rows[2 * LEN :]
    along_rows = along_rows[: 2 * LEN]
    segb = jnp.broadcast_to(segment_ids[:, None], (LEN, TILE))
    attended_wide, inverse, probs = attend_forward(
        bounds, query, key_rows, value_rows, along_rows, against_rows, segb, segment_ids[None, :]
    )
    attended = attended_wide.astype(bf)
    branch = jnp.dot(attended, output_full, preferred_element_type=f4)
    first_sum = hidden.astype(f4) + branch
    normed = layer_norm(first_sum, gain_one, shift_one)
    normed_low = normed.astype(bf)
    expanded = jnp.dot(normed_low, expand_full, preferred_element_type=f4)
    activated = gelu_exact(expanded).astype(bf)
    branch_two = jnp.dot(activated, contract_full, preferred_element_type=f4)
    second_sum = normed + branch_two
    result = layer_norm(second_sum, gain_two, shift_two)
    mask = valid.astype(f4)[:, None]
    upstream = cotangent.astype(f4) * mask
    _, norm_two_back = jax.vjp(layer_norm, second_sum, gain_two, shift_two)
    d_second, d_gain_two, d_shift_two = norm_two_back(upstream)
    d_branch_two = d_second.astype(bf)
    d_activated = lax.dot_general(
        d_branch_two, contract_full, ROWS_LAST, preferred_element_type=f4
    )
    _, gelu_back = jax.vjp(gelu_exact, expanded)
    d_expanded = gelu_back(d_activated)[0].astype(bf)
    normed_gradient = d_second + lax.dot_general(
        d_expanded, expand_full, ROWS_LAST, preferred_element_type=f4
    )
    _, norm_one_back = jax.vjp(layer_norm, first_sum, gain_one, shift_one)
    d_first, d_gain_one, d_shift_one = norm_one_back(normed_gradient)
    grad_contract = lax.dot_general(
        activated, d_branch_two, ROWS_FIRST, preferred_element_type=f4
    )
    grad_expand = lax.dot_general(normed_low, d_expanded, ROWS_FIRST, preferred_element_type=f4)
    expand_owned = lax.psum_scatter(
        grad_expand.astype(bf), "fsdp", scatter_dimension=0, tiled=True
    ).astype(f4)
    contract_owned = lax.psum_scatter(
        grad_contract.astype(bf), "fsdp", scatter_dimension=0, tiled=True
    ).astype(f4)
    d_branch = d_first.astype(bf)
    attended_gradient = lax.dot_general(
        d_branch, output_full, ROWS_LAST, preferred_element_type=f4
    ).astype(bf)
    query_low, key_low, value_low, along_grad, against_grad = attend_backward(
        bounds,
        query,
        key_rows,
        value_rows,
        attended_gradient,
        attended_wide,
        inverse,
        along_back,
        against_rows,
        probs,
    )
    pos_key_low = jnp.dot(along_grad, onehot[2 * LEN :], preferred_element_type=f4).astype(bf)
    pos_query_low = jnp.dot(against_grad, onehot[: 2 * LEN], preferred_element_type=f4).astype(bf)
    both = (((0,), (1,)), ((), ()))
    grad_table = lax.dot_general(
        pos_query_low, query_full, both, preferred_element_type=f4
    ) + lax.dot_general(pos_key_low, key_full, both, preferred_element_type=f4)
    d_input = (
        d_first
        + lax.dot_general(query_low, query_full, ROWS_LAST, preferred_element_type=f4)
        + lax.dot_general(key_low, key_full, ROWS_LAST, preferred_element_type=f4)
        + lax.dot_general(value_low, value_full, ROWS_LAST, preferred_element_type=f4)
    )
    grad_query = lax.dot_general(
        hidden, query_low, ROWS_FIRST, preferred_element_type=f4
    ) + lax.dot_general(table_full, pos_query_low, both, preferred_element_type=f4)
    grad_key = lax.dot_general(
        hidden, key_low, ROWS_FIRST, preferred_element_type=f4
    ) + lax.dot_general(table_full, pos_key_low, both, preferred_element_type=f4)
    grad_value = lax.dot_general(hidden, value_low, ROWS_FIRST, preferred_element_type=f4)
    grad_output = lax.dot_general(attended, d_branch, ROWS_FIRST, preferred_element_type=f4)
    sums = jnp.stack(
        [jnp.sum(mask * second_sum * second_sum), jnp.sum(mask * branch_two * branch_two)]
    )
    cut = lambda x: x.reshape(count, x.shape[0] // count, width)
    grads = jnp.concatenate(
        [cut(grad_query), cut(grad_key), cut(grad_value), cut(grad_output), cut(grad_table)],
        axis=1,
    ).astype(bf)
    owned = lax.psum_scatter(grads, "fsdp", scatter_dimension=0, tiled=False).astype(f4)
    gains = jnp.concatenate([d_gain_one, d_shift_one, d_gain_two, d_shift_two, sums])
    gains = lax.psum(gains, "fsdp")
    me = lax.axis_index("fsdp")
    mine = lambda at: lax.dynamic_slice_in_dim(gains, at * width + me * per, per)
    cells = f4(hidden.shape[0] * count * width)
    return (
        result.astype(bf),
        d_input.astype(bf),
        owned[:per],
        owned[per : 2 * per],
        owned[2 * per : 3 * per],
        owned[3 * per : 4 * per],
        owned[4 * per :],
        mine(0),
        mine(1),
        expand_owned,
        contract_owned,
        mine(2),
        mine(3),
        jnp.sqrt(gains[4 * width] / cells),
        jnp.sqrt(gains[4 * width + 1] / cells),
    )


def solution(mesh):
    in_specs = (
        P("fsdp", None),
        P("fsdp", None),
        P("fsdp", None),
        P("fsdp", None),
        P("fsdp", None),
        P("fsdp", None),
        P("fsdp"),
        P("fsdp"),
        P("fsdp", None),
        P("fsdp", None),
        P("fsdp"),
        P("fsdp"),
        P("fsdp"),
        P("fsdp"),
        P("fsdp", None),
    )
    out_specs = (
        P("fsdp", None),
        P("fsdp", None),
        P("fsdp", None),
        P("fsdp", None),
        P("fsdp", None),
        P("fsdp", None),
        P("fsdp", None),
        P("fsdp"),
        P("fsdp"),
        P("fsdp", None),
        P("fsdp", None),
        P("fsdp"),
        P("fsdp"),
        P(),
        P(),
    )
    return jax.shard_map(shards, mesh=mesh, in_specs=in_specs, out_specs=out_specs, check_vma=False)
```

```python
from functools import partial
import math

import jax
import jax.numpy as jnp
import numpy as np
from jax import lax
from jax.experimental import pallas as pl
from jax.experimental.pallas import tpu as pltpu
from jax.sharding import PartitionSpec as P

bf = jnp.bfloat16
f4 = jnp.float32
HEADS = 12
BUCKETS = 256
LEN = 1024
TILE = 128
CH = 256
NCH = LEN // CH
SCALE = 1.0 / math.sqrt(192.0)
NORM_EPS = 1e-07
MASKED = -1e30
TOK = 256
FCH = 768
ROWS_FIRST = (((0,), (0,)), ((), ()))
ROWS_LAST = (((1,), (1,)), ((), ()))
NT = ROWS_LAST
NN = (((1,), (0,)), ((), ()))


def bucket_index(offsets, buckets):
    middle = buckets // 2
    limit = 2 * buckets
    magnitude = np.abs(offsets)
    inside = (offsets < middle) & (offsets > -middle)
    clipped = np.where(inside, middle - 1, magnitude)
    logged = (
        np.ceil(np.log(clipped / middle) / np.log((limit - 1) / middle) * (middle - 1)) + middle
    )
    bucket = np.where(magnitude <= middle, offsets, (logged * np.sign(offsets)).astype(np.int32))
    return np.clip(bucket + buckets, 0, 2 * buckets - 1).astype(np.int32)


def dot(a,b,dims=NN): return lax.dot_general(a,b,dims,preferred_element_type=f4)
def al(x,m): return pl.multiple_of(x,m)
def iotas():
    r=lax.broadcasted_iota(jnp.int32,(TILE,TILE),0); c=lax.broadcasted_iota(jnp.int32,(TILE,TILE),1)
    return r,c
def fwd_kernel(b_ref,q_ref,k_ref,v_ref,rk_ref,rq_ref,segb_ref,segr_ref,
               att_ref,inv_ref,p_ref, qm,km,vj,xs,ys,sc,mx,sm,acc):
    r,c=iotas()
    eye=(r==c).astype(f4).astype(bf); rev=(r+c==TILE-1).astype(f4).astype(bf)
    early=(r+c)<TILE
    half=lax.broadcasted_iota(jnp.int32,(LEN,TILE),1)<64
    zero=jnp.zeros((LEN,TILE),bf)
    q=q_ref[...]; k=k_ref[...]; v=v_ref[...]
    for h in range(2):
        m=half if h==0 else jnp.logical_not(half)
        qm[h]=jnp.where(m,q,zero); km[h]=jnp.where(m,k,zero)
        vj[h,:,:TILE]=jnp.where(m,v,zero)
        for t in range(LEN//TILE): vj[h,t*TILE:(t+1)*TILE,TILE:]=rev
    halft=lax.broadcasted_iota(jnp.int32,(CH,TILE),1)<64
    def prod(ic,_):
        lo=b_ref[ic]; hi=b_ref[NCH+ic]
        rows=pl.ds(al(ic*CH,CH),CH)
        def one(d,_):
            w=pl.ds(al((d+4)*CH,CH),CH)
            for h in range(2):
                xs[h,rows,w]=dot(qm[h,rows,:],rk_ref[w,:],NT).astype(bf)
                ys[h,rows,w]=dot(km[h,rows,:],rq_ref[w,:],NT).astype(bf)
            return 0
        lax.fori_loop(lo-ic-1,hi-ic,one,0)
        return 0
    lax.fori_loop(0,NCH,prod,0)
    def skewed(ref,h,row,kk):
        rr=pl.ds(al(row*TILE,TILE),TILE)
        a=ref[h,rr,pl.ds(al((kk+8)*TILE,TILE),TILE)]
        b=ref[h,rr,pl.ds(al((kk+7)*TILE,TILE),TILE)]
        return pltpu.roll(jnp.where(early,a,b),0,1,stride=1,stride_axis=0)
    def chunk(ic,_):
        lo=b_ref[ic]; hi=b_ref[NCH+ic]
        rows=pl.ds(al(ic*CH,CH),CH)
        for h in range(2):
            mx[h]=jnp.full((CH,TILE),MASKED,f4)
            sm[h]=jnp.zeros((CH,TILE),f4)
        acc[...]=jnp.zeros((CH,TILE),f4)
        def score(jc,_):
            cols=pl.ds(al(jc*CH,CH),CH)
            segc=segr_ref[:,cols]
            for s in range(2):
                i=2*ic+s
                srow=segb_ref[pl.ds(al(i*TILE,TILE),TILE),:]
                for h in range(2):
                    aks=[]
                    for t in range(2):
                        aks.append(skewed(ys,h,2*jc+t,i-(2*jc+t)))
                    lhs=jnp.concatenate([qm[h,pl.ds(al(i*TILE,TILE),TILE),:],eye],axis=1)
                    rhs=jnp.concatenate([k_ref[cols,:],jnp.concatenate(aks,axis=0)],axis=1)
                    content=dot(lhs,rhs,NT)
                    best=mx[h,s*TILE:(s+1)*TILE,:]
                    for t in range(2):
                        along=skewed(xs,h,i,2*jc+t-i).astype(f4)
                        ok=srow==segc[:,t*TILE:(t+1)*TILE]
                        val=jnp.where(ok,content[:,t*TILE:(t+1)*TILE]+along,MASKED)
                        sc[h,s*TILE:(s+1)*TILE,pl.ds(al(jc*CH+t*TILE,TILE),TILE)]=val
                        best=jnp.maximum(best,val)
                    mx[h,s*TILE:(s+1)*TILE,:]=best
            return 0
        lax.fori_loop(lo,hi,score,0)
        for h in range(2):
            mx[h]=jnp.broadcast_to(jnp.max(mx[h],axis=1,keepdims=True),(CH,TILE))
        fac=SCALE*math.log2(math.e)
        def mix(jc,_):
            for h in range(2):
                top=mx[h]; tot=sm[h]
                for t in range(2):
                    cols=pl.ds(al(jc*CH+t*TILE,TILE),TILE)
                    e=jnp.exp2((sc[h,:,cols]-top)*fac)
                    tot=tot+e
                    res=dot(e.astype(bf),vj[h,cols,:])
                    acc[...]+=res[:,:TILE]
                    p_ref[h,rows,cols]=res[:,TILE:].astype(bf)
                sm[h]=tot
            return 0
        lax.fori_loop(lo,hi,mix,0)
        inv=[1.0/jnp.sum(sm[h],axis=1,keepdims=True) for h in range(2)]
        invp=jnp.where(halft,jnp.broadcast_to(inv[0],(CH,TILE)),jnp.broadcast_to(inv[1],(CH,TILE)))
        inv_ref[rows,:]=invp
        att_ref[rows,:]=acc[...]*invp
        return 0
    lax.fori_loop(0,NCH,chunk,0)
def attend_forward(bounds, both, v, spread, segb, segr):
    pairs = v.shape[1] // TILE
    col = lambda n, at=0: pl.BlockSpec((n, TILE), lambda p, *_: (0, at + p))
    return pl.pallas_call(
        fwd_kernel,
        grid_spec=pltpu.PrefetchScalarGridSpec(
            num_scalar_prefetch=1,
            grid=(pairs,),
            in_specs=[
                col(LEN),
                col(LEN, pairs),
                col(LEN),
                col(2 * LEN, pairs),
                col(2 * LEN),
                pl.BlockSpec((LEN, TILE), lambda p, *_: (0, 0)),
                pl.BlockSpec((1, LEN), lambda p, *_: (0, 0)),
            ],
            out_specs=[col(LEN), col(LEN), pl.BlockSpec((2, LEN, LEN), lambda p, *_: (p, 0, 0))],
            scratch_shapes=[
                pltpu.VMEM((2, LEN, TILE), bf),
                pltpu.VMEM((2, LEN, TILE), bf),
                pltpu.VMEM((2, LEN, 2 * TILE), bf),
                pltpu.VMEM((2, LEN, 2 * LEN), bf),
                pltpu.VMEM((2, LEN, 2 * LEN), bf),
                pltpu.VMEM((2, CH, LEN), f4),
                pltpu.VMEM((2, CH, TILE), f4),
                pltpu.VMEM((2, CH, TILE), f4),
                pltpu.VMEM((CH, TILE), f4),
            ],
        ),
        out_shape=[
            jax.ShapeDtypeStruct(v.shape, f4),
            jax.ShapeDtypeStruct(v.shape, f4),
            jax.ShapeDtypeStruct((2 * pairs, LEN, LEN), bf),
        ],
        compiler_params=pltpu.CompilerParams(vmem_limit_bytes=58 << 20),
        name="attend_forward",
    )(bounds, both, both, v, spread, spread, segb, segr)


def bwd_kernel(b_ref,q_ref,k_ref,v_ref,da_ref,att_ref,inv_ref,rk_ref,rq_ref,p_ref,
               dq_ref,dk_ref,dv_ref,gk_ref,gq_ref,
               dah,vr,krc,rkc,rqc,bdq,bda,bdk,ws,wt,gk,gq,dkt,dvt,dq,dk2,ds_,iv_):
    r,c=iotas()
    eye=(r==c).astype(f4).astype(bf); rev=(r+c==TILE-1).astype(f4).astype(bf)
    late=c>=r; early=c<=r
    half=lax.broadcasted_iota(jnp.int32,(LEN,TILE),1)<64
    zero=jnp.zeros((LEN,TILE),bf)
    low=lax.broadcasted_iota(jnp.int32,(TILE,LEN),0)<64
    zerot=jnp.zeros((TILE,LEN),bf)
    da=da_ref[...]
    dah[0]=jnp.where(half,da,zero); dah[1]=jnp.where(half,zero,da)
    das=(da.astype(f4)*inv_ref[...]).astype(bf)
    kr=[]
    for t in range(LEN//TILE):
        rows=slice(t*TILE,(t+1)*TILE)
        vr[rows,:]=dot(rev,v_ref[rows,:]).astype(bf)
        kr.append(dot(rev,k_ref[rows,:]).astype(bf))
    kr=jnp.concatenate(kr,axis=0)
    k0=jnp.where(half,kr,zero); k1=jnp.where(half,zero,kr)
    for t in range(NCH):
        krc[t,:CH,:]=k0[t*CH:(t+1)*CH]; krc[t,CH:,:]=k1[t*CH:(t+1)*CH]
    halfc=lax.broadcasted_iota(jnp.int32,(CH,TILE),1)<64
    zeroc=jnp.zeros((CH,TILE),bf)
    for t in range(2*NCH):
        rows=slice(t*CH,(t+1)*CH)
        a=rk_ref[rows,:]; b=rq_ref[rows,:]
        rkc[t,:CH,:]=jnp.where(halfc,a,zeroc); rkc[t,CH:,:]=jnp.where(halfc,zeroc,a)
        rqc[t,:CH,:]=jnp.where(halfc,b,zeroc); rqc[t,CH:,:]=jnp.where(halfc,zeroc,b)
    for ref,val in ((bdq,q_ref[...]),(bda,das),(bdk,kr)):
        vt=val.T
        v0=jnp.where(low,vt,zerot); v1=jnp.where(low,zerot,vt)
        for t in range(NCH):
            ref[t,:,:CH]=v0[:,t*CH:(t+1)*CH]; ref[t,:,CH:]=v1[:,t*CH:(t+1)*CH]
    gk[...]=jnp.zeros(gk.shape,f4); gq[...]=jnp.zeros(gq.shape,f4)
    dkt[...]=jnp.zeros(dkt.shape,f4); dvt[...]=jnp.zeros(dvt.shape,f4)
    dq[...]=jnp.zeros(dq.shape,f4); dk2[...]=jnp.zeros(dk2.shape,f4)
    def chunk(ic,_):
        lo=b_ref[2*NCH+ic]; hi=b_ref[3*NCH+ic]
        rows=pl.ds(al(ic*CH,CH),CH)
        @pl.when(hi>lo)
        def _():
            x=att_ref[rows,:]*da_ref[rows,:].astype(f4)
            ivp=inv_ref[rows,:]
            zf=jnp.zeros((CH,TILE),f4)
            ivr=pltpu.roll(ivp,64,1)
            for h in range(2):
                xm=jnp.where(halfc,x,zf) if h==0 else jnp.where(halfc,zf,x)
                ds_[h]=jnp.broadcast_to(jnp.sum(xm,axis=1,keepdims=True),(CH,TILE))
                iv_[h]=jnp.where(halfc,ivp,ivr) if h==0 else jnp.where(halfc,ivr,ivp)
            zz=jnp.zeros((CH,CH),bf)
            for h in range(2):
                for ref in (ws,wt):
                    ref[h,rows,pl.ds(al(lo*CH,CH),CH)]=zz
                    ref[h,rows,pl.ds(al((hi+1)*CH,CH),CH)]=zz
        def grad(jc,_):
            cols=pl.ds(al(jc*CH,CH),CH)
            dss=[];ps=[]
            for h in range(2):
                dp=dot(dah[h,rows,:],vr[cols,:],NT)
                pt=p_ref[h,rows,cols]
                d=ds_[h]; iv=iv_[h]
                parts=[]
                for t in range(2):
                    sl=slice(t*TILE,(t+1)*TILE)
                    parts.append((pt[:,sl].astype(f4)*((dp[:,sl]-d)*iv)).astype(bf))
                for t in range(2):
                    tt=dot(eye,parts[t],NT).astype(bf)
                    for s in range(2):
                        sr=slice(s*TILE,(s+1)*TILE)
                        ws[h,pl.ds(al(ic*CH+s*TILE,TILE),TILE),pl.ds(al((jc+1)*CH+t*TILE,TILE),TILE)]=pltpu.roll(parts[t][sr],0,1,stride=1,stride_axis=0)
                        wt[h,pl.ds(al(jc*CH+t*TILE,TILE),TILE),pl.ds(al((ic+1)*CH+s*TILE,TILE),TILE)]=pltpu.roll(tt[:,sr],1,1,stride=1,stride_axis=0)
                dss.append(jnp.concatenate(parts,axis=1)); ps.append(pt)
            dq[rows,:]+=dot(jnp.concatenate(dss,axis=1),krc[jc])
            dkt[:,cols]+=dot(bdq[ic],jnp.concatenate(dss,axis=0))
            dvt[:,cols]+=dot(bda[ic],jnp.concatenate(ps,axis=0))
            return 0
        lax.fori_loop(lo,hi,grad,0)
        return 0
    lax.fori_loop(0,NCH,chunk,0)
    def fold(ic,_):
        lo=b_ref[2*NCH+ic]; hi=b_ref[3*NCH+ic]
        rows=pl.ds(al(ic*CH,CH),CH)
        def one(d,_):
            w=pl.ds(al((d+4)*CH,CH),CH)
            for ref,mask,left,rc,outr,bd,g in ((ws,late,None,rkc,dq,bdq,gk),(wt,early,None,rqc,dk2,bdk,gq)):
                us=[]
                for h in range(2):
                    rr=[]
                    for s in range(2):
                        i=2*ic+s
                        rs=pl.ds(al(i*TILE,TILE),TILE)
                        cc=[]
                        for b in range(2):
                            j=i+2*d+b
                            x=ref[h,rs,pl.ds(al((j+2)*TILE,TILE),TILE)]
                            y=ref[h,rs,pl.ds(al((j+3)*TILE,TILE),TILE)]
                            cc.append(jnp.where(mask,x,y))
                        rr.append(jnp.concatenate(cc,axis=1))
                    us.append(jnp.concatenate(rr,axis=0))
                outr[rows,:]+=dot(jnp.concatenate(us,axis=1),rc[d+4])
                g[:,w]+=dot(bd[ic],jnp.concatenate(us,axis=0))
            return 0
        lax.fori_loop(lo-ic-1,jnp.where(hi>lo,hi-ic,lo-ic-1),one,0)
        return 0
    lax.fori_loop(0,NCH,fold,0)
    dq_ref[...]=(dq[...]*SCALE).astype(bf)
    for t in range(LEN//TILE):
        rows=slice(t*TILE,(t+1)*TILE)
        x=((dkt[:,rows].T+dk2[rows,:])*SCALE).astype(bf)
        dk_ref[rows,:]=dot(rev,x).astype(bf)
        dv_ref[rows,:]=dot(rev,dvt[:,rows].T.astype(bf)).astype(bf)
    gk_ref[...]=(gk[...]*SCALE).astype(bf)
    gq_ref[...]=(gq[...]*SCALE).astype(bf)
def attend_backward(bounds, both, v, da, att, inv, rkr, spread, p):
    pairs = v.shape[1] // TILE
    col = lambda n, at=0: pl.BlockSpec((n, TILE), lambda p, *_: (0, at + p))
    colr = pl.BlockSpec((TILE, 2 * LEN), lambda p, *_: (p, 0))
    half = [pltpu.VMEM((NCH, TILE, 2 * CH), bf)]
    return pl.pallas_call(
        bwd_kernel,
        grid_spec=pltpu.PrefetchScalarGridSpec(
            num_scalar_prefetch=1,
            grid=(pairs,),
            in_specs=[
                col(LEN),
                col(LEN, pairs),
                col(LEN),
                col(LEN),
                col(LEN),
                col(LEN),
                col(2 * LEN),
                col(2 * LEN),
                pl.BlockSpec((2, LEN, LEN), lambda p, *_: (p, 0, 0)),
            ],
            out_specs=[col(LEN)] * 3 + [colr] * 2,
            scratch_shapes=[
                pltpu.VMEM((2, LEN, TILE), bf),
                pltpu.VMEM((LEN, TILE), bf),
                pltpu.VMEM((NCH, 2 * CH, TILE), bf),
                pltpu.VMEM((2 * NCH, 2 * CH, TILE), bf),
                pltpu.VMEM((2 * NCH, 2 * CH, TILE), bf),
            ]
            + half * 3
            + [pltpu.VMEM((2, LEN, LEN + 2 * CH), bf)] * 2
            + [pltpu.VMEM((TILE, 2 * LEN), f4)] * 2
            + [pltpu.VMEM((TILE, LEN), f4)] * 2
            + [pltpu.VMEM((LEN, TILE), f4)] * 2
            + [pltpu.VMEM((2, CH, TILE), f4)] * 2,
        ),
        out_shape=[jax.ShapeDtypeStruct(v.shape, bf)] * 3
        + [jax.ShapeDtypeStruct((v.shape[1], 2 * LEN), bf)] * 2,
        compiler_params=pltpu.CompilerParams(vmem_limit_bytes=58 << 20),
        name="attend_backward",
    )(bounds, both, both, v, da, att, inv, rkr, spread, p)


def gelu_pair(u):
    size = jnp.abs(u)
    bell = jnp.exp2(u * u * (-0.5 * math.log2(math.e)))
    t = 1.0 / (1.0 + (0.3275911 / math.sqrt(2.0)) * size)
    poly = 0.5 * 1.061405429
    for c in (-1.453152027, 1.421413741, -0.284496736, 0.254829592):
        poly = poly * t + 0.5 * c
    tail = poly * t * bell
    phi = jnp.where(u < 0.0, tail, 1.0 - tail)
    return u * phi, phi + u * bell * (1.0 / math.sqrt(2.0 * math.pi))


def middle_kernel(
    hid_ref, att_ref, wo_ref, we_ref, wc_ref, vec_ref, mask_ref, cot_ref,
    out_ref, dfirst_ref, dbranch_ref, datt_ref, act_ref, dtwo_ref, low_ref, dexp_ref, sums_ref,
    pre, slope, acc, norm_,
):
    width = hid_ref.shape[1]
    chunks = we_ref.shape[1] // FCH
    gain_one = vec_ref[0:1, :]
    shift_one = vec_ref[1:2, :]
    gain_two = vec_ref[2:3, :]
    shift_two = vec_ref[3:4, :]
    inv = 1.0 / width
    first = hid_ref[...].astype(f4) + dot(att_ref[...].astype(bf), wo_ref[...])
    cen = first - jnp.sum(first, axis=1, keepdims=True) * inv
    rstd_one = lax.rsqrt(jnp.sum(cen * cen, axis=1, keepdims=True) * inv + NORM_EPS)
    n_one = cen * rstd_one
    norm_[...] = n_one
    normed = n_one * gain_one + shift_one
    low_ref[...] = normed.astype(bf)
    acc[...] = jnp.zeros(acc.shape, f4)

    def cols(c):
        return slice(c * FCH, (c + 1) * FCH)

    def expand(c):
        pre[c % 2] = dot(low_ref[...], we_ref[:, cols(c)])

    def bend(c):
        value, grad = gelu_pair(pre[c % 2])
        act_ref[:, cols(c)] = value.astype(bf)
        slope[:, cols(c)] = grad.astype(bf)

    def contract(c):
        acc[...] += dot(act_ref[:, cols(c)], wc_ref[cols(c), :])

    expand(0)
    expand(1)
    bend(0)

    def steady(c, _):
        expand(c + 1)
        bend(c)
        contract(c - 1)
        return 0

    for c in range(1, chunks - 1):
        steady(c, 0)
    bend(chunks - 1)
    contract(chunks - 2)
    contract(chunks - 1)
    branch = acc[...]
    mask = mask_ref[:, 0:1]
    normed = norm_[...] * gain_one + shift_one
    second = normed + branch
    row_res = jnp.sum(mask * second * second, axis=0, keepdims=True)
    row_sub = jnp.sum(mask * branch * branch, axis=0, keepdims=True)
    cen = second - jnp.sum(second, axis=1, keepdims=True) * inv
    rstd = lax.rsqrt(jnp.sum(cen * cen, axis=1, keepdims=True) * inv + NORM_EPS)
    n_two = cen * rstd
    out_ref[...] = (n_two * gain_two + shift_two).astype(bf)
    up = cot_ref[...].astype(f4) * mask
    row_g2 = jnp.sum(up * n_two, axis=0, keepdims=True)
    row_s2 = jnp.sum(up, axis=0, keepdims=True)
    g = up * gain_two
    d_second = (
        g
        - jnp.sum(g, axis=1, keepdims=True) * inv
        - n_two * (jnp.sum(g * n_two, axis=1, keepdims=True) * inv)
    ) * rstd
    dtwo_ref[...] = d_second.astype(bf)
    acc[...] = d_second

    def back(c):
        grad = dot(dtwo_ref[...], wc_ref[cols(c), :], NT) * slope[:, cols(c)].astype(f4)
        dexp_ref[:, cols(c)] = grad.astype(bf)

    def into(c):
        acc[...] += dot(dexp_ref[:, cols(c)], we_ref[:, cols(c)], NT)

    back(0)

    def steady_back(c, _):
        back(c)
        into(c - 1)
        return 0

    for c in range(1, chunks):
        steady_back(c, 0)
    into(chunks - 1)
    up = acc[...]
    n_one = norm_[...]
    row_g1 = jnp.sum(up * n_one, axis=0, keepdims=True)
    row_s1 = jnp.sum(up, axis=0, keepdims=True)
    g = up * gain_one
    d_first = (
        g
        - jnp.sum(g, axis=1, keepdims=True) * inv
        - n_one * (jnp.sum(g * n_one, axis=1, keepdims=True) * inv)
    ) * rstd_one
    dfirst_ref[...] = d_first
    low = d_first.astype(bf)
    dbranch_ref[...] = low
    datt_ref[...] = dot(low, wo_ref[...], NT).astype(bf)
    rows = jnp.concatenate(
        [row_g1, row_s1, row_g2, row_s2, row_res, row_sub, jnp.zeros((2, width), f4)], axis=0
    )

    @pl.when(pl.program_id(0) == 0)
    def _():
        sums_ref[...] = rows

    @pl.when(pl.program_id(0) > 0)
    def _():
        sums_ref[...] += rows


def middle(hidden, attended, wo, we, wc, vectors, mask, cotangent):
    tokens, width = hidden.shape
    wide = we.shape[1]
    tok = lambda n: pl.BlockSpec((TOK, n), lambda i: (i, 0))
    once = lambda a, b: pl.BlockSpec((a, b), lambda i: (0, 0), pipeline_mode=pl.Buffered(1))
    shape = lambda n, dtype: jax.ShapeDtypeStruct((tokens, n), dtype)
    return pl.pallas_call(
        middle_kernel,
        grid=(tokens // TOK,),
        in_specs=[
            tok(width), tok(width), once(width, width), once(width, wide), once(wide, width),
            once(4, width), tok(TILE), tok(width),
        ],
        out_specs=[
            tok(width), tok(width), tok(width), tok(width), tok(wide), tok(width), tok(width),
            tok(wide), pl.BlockSpec((8, width), lambda i: (0, 0)),
        ],
        out_shape=[
            shape(width, bf), shape(width, f4), shape(width, bf), shape(width, bf),
            shape(wide, bf), shape(width, bf), shape(width, bf), shape(wide, bf),
            jax.ShapeDtypeStruct((8, width), f4),
        ],
        scratch_shapes=[
            pltpu.VMEM((2, TOK, FCH), f4),
            pltpu.VMEM((TOK, wide), bf),
            pltpu.VMEM((TOK, width), f4),
            pltpu.VMEM((TOK, width), f4),
        ],
        compiler_params=pltpu.CompilerParams(vmem_limit_bytes=60 << 20),
        name="middle",
    )(hidden, attended, wo, we, wc, vectors, mask, cotangent)


def digits(count):
    found = [(1, 2)]
    stride = 2
    while stride < count:
        radix = 4 if count // stride >= 4 else 2
        found.append((stride, radix))
        stride *= radix
    return found


def place(relative, count):
    spot = relative * 0
    for stride, radix in digits(count):
        spot = spot * radix + ((relative >> (stride.bit_length() - 1)) & (radix - 1))
    return spot


def mixing(size, count, me):
    per = size // count
    row = np.arange(size)
    target = place(jnp.asarray(row // per, jnp.int32) ^ me, count) * per + (row % per)
    spots = lax.broadcasted_iota(jnp.int32, (size, size), 1)
    return (target[:, None] == spots).astype(bf)


def offset_rows(count, me):
    index = bucket_index(LEN - np.arange(2 * LEN), BUCKETS)
    back = index.reshape(-1, TILE)[:, ::-1].reshape(-1)
    size = 2 * BUCKETS
    per = size // count
    both = np.concatenate([index, back])
    target = place(jnp.asarray(both // per, jnp.int32) ^ me, count) * per + (both % per)
    spots = lax.broadcasted_iota(jnp.int32, (4 * LEN, size), 1)
    return (target[:, None] == spots).astype(bf)


def swap(value, offset, count):
    return lax.ppermute(value, "fsdp", [(i, i ^ offset) for i in range(count)])


def together(values):
    return list(lax.optimization_barrier(tuple(values)))


def gather_pair(first, second, count):
    middle = digits(count)[1:]
    one, two = first[None], second[None]
    for (stride_a, radix_a), (stride_b, radix_b) in zip(middle[::-1], middle):
        got_a = [one]
        got_b = [two]
        for step in range(1, max(radix_a, radix_b)):
            if step < radix_a:
                got_a.append(swap(one, step * stride_a, count))
            if step < radix_b:
                got_b.append(swap(two, step * stride_b, count))
        one, two = together([jnp.concatenate(got_a, axis=0), jnp.concatenate(got_b, axis=0)])
    radices = [radix for _, radix in middle[::-1]]
    two = two.reshape(*radices, *second.shape)
    turn = tuple(range(len(middle)))[::-1]
    two = two.transpose(turn + (len(middle), len(middle) + 1)).reshape(-1, *second.shape)
    return (one, swap(one, 1, count)), (two, swap(two, 1, count))


def scatter_pair(first, second, count):
    middle = digits(count)[1:]
    radices = [radix for _, radix in middle]
    shape_a, shape_b = first.shape[1:], second.shape[1:]
    half_a = first.reshape(2, -1, *shape_a)
    half_b = second.reshape(2, -1, *shape_b)
    one, two = together(
        [
            half_a[0].astype(f4) + swap(half_a[1], 1, count).astype(f4),
            half_b[0].astype(f4) + swap(half_b[1], 1, count).astype(f4),
        ]
    )
    one = one.astype(bf).reshape(*radices, *shape_a)
    two = two.astype(bf).reshape(*radices, *shape_b)
    for step, ((stride_a, radix_a), (stride_b, radix_b)) in enumerate(zip(middle, middle[::-1])):
        last = two.ndim - 3
        got_a = []
        got_b = []
        for hop in range(1, max(radix_a, radix_b)):
            if hop < radix_a:
                got_a.append(swap(one[hop], hop * stride_a, count))
            if hop < radix_b:
                got_b.append(
                    swap(lax.index_in_dim(two, hop, last, keepdims=False), hop * stride_b, count)
                )
        sum_a = one[0].astype(f4)
        sum_b = lax.index_in_dim(two, 0, last, keepdims=False).astype(f4)
        got = together(got_a + got_b)
        for piece in got[: len(got_a)]:
            sum_a = sum_a + piece.astype(f4)
        for piece in got[len(got_a) :]:
            sum_b = sum_b + piece.astype(f4)
        if step == len(middle) - 1:
            return sum_a, sum_b
        one, two = sum_a.astype(bf), sum_b.astype(bf)


def active_chunks(segment, valid):
    rows = segment.reshape(NCH, CH)
    ok = valid.reshape(NCH, CH) > 0
    first = rows[:, 0]
    last = rows[:, -1]
    over = (first[None, :] <= last[:, None]) & (last[None, :] >= first[:, None])
    real = jnp.max(jnp.where(ok, rows, -1), axis=1)
    back = (first[None, :] <= real[:, None]) & (last[None, :] >= first[:, None])
    back = back | back.T
    place_ = jnp.arange(NCH)[None, :]

    def limits(mask):
        lo = jnp.min(jnp.where(mask, place_, NCH), axis=1)
        hi = jnp.max(jnp.where(mask, place_ + 1, 0), axis=1)
        return jnp.where(hi > 0, lo, 0), hi

    return jnp.concatenate(limits(over) + limits(back)).astype(jnp.int32)


def mm(left, right, dims=NN):
    return lax.dot_general(left, right, dims, preferred_element_type=f4)


def shards(
    hidden,
    query_weight,
    key_weight,
    value_weight,
    output_weight,
    relative_table,
    first_gain,
    first_shift,
    expand_weight,
    contract_weight,
    second_gain,
    second_shift,
    segment_ids,
    valid,
    cotangent,
):
    count = lax.axis_size("fsdp")
    me = lax.axis_index("fsdp")
    width = hidden.shape[1]
    wide = expand_weight.shape[1]
    per = query_weight.shape[0]
    per_t = relative_table.shape[0]
    per_c = contract_weight.shape[0]
    parts = wide // width

    pack = jnp.concatenate(
        [
            jnp.concatenate([query_weight, key_weight], axis=1),
            relative_table.reshape(per_t // 2, 2 * width),
        ],
        axis=0,
    )
    pair_a, pair_b = gather_pair(pack, value_weight, count)
    query_key = jnp.concatenate([x[:, :per] for x in pair_a], axis=0)
    query_key = query_key.reshape(count * per, 2 * width)
    table = jnp.concatenate([x[:, per:] for x in pair_a], axis=0).reshape(count * per_t, width)
    value_full = jnp.concatenate(pair_b, axis=0).reshape(count * per, width)

    small = jnp.concatenate([first_gain, first_shift, second_gain, second_shift])
    small = jnp.pad(small, (0, width - 4 * per))[None, :]
    whole = lax.all_gather(jnp.concatenate([output_weight, small], axis=0), "fsdp", tiled=False)
    output_full = whole[:, :per].reshape(count * per, width)
    vectors = whole[:, per, : 4 * per].reshape(count, 4, per).transpose(1, 0, 2)
    vectors = vectors.reshape(4, count * per).astype(f4)
    expand_full = lax.all_gather(expand_weight, "fsdp", axis=0, tiled=True)
    contract_full = lax.all_gather(contract_weight, "fsdp", axis=0, tiled=True)

    bounds = active_chunks(segment_ids, valid)
    mix = mixing(width, count, me)
    onehot = offset_rows(count, me)
    segb = jnp.broadcast_to(segment_ids[:, None], (LEN, TILE))
    hidden_mixed = mm(hidden, mix).astype(bf)
    bounds, mix, onehot, segb, hidden_mixed = together([bounds, mix, onehot, segb, hidden_mixed])
    table_mixed = mm(table, mix).astype(bf)
    both_rows = mm(hidden_mixed, query_key).astype(bf)
    value_rows = mm(hidden_mixed, value_full).astype(bf)
    position = mm(table_mixed, query_key).astype(bf)
    spread_rows = mm(onehot[: 2 * LEN], position).astype(bf)
    along_back = mm(onehot[2 * LEN :], position[:, width:]).astype(bf)
    attended_wide, inverse, probs = attend_forward(
        bounds, both_rows, value_rows, spread_rows, segb, segment_ids[None, :]
    )
    attended = attended_wide.astype(bf)
    mask = jnp.broadcast_to(valid.astype(f4)[:, None], (LEN, TILE))
    result, d_first, d_branch, attended_gradient, activated, d_branch_two, normed_low, d_expanded, rows = middle(
        hidden, attended_wide, output_full, expand_full, contract_full, vectors, mask, cotangent
    )
    grad_contract = mm(activated, d_branch_two, ROWS_FIRST).astype(bf)
    grad_expand = mm(normed_low, d_expanded, ROWS_FIRST).astype(bf)
    grad_output = mm(attended, d_branch, ROWS_FIRST).astype(bf)
    sums = jnp.sum(rows[4:6], axis=1)
    gains = rows[:4]
    gains = gains.reshape(4, count, per).transpose(1, 0, 2).reshape(count, 4 * per)
    tail = jnp.concatenate(
        [
            gains,
            jnp.broadcast_to(sums[None, :], (count, 2)),
            jnp.zeros((count, width - 4 * per - 2), f4),
        ],
        axis=1,
    )
    cut = grad_expand.reshape(count, per, wide)
    grads = jnp.concatenate(
        [cut[:, :, n * width : (n + 1) * width] for n in range(parts)]
        + [
            grad_contract.reshape(count, per_c, width),
            grad_output.reshape(count, per, width),
            tail.astype(bf)[:, None, :],
        ],
        axis=1,
    )
    owned = lax.psum_scatter(grads, "fsdp", scatter_dimension=0, tiled=False).astype(f4)

    query_low, key_low, value_low, along_grad, against_grad = attend_backward(
        bounds,
        both_rows,
        value_rows,
        attended_gradient,
        attended_wide,
        inverse,
        along_back,
        spread_rows,
        probs,
    )
    both = (((0,), (1,)), ((), ()))
    pos_key_low = mm(onehot[2 * LEN :], along_grad, both).astype(bf)
    pos_query_low = mm(onehot[: 2 * LEN], against_grad, both).astype(bf)
    query_mixed, key_mixed = query_key[:, :width], query_key[:, width:]
    grad_query = mm(hidden_mixed, query_low, ROWS_FIRST) + mm(
        table_mixed, pos_query_low, ROWS_FIRST
    )
    grad_key = mm(hidden_mixed, key_low, ROWS_FIRST) + mm(table_mixed, pos_key_low, ROWS_FIRST)
    grad_value = mm(hidden_mixed, value_low, ROWS_FIRST)
    grad_table = mm(pos_query_low, query_mixed, NT) + mm(pos_key_low, key_mixed, NT)
    grad_table = mm(grad_table.astype(bf), mix, NT).astype(bf)
    grad_pack = jnp.concatenate(
        [
            jnp.concatenate([grad_query.astype(bf), grad_key.astype(bf)], axis=1).reshape(
                count, per, 2 * width
            ),
            grad_table.reshape(count, per_t // 2, 2 * width),
        ],
        axis=1,
    )
    grad_value = grad_value.astype(bf).reshape(count, per, width)
    own_pack, own_value = scatter_pair(grad_pack, grad_value, count)
    d_input = (
        mm(query_low, query_mixed, NT) + mm(key_low, key_mixed, NT) + mm(value_low, value_full, NT)
    )
    d_input = d_first + mm(d_input.astype(bf), mix, NT)
    cells = f4(hidden.shape[0] * count * width)
    at = parts * per
    out_at = at + per_c
    last = owned[out_at + per]
    return (
        result,
        d_input.astype(bf),
        own_pack[:per, :width],
        own_pack[:per, width:],
        own_value,
        owned[out_at : out_at + per],
        own_pack[per:].reshape(per_t, width),
        last[:per],
        last[per : 2 * per],
        jnp.concatenate([owned[n * per : (n + 1) * per] for n in range(parts)], axis=1),
        owned[at:out_at],
        last[2 * per : 3 * per],
        last[3 * per : 4 * per],
        jnp.sqrt(last[4 * per] / cells),
        jnp.sqrt(last[4 * per + 1] / cells),
    )


def solution(mesh):
    in_specs = (
        P("fsdp", None),
        P("fsdp", None),
        P("fsdp", None),
        P("fsdp", None),
        P("fsdp", None),
        P("fsdp", None),
        P("fsdp"),
        P("fsdp"),
        P("fsdp", None),
        P("fsdp", None),
        P("fsdp"),
        P("fsdp"),
        P("fsdp"),
        P("fsdp"),
        P("fsdp", None),
    )
    out_specs = (
        P("fsdp", None),
        P("fsdp", None),
        P("fsdp", None),
        P("fsdp", None),
        P("fsdp", None),
        P("fsdp", None),
        P("fsdp", None),
        P("fsdp"),
        P("fsdp"),
        P("fsdp", None),
        P("fsdp", None),
        P("fsdp"),
        P("fsdp"),
        P(),
        P(),
    )
    return jax.shard_map(shards, mesh=mesh, in_specs=in_specs, out_specs=out_specs, check_vma=False)
```

```python
from functools import partial
import math

import jax
import jax.numpy as jnp
import numpy as np
from jax import lax
from jax.experimental import pallas as pl
from jax.experimental.pallas import tpu as pltpu
from jax.sharding import PartitionSpec as P

bf = jnp.bfloat16
f4 = jnp.float32
HEADS = 12
BUCKETS = 256
LEN = 1024
TILE = 128
CH = 256
NCH = LEN // CH
SCALE = 1.0 / math.sqrt(192.0)
NORM_EPS = 1e-07
MASKED = -1e30
TOK = 256
FCH = 768
ROWS_FIRST = (((0,), (0,)), ((), ()))
ROWS_LAST = (((1,), (1,)), ((), ()))
NT = ROWS_LAST
NN = (((1,), (0,)), ((), ()))


def bucket_index(offsets, buckets):
    middle = buckets // 2
    limit = 2 * buckets
    magnitude = np.abs(offsets)
    inside = (offsets < middle) & (offsets > -middle)
    clipped = np.where(inside, middle - 1, magnitude)
    logged = (
        np.ceil(np.log(clipped / middle) / np.log((limit - 1) / middle) * (middle - 1)) + middle
    )
    bucket = np.where(magnitude <= middle, offsets, (logged * np.sign(offsets)).astype(np.int32))
    return np.clip(bucket + buckets, 0, 2 * buckets - 1).astype(np.int32)


def dot(a,b,dims=NN): return lax.dot_general(a,b,dims,preferred_element_type=f4)
def al(x,m): return pl.multiple_of(x,m)
def iotas():
    r=lax.broadcasted_iota(jnp.int32,(TILE,TILE),0); c=lax.broadcasted_iota(jnp.int32,(TILE,TILE),1)
    return r,c


def fwd_kernel(
    b_ref, qa_ref, ka_ref, rk_ref, rq_ref, qb_ref, kb_ref, v_ref, segb_ref, segr_ref,
    att_ref, inv_ref, p_ref,
    xs0, xs1, ys0, ys1, sc0, sc1, mx0, mx1, top, sm, acc,
):
    r, c = iotas()
    eye = (r == c).astype(f4).astype(bf)
    rev = (r + c == TILE - 1).astype(f4).astype(bf)
    early = (r + c) < TILE
    lane = lax.broadcasted_iota(jnp.int32, (CH, TILE), 1)
    left = lane < 64
    lane_t = lax.broadcasted_iota(jnp.int32, (TILE, TILE), 1)
    left_t = lane_t < 64
    step = pl.program_id(0)
    last = pl.num_programs(0) - 1
    fac = SCALE * math.log2(math.e)

    def head(x, h, mask):
        zero = jnp.zeros(x.shape, bf)
        return jnp.where(mask, x, zero) if h == 0 else jnp.where(mask, zero, x)

    def product(ic, slot, xs, ys):
        rows = pl.ds(al(ic * CH, CH), CH)
        w = pl.ds(al((slot + 3 - ic) * CH, CH), CH)
        out = pl.ds(al(slot * CH, CH), CH)
        q = qa_ref[rows, :]
        k = ka_ref[rows, :]
        for h in range(2):
            xs[h, rows, out] = dot(head(q, h, left), rk_ref[w, :], NT).astype(bf)
            ys[h, rows, out] = dot(head(k, h, left), rq_ref[w, :], NT).astype(bf)

    def skewed(ref, h, row, spot):
        rr = pl.ds(al(row * TILE, TILE), TILE)
        a = ref[h, rr, pl.ds(al((spot + 2) * TILE, TILE), TILE)]
        b = ref[h, rr, pl.ds(al((spot + 1) * TILE, TILE), TILE)]
        return pltpu.roll(jnp.where(early, a, b), 0, 1, stride=1, stride_axis=0)

    def score(ic, jc, xs, ys, sc, mx):
        cols = pl.ds(al(jc * CH, CH), CH)
        segc = segr_ref[:, cols]
        keys = kb_ref[cols, :]
        for s in range(2):
            i = 2 * ic + s
            rows = pl.ds(al(i * TILE, TILE), TILE)
            srow = segb_ref[rows, :]
            q = qb_ref[rows, :]
            for h in range(2):
                turned = [skewed(ys, h, 2 * jc + t, i - t) for t in range(2)]
                lhs = jnp.concatenate([head(q, h, left_t), eye], axis=1)
                rhs = jnp.concatenate([keys, jnp.concatenate(turned, axis=0)], axis=1)
                content = dot(lhs, rhs, NT)
                best = mx[h, rows, :]
                for t in range(2):
                    along = skewed(xs, h, i, 2 * jc + t - s).astype(f4)
                    ok = srow == segc[:, t * TILE : (t + 1) * TILE]
                    val = jnp.where(ok, content[:, t * TILE : (t + 1) * TILE] + along, MASKED)
                    sc[h, rows, pl.ds(al(jc * CH + t * TILE, TILE), TILE)] = val
                    best = jnp.maximum(best, val)
                mx[h, rows, :] = best

    def mix(ic, jc, sc):
        rows = pl.ds(al(ic * CH, CH), CH)
        for h in range(2):
            tot = sm[h]
            peak = top[h]
            for t in range(2):
                cols = pl.ds(al(jc * CH + t * TILE, TILE), TILE)
                e = jnp.exp2((sc[h, rows, cols] - peak) * fac)
                tot = tot + e
                rhs = jnp.concatenate([head(v_ref[cols, :], h, left_t), rev], axis=1)
                res = dot(e.astype(bf), rhs)
                acc[...] += res[:, :TILE]
                p_ref[h, rows, cols] = res[:, TILE:].astype(bf)
            sm[h] = tot

    def open_scores(ic, mx):
        rows = pl.ds(al(ic * CH, CH), CH)
        for h in range(2):
            mx[h, rows, :] = jnp.full((CH, TILE), MASKED, f4)

    def open_mix(ic, mx):
        rows = pl.ds(al(ic * CH, CH), CH)
        for h in range(2):
            peak = jnp.max(mx[h, rows, :], axis=1, keepdims=True)
            top[h] = jnp.broadcast_to(peak, (CH, TILE))
            sm[h] = jnp.zeros((CH, TILE), f4)
        acc[...] = jnp.zeros((CH, TILE), f4)

    def close_mix(ic):
        rows = pl.ds(al(ic * CH, CH), CH)
        inv = [1.0 / jnp.sum(sm[h], axis=1, keepdims=True) for h in range(2)]
        pair = jnp.where(
            left, jnp.broadcast_to(inv[0], (CH, TILE)), jnp.broadcast_to(inv[1], (CH, TILE))
        )
        inv_ref[rows, :] = pair
        att_ref[rows, :] = acc[...] * pair

    def sweep(before, body, after):
        def chunk(ic, _):
            lo = b_ref[ic]
            hi = b_ref[NCH + ic]
            before(ic, lo)

            def block(jc, _):
                body(ic, jc)
                return 0

            lax.fori_loop(lo, hi, block, 0)
            after(ic)
            return 0

        lax.fori_loop(0, NCH, chunk, 0)

    def fused(xs_new, ys_new, xs, ys, sc_new, mx_new, sc, mx):
        def before(ic, lo):
            product(ic, lo, xs_new, ys_new)
            open_scores(ic, mx_new)
            open_mix(ic, mx)

        def body(ic, jc):
            product(ic, jc + 1, xs_new, ys_new)
            mix(ic, jc, sc)
            score(ic, jc, xs, ys, sc_new, mx_new)

        sweep(before, body, close_mix)

    @pl.when(step == 0)
    def _():
        sweep(
            lambda ic, lo: product(ic, lo, xs0, ys0),
            lambda ic, jc: product(ic, jc + 1, xs0, ys0),
            lambda ic: None,
        )

    @pl.when((step > 0) & (step < last) & (step % 2 == 1))
    def _():
        fused(xs1, ys1, xs0, ys0, sc1, mx1, sc0, mx0)

    @pl.when((step > 0) & (step < last) & (step % 2 == 0))
    def _():
        fused(xs0, ys0, xs1, ys1, sc0, mx0, sc1, mx1)

    @pl.when(step == last)
    def _():
        sweep(lambda ic, lo: open_mix(ic, mx0), lambda ic, jc: mix(ic, jc, sc0), close_mix)


def attend_forward(bounds, both, v, spread, segb, segr):
    pairs = v.shape[1] // TILE

    def col(n, lag, at=0):
        return pl.BlockSpec((n, TILE), lambda s, *_: (0, at + jnp.clip(s - lag, 0, pairs - 1)))

    def wide(lag):
        return pl.BlockSpec((2, LEN, LEN), lambda s, *_: (jnp.clip(s - lag, 0, pairs - 1), 0, 0))

    window = pltpu.VMEM((2, LEN, LEN + CH), bf)
    return pl.pallas_call(
        fwd_kernel,
        grid_spec=pltpu.PrefetchScalarGridSpec(
            num_scalar_prefetch=1,
            grid=(pairs + 2,),
            in_specs=[
                col(LEN, 0),
                col(LEN, 0, pairs),
                col(2 * LEN, 0, pairs),
                col(2 * LEN, 0),
                col(LEN, 1),
                col(LEN, 1, pairs),
                col(LEN, 2),
                pl.BlockSpec((LEN, TILE), lambda s, *_: (0, 0)),
                pl.BlockSpec((1, LEN), lambda s, *_: (0, 0)),
            ],
            out_specs=[col(LEN, 2), col(LEN, 2), wide(2)],
            scratch_shapes=[window] * 4
            + [pltpu.VMEM((2, LEN, LEN), f4)] * 2
            + [pltpu.VMEM((2, LEN, TILE), f4)] * 2
            + [pltpu.VMEM((2, CH, TILE), f4)] * 2
            + [pltpu.VMEM((CH, TILE), f4)],
        ),
        out_shape=[
            jax.ShapeDtypeStruct(v.shape, f4),
            jax.ShapeDtypeStruct(v.shape, f4),
            jax.ShapeDtypeStruct((2 * pairs, LEN, LEN), bf),
        ],
        compiler_params=pltpu.CompilerParams(vmem_limit_bytes=60 << 20),
        name="attend_forward",
    )(bounds, both, both, spread, spread, both, both, v, segb, segr)


def bwd_kernel(b_ref,q_ref,k_ref,v_ref,da_ref,att_ref,inv_ref,rk_ref,rq_ref,p_ref,
               dq_ref,dk_ref,dv_ref,gk_ref,gq_ref,
               dah,vr,krc,rkc,rqc,bdq,bda,bdk,ws,wt,gk,gq,dkt,dvt,dq,dk2,ds_,iv_):
    r,c=iotas()
    eye=(r==c).astype(f4).astype(bf); rev=(r+c==TILE-1).astype(f4).astype(bf)
    late=c>=r; early=c<=r
    half=lax.broadcasted_iota(jnp.int32,(LEN,TILE),1)<64
    zero=jnp.zeros((LEN,TILE),bf)
    low=lax.broadcasted_iota(jnp.int32,(TILE,LEN),0)<64
    zerot=jnp.zeros((TILE,LEN),bf)
    da=da_ref[...]
    dah[0]=jnp.where(half,da,zero); dah[1]=jnp.where(half,zero,da)
    das=(da.astype(f4)*inv_ref[...]).astype(bf)
    kr=[]
    for t in range(LEN//TILE):
        rows=slice(t*TILE,(t+1)*TILE)
        vr[rows,:]=dot(rev,v_ref[rows,:]).astype(bf)
        kr.append(dot(rev,k_ref[rows,:]).astype(bf))
    kr=jnp.concatenate(kr,axis=0)
    k0=jnp.where(half,kr,zero); k1=jnp.where(half,zero,kr)
    for t in range(NCH):
        krc[t,:CH,:]=k0[t*CH:(t+1)*CH]; krc[t,CH:,:]=k1[t*CH:(t+1)*CH]
    halfc=lax.broadcasted_iota(jnp.int32,(CH,TILE),1)<64
    zeroc=jnp.zeros((CH,TILE),bf)
    for t in range(2*NCH):
        rows=slice(t*CH,(t+1)*CH)
        a=rk_ref[rows,:]; b=rq_ref[rows,:]
        rkc[t,:CH,:]=jnp.where(halfc,a,zeroc); rkc[t,CH:,:]=jnp.where(halfc,zeroc,a)
        rqc[t,:CH,:]=jnp.where(halfc,b,zeroc); rqc[t,CH:,:]=jnp.where(halfc,zeroc,b)
    for ref,val in ((bdq,q_ref[...]),(bda,das),(bdk,kr)):
        vt=val.T
        v0=jnp.where(low,vt,zerot); v1=jnp.where(low,zerot,vt)
        for t in range(NCH):
            ref[t,:,:CH]=v0[:,t*CH:(t+1)*CH]; ref[t,:,CH:]=v1[:,t*CH:(t+1)*CH]
    gk[...]=jnp.zeros(gk.shape,f4); gq[...]=jnp.zeros(gq.shape,f4)
    dkt[...]=jnp.zeros(dkt.shape,f4); dvt[...]=jnp.zeros(dvt.shape,f4)
    dq[...]=jnp.zeros(dq.shape,f4); dk2[...]=jnp.zeros(dk2.shape,f4)
    def chunk(ic,_):
        lo=b_ref[2*NCH+ic]; hi=b_ref[3*NCH+ic]
        rows=pl.ds(al(ic*CH,CH),CH)
        @pl.when(hi>lo)
        def _():
            x=att_ref[rows,:]*da_ref[rows,:].astype(f4)
            ivp=inv_ref[rows,:]
            zf=jnp.zeros((CH,TILE),f4)
            ivr=pltpu.roll(ivp,64,1)
            for h in range(2):
                xm=jnp.where(halfc,x,zf) if h==0 else jnp.where(halfc,zf,x)
                ds_[h]=jnp.broadcast_to(jnp.sum(xm,axis=1,keepdims=True),(CH,TILE))
                iv_[h]=jnp.where(halfc,ivp,ivr) if h==0 else jnp.where(halfc,ivr,ivp)
            zz=jnp.zeros((CH,CH),bf)
            for h in range(2):
                for ref in (ws,wt):
                    ref[h,rows,pl.ds(al(lo*CH,CH),CH)]=zz
                    ref[h,rows,pl.ds(al((hi+1)*CH,CH),CH)]=zz
        def grad(jc,_):
            cols=pl.ds(al(jc*CH,CH),CH)
            dss=[];ps=[]
            for h in range(2):
                dp=dot(dah[h,rows,:],vr[cols,:],NT)
                pt=p_ref[h,rows,cols]
                d=ds_[h]; iv=iv_[h]
                parts=[]
                for t in range(2):
                    sl=slice(t*TILE,(t+1)*TILE)
                    parts.append((pt[:,sl].astype(f4)*((dp[:,sl]-d)*iv)).astype(bf))
                for t in range(2):
                    tt=dot(eye,parts[t],NT).astype(bf)
                    for s in range(2):
                        sr=slice(s*TILE,(s+1)*TILE)
                        ws[h,pl.ds(al(ic*CH+s*TILE,TILE),TILE),pl.ds(al((jc+1)*CH+t*TILE,TILE),TILE)]=pltpu.roll(parts[t][sr],0,1,stride=1,stride_axis=0)
                        wt[h,pl.ds(al(jc*CH+t*TILE,TILE),TILE),pl.ds(al((ic+1)*CH+s*TILE,TILE),TILE)]=pltpu.roll(tt[:,sr],1,1,stride=1,stride_axis=0)
                dss.append(jnp.concatenate(parts,axis=1)); ps.append(pt)
            dq[rows,:]+=dot(jnp.concatenate(dss,axis=1),krc[jc])
            dkt[:,cols]+=dot(bdq[ic],jnp.concatenate(dss,axis=0))
            dvt[:,cols]+=dot(bda[ic],jnp.concatenate(ps,axis=0))
            return 0
        lax.fori_loop(lo,hi,grad,0)
        return 0
    lax.fori_loop(0,NCH,chunk,0)
    def fold(ic,_):
        lo=b_ref[2*NCH+ic]; hi=b_ref[3*NCH+ic]
        rows=pl.ds(al(ic*CH,CH),CH)
        def one(d,_):
            w=pl.ds(al((d+4)*CH,CH),CH)
            for ref,mask,left,rc,outr,bd,g in ((ws,late,None,rkc,dq,bdq,gk),(wt,early,None,rqc,dk2,bdk,gq)):
                us=[]
                for h in range(2):
                    rr=[]
                    for s in range(2):
                        i=2*ic+s
                        rs=pl.ds(al(i*TILE,TILE),TILE)
                        cc=[]
                        for b in range(2):
                            j=i+2*d+b
                            x=ref[h,rs,pl.ds(al((j+2)*TILE,TILE),TILE)]
                            y=ref[h,rs,pl.ds(al((j+3)*TILE,TILE),TILE)]
                            cc.append(jnp.where(mask,x,y))
                        rr.append(jnp.concatenate(cc,axis=1))
                    us.append(jnp.concatenate(rr,axis=0))
                outr[rows,:]+=dot(jnp.concatenate(us,axis=1),rc[d+4])
                g[:,w]+=dot(bd[ic],jnp.concatenate(us,axis=0))
            return 0
        lax.fori_loop(lo-ic-1,jnp.where(hi>lo,hi-ic,lo-ic-1),one,0)
        return 0
    lax.fori_loop(0,NCH,fold,0)
    dq_ref[...]=(dq[...]*SCALE).astype(bf)
    for t in range(LEN//TILE):
        rows=slice(t*TILE,(t+1)*TILE)
        x=((dkt[:,rows].T+dk2[rows,:])*SCALE).astype(bf)
        dk_ref[rows,:]=dot(rev,x).astype(bf)
        dv_ref[rows,:]=dot(rev,dvt[:,rows].T.astype(bf)).astype(bf)
    gk_ref[...]=(gk[...]*SCALE).astype(bf)
    gq_ref[...]=(gq[...]*SCALE).astype(bf)
def attend_backward(bounds, both, v, da, att, inv, rkr, spread, p):
    pairs = v.shape[1] // TILE
    col = lambda n, at=0: pl.BlockSpec((n, TILE), lambda p, *_: (0, at + p))
    colr = pl.BlockSpec((TILE, 2 * LEN), lambda p, *_: (p, 0))
    half = [pltpu.VMEM((NCH, TILE, 2 * CH), bf)]
    return pl.pallas_call(
        bwd_kernel,
        grid_spec=pltpu.PrefetchScalarGridSpec(
            num_scalar_prefetch=1,
            grid=(pairs,),
            in_specs=[
                col(LEN),
                col(LEN, pairs),
                col(LEN),
                col(LEN),
                col(LEN),
                col(LEN),
                col(2 * LEN),
                col(2 * LEN),
                pl.BlockSpec((2, LEN, LEN), lambda p, *_: (p, 0, 0)),
            ],
            out_specs=[col(LEN)] * 3 + [colr] * 2,
            scratch_shapes=[
                pltpu.VMEM((2, LEN, TILE), bf),
                pltpu.VMEM((LEN, TILE), bf),
                pltpu.VMEM((NCH, 2 * CH, TILE), bf),
                pltpu.VMEM((2 * NCH, 2 * CH, TILE), bf),
                pltpu.VMEM((2 * NCH, 2 * CH, TILE), bf),
            ]
            + half * 3
            + [pltpu.VMEM((2, LEN, LEN + 2 * CH), bf)] * 2
            + [pltpu.VMEM((TILE, 2 * LEN), f4)] * 2
            + [pltpu.VMEM((TILE, LEN), f4)] * 2
            + [pltpu.VMEM((LEN, TILE), f4)] * 2
            + [pltpu.VMEM((2, CH, TILE), f4)] * 2,
        ),
        out_shape=[jax.ShapeDtypeStruct(v.shape, bf)] * 3
        + [jax.ShapeDtypeStruct((v.shape[1], 2 * LEN), bf)] * 2,
        compiler_params=pltpu.CompilerParams(vmem_limit_bytes=58 << 20),
        name="attend_backward",
    )(bounds, both, both, v, da, att, inv, rkr, spread, p)


def gelu_pair(u):
    size = jnp.abs(u)
    bell = jnp.exp2(u * u * (-0.5 * math.log2(math.e)))
    t = 1.0 / (1.0 + (0.3275911 / math.sqrt(2.0)) * size)
    poly = 0.5 * 1.061405429
    for c in (-1.453152027, 1.421413741, -0.284496736, 0.254829592):
        poly = poly * t + 0.5 * c
    tail = poly * t * bell
    phi = jnp.where(u < 0.0, tail, 1.0 - tail)
    return u * phi, phi + u * bell * (1.0 / math.sqrt(2.0 * math.pi))


def middle_kernel(
    hid_ref, att_ref, wo_ref, we_ref, wc_ref, vec_ref, mask_ref, cot_ref,
    out_ref, dfirst_ref, dbranch_ref, datt_ref, act_ref, dtwo_ref, low_ref, dexp_ref, sums_ref,
    pre, slope, acc, norm_,
):
    width = hid_ref.shape[1]
    chunks = we_ref.shape[1] // FCH
    vectors = vec_ref[...].astype(f4).T
    gain_one = vectors[0:1, :]
    shift_one = vectors[1:2, :]
    gain_two = vectors[2:3, :]
    shift_two = vectors[3:4, :]
    inv = 1.0 / width
    first = hid_ref[...].astype(f4) + dot(att_ref[...].astype(bf), wo_ref[...])
    cen = first - jnp.sum(first, axis=1, keepdims=True) * inv
    rstd_one = lax.rsqrt(jnp.sum(cen * cen, axis=1, keepdims=True) * inv + NORM_EPS)
    n_one = cen * rstd_one
    norm_[...] = n_one
    normed = n_one * gain_one + shift_one
    low_ref[...] = normed.astype(bf)
    acc[...] = jnp.zeros(acc.shape, f4)

    def cols(c):
        return slice(c * FCH, (c + 1) * FCH)

    def expand(c):
        pre[c % 2] = dot(low_ref[...], we_ref[:, cols(c)])

    def bend(c):
        value, grad = gelu_pair(pre[c % 2])
        act_ref[:, cols(c)] = value.astype(bf)
        slope[:, cols(c)] = grad.astype(bf)

    def contract(c):
        acc[...] += dot(act_ref[:, cols(c)], wc_ref[:, cols(c)])

    expand(0)
    expand(1)
    bend(0)

    def steady(c, _):
        expand(c + 1)
        bend(c)
        contract(c - 1)
        return 0

    for c in range(1, chunks - 1):
        steady(c, 0)
    bend(chunks - 1)
    contract(chunks - 2)
    contract(chunks - 1)
    branch = acc[...]
    mask = mask_ref[:, 0:1]
    normed = norm_[...] * gain_one + shift_one
    second = normed + branch
    row_res = jnp.sum(mask * second * second, axis=0, keepdims=True)
    row_sub = jnp.sum(mask * branch * branch, axis=0, keepdims=True)
    cen = second - jnp.sum(second, axis=1, keepdims=True) * inv
    rstd = lax.rsqrt(jnp.sum(cen * cen, axis=1, keepdims=True) * inv + NORM_EPS)
    n_two = cen * rstd
    out_ref[...] = (n_two * gain_two + shift_two).astype(bf)
    up = cot_ref[...].astype(f4) * mask
    row_g2 = jnp.sum(up * n_two, axis=0, keepdims=True)
    row_s2 = jnp.sum(up, axis=0, keepdims=True)
    g = up * gain_two
    d_second = (
        g
        - jnp.sum(g, axis=1, keepdims=True) * inv
        - n_two * (jnp.sum(g * n_two, axis=1, keepdims=True) * inv)
    ) * rstd
    dtwo_ref[...] = d_second.astype(bf)
    acc[...] = d_second

    def back(c):
        grad = dot(dtwo_ref[...], wc_ref[:, cols(c)], NT) * slope[:, cols(c)].astype(f4)
        dexp_ref[:, cols(c)] = grad.astype(bf)

    def into(c):
        acc[...] += dot(dexp_ref[:, cols(c)], we_ref[:, cols(c)], NT)

    back(0)

    def steady_back(c, _):
        back(c)
        into(c - 1)
        return 0

    for c in range(1, chunks):
        steady_back(c, 0)
    into(chunks - 1)
    up = acc[...]
    n_one = norm_[...]
    row_g1 = jnp.sum(up * n_one, axis=0, keepdims=True)
    row_s1 = jnp.sum(up, axis=0, keepdims=True)
    g = up * gain_one
    d_first = (
        g
        - jnp.sum(g, axis=1, keepdims=True) * inv
        - n_one * (jnp.sum(g * n_one, axis=1, keepdims=True) * inv)
    ) * rstd_one
    dfirst_ref[...] = d_first
    low = d_first.astype(bf)
    dbranch_ref[...] = low
    datt_ref[...] = dot(low, wo_ref[...], NT).astype(bf)
    rows = jnp.concatenate(
        [row_g1, row_s1, row_g2, row_s2, row_res, row_sub, jnp.zeros((2, width), f4)], axis=0
    )

    @pl.when(pl.program_id(0) == 0)
    def _():
        sums_ref[...] = rows

    @pl.when(pl.program_id(0) > 0)
    def _():
        sums_ref[...] += rows


def middle(hidden, attended, weights, wide, mask, cotangent):
    tokens, width = hidden.shape
    tok = lambda n: pl.BlockSpec((TOK, n), lambda i: (i, 0))
    once = lambda n, at: pl.BlockSpec(
        (width, n), lambda i: (0, at // n), pipeline_mode=pl.Buffered(1)
    )
    shape = lambda n, dtype: jax.ShapeDtypeStruct((tokens, n), dtype)
    return pl.pallas_call(
        middle_kernel,
        grid=(tokens // TOK,),
        in_specs=[
            tok(width),
            tok(width),
            once(width, 2 * wide),
            once(wide, 0),
            once(wide, wide),
            once(TILE, 2 * wide + width),
            tok(TILE),
            tok(width),
        ],
        out_specs=[
            tok(width),
            tok(width),
            tok(width),
            tok(width),
            tok(wide),
            tok(width),
            tok(width),
            tok(wide),
            pl.BlockSpec((8, width), lambda i: (0, 0)),
        ],
        out_shape=[
            shape(width, bf),
            shape(width, f4),
            shape(width, bf),
            shape(width, bf),
            shape(wide, bf),
            shape(width, bf),
            shape(width, bf),
            shape(wide, bf),
            jax.ShapeDtypeStruct((8, width), f4),
        ],
        scratch_shapes=[
            pltpu.VMEM((2, TOK, FCH), f4),
            pltpu.VMEM((TOK, wide), bf),
            pltpu.VMEM((TOK, width), f4),
            pltpu.VMEM((TOK, width), f4),
        ],
        compiler_params=pltpu.CompilerParams(vmem_limit_bytes=60 << 20),
        name="middle",
    )(hidden, attended, weights, weights, weights, weights, mask, cotangent)


def weight_kernel(
    low_ref, dexp_ref, act_ref, dtwo_ref, att_ref, dbranch_ref, sums_ref, out_ref, turned
):
    step = pl.program_id(0)
    width = low_ref.shape[1]
    parts = (pl.num_programs(0) - 2) // 2

    @pl.when(step == 0)
    def _():
        turned[...] = low_ref[...].T

    @pl.when(step < parts)
    def _():
        out_ref[...] = dot(turned[...], dexp_ref[...]).astype(bf)

    @pl.when((step >= parts) & (step < 2 * parts))
    def _():
        out_ref[...] = dot(act_ref[...].T, dtwo_ref[...]).astype(bf)

    @pl.when(step == 2 * parts)
    def _():
        out_ref[...] = dot(att_ref[...].astype(bf).T, dbranch_ref[...]).astype(bf)

    @pl.when(step == 2 * parts + 1)
    def _():
        rows = sums_ref[...]
        total = jnp.broadcast_to(jnp.sum(rows[4:6], axis=1, keepdims=True), (2, width))
        full = jnp.concatenate([rows[:4], total, jnp.zeros((TILE - 6, width), f4)], axis=0)
        out_ref[:, :TILE] = full.T.astype(bf)


def weight_grads(low, dexp, act, dtwo, att, dbranch, sums):
    tokens, width = low.shape
    wide = dexp.shape[1]
    parts = wide // width
    full = lambda: pl.BlockSpec((tokens, width), lambda j: (0, 0), pipeline_mode=pl.Buffered(1))
    return pl.pallas_call(
        weight_kernel,
        grid=(2 * parts + 2,),
        in_specs=[
            full(),
            pl.BlockSpec((tokens, width), lambda j: (0, jnp.minimum(j, parts - 1))),
            pl.BlockSpec((tokens, width), lambda j: (0, jnp.clip(j - parts, 0, parts - 1))),
            full(),
            full(),
            full(),
            pl.BlockSpec((8, width), lambda j: (0, 0)),
        ],
        out_specs=pl.BlockSpec((width, width), lambda j: (0, j)),
        out_shape=jax.ShapeDtypeStruct((width, 2 * wide + width + TILE), bf),
        scratch_shapes=[pltpu.VMEM((width, tokens), bf)],
        compiler_params=pltpu.CompilerParams(vmem_limit_bytes=48 << 20),
        name="weight_grads",
    )(low, dexp, act, dtwo, att, dbranch, sums)


def digits(count):
    found = [(1, 2)]
    stride = 2
    while stride < count:
        radix = 4 if count // stride >= 4 else 2
        found.append((stride, radix))
        stride *= radix
    return found


def place(relative, count):
    spot = relative * 0
    for stride, radix in digits(count):
        spot = spot * radix + ((relative >> (stride.bit_length() - 1)) & (radix - 1))
    return spot


def mixing(size, count, me):
    per = size // count
    row = np.arange(size)
    target = place(jnp.asarray(row // per, jnp.int32) ^ me, count) * per + (row % per)
    spots = lax.broadcasted_iota(jnp.int32, (size, size), 1)
    return (target[:, None] == spots).astype(bf)


def offset_rows(count, me):
    index = bucket_index(LEN - np.arange(2 * LEN), BUCKETS)
    back = index.reshape(-1, TILE)[:, ::-1].reshape(-1)
    size = 2 * BUCKETS
    per = size // count
    both = np.concatenate([index, back])
    target = place(jnp.asarray(both // per, jnp.int32) ^ me, count) * per + (both % per)
    spots = lax.broadcasted_iota(jnp.int32, (4 * LEN, size), 1)
    return (target[:, None] == spots).astype(bf)


def swap(value, offset, count):
    return lax.ppermute(value, "fsdp", [(i, i ^ offset) for i in range(count)])


def together(values):
    return list(lax.optimization_barrier(tuple(values)))


def gather_pair(first, second, count):
    middle = digits(count)[1:]
    one, two = first[None], second[None]
    for (stride_a, radix_a), (stride_b, radix_b) in zip(middle[::-1], middle):
        got_a = [one]
        got_b = [two]
        for step in range(1, max(radix_a, radix_b)):
            if step < radix_a:
                got_a.append(swap(one, step * stride_a, count))
            if step < radix_b:
                got_b.append(swap(two, step * stride_b, count))
        one, two = together([jnp.concatenate(got_a, axis=0), jnp.concatenate(got_b, axis=0)])
    radices = [radix for _, radix in middle[::-1]]
    two = two.reshape(*radices, *second.shape)
    turn = tuple(range(len(middle)))[::-1]
    two = two.transpose(turn + (len(middle), len(middle) + 1)).reshape(-1, *second.shape)
    return (one, swap(one, 1, count)), (two, swap(two, 1, count))


def scatter_pair(first, second, count):
    middle = digits(count)[1:]
    radices = [radix for _, radix in middle]
    shape_a, shape_b = first.shape[1:], second.shape[1:]
    half_a = first.reshape(2, -1, *shape_a)
    half_b = second.reshape(2, -1, *shape_b)
    one, two = together(
        [
            half_a[0].astype(f4) + swap(half_a[1], 1, count).astype(f4),
            half_b[0].astype(f4) + swap(half_b[1], 1, count).astype(f4),
        ]
    )
    one = one.astype(bf).reshape(*radices, *shape_a)
    two = two.astype(bf).reshape(*radices, *shape_b)
    for step, ((stride_a, radix_a), (stride_b, radix_b)) in enumerate(zip(middle, middle[::-1])):
        last = two.ndim - 3
        got_a = []
        got_b = []
        for hop in range(1, max(radix_a, radix_b)):
            if hop < radix_a:
                got_a.append(swap(one[hop], hop * stride_a, count))
            if hop < radix_b:
                got_b.append(
                    swap(lax.index_in_dim(two, hop, last, keepdims=False), hop * stride_b, count)
                )
        sum_a = one[0].astype(f4)
        sum_b = lax.index_in_dim(two, 0, last, keepdims=False).astype(f4)
        got = together(got_a + got_b)
        for piece in got[: len(got_a)]:
            sum_a = sum_a + piece.astype(f4)
        for piece in got[len(got_a) :]:
            sum_b = sum_b + piece.astype(f4)
        if step == len(middle) - 1:
            return sum_a, sum_b
        one, two = sum_a.astype(bf), sum_b.astype(bf)


def active_chunks(segment, valid):
    rows = segment.reshape(NCH, CH)
    ok = valid.reshape(NCH, CH) > 0
    first = rows[:, 0]
    last = rows[:, -1]
    over = (first[None, :] <= last[:, None]) & (last[None, :] >= first[:, None])
    real = jnp.max(jnp.where(ok, rows, -1), axis=1)
    back = (first[None, :] <= real[:, None]) & (last[None, :] >= first[:, None])
    back = back | back.T
    place_ = jnp.arange(NCH)[None, :]

    def limits(mask):
        lo = jnp.min(jnp.where(mask, place_, NCH), axis=1)
        hi = jnp.max(jnp.where(mask, place_ + 1, 0), axis=1)
        return jnp.where(hi > 0, lo, 0), hi

    return jnp.concatenate(limits(over) + limits(back)).astype(jnp.int32)


def mm(left, right, dims=NN):
    return lax.dot_general(left, right, dims, preferred_element_type=f4)


def shards(
    hidden,
    query_weight,
    key_weight,
    value_weight,
    output_weight,
    relative_table,
    first_gain,
    first_shift,
    expand_weight,
    contract_weight,
    second_gain,
    second_shift,
    segment_ids,
    valid,
    cotangent,
):
    count = lax.axis_size("fsdp")
    me = lax.axis_index("fsdp")
    width = hidden.shape[1]
    wide = expand_weight.shape[1]
    per = query_weight.shape[0]
    per_t = relative_table.shape[0]
    per_c = contract_weight.shape[0]
    parts = wide // width

    pack = jnp.concatenate(
        [
            jnp.concatenate([query_weight, key_weight], axis=1),
            relative_table.reshape(per_t // 2, 2 * width),
        ],
        axis=0,
    )
    pair_a, pair_b = gather_pair(pack, value_weight, count)
    query_key = jnp.concatenate([x[:, :per] for x in pair_a], axis=0)
    query_key = query_key.reshape(count * per, 2 * width)
    table = jnp.concatenate([x[:, per:] for x in pair_a], axis=0).reshape(count * per_t, width)
    value_full = jnp.concatenate(pair_b, axis=0).reshape(count * per, width)

    small = jnp.stack([first_gain, first_shift, second_gain, second_shift], axis=1)
    rest = jnp.concatenate(
        [
            expand_weight.reshape(per, count, parts, per).transpose(0, 2, 1, 3).reshape(per, wide),
            *[contract_weight[n * per : (n + 1) * per] for n in range(parts)],
            output_weight,
            jnp.pad(small, ((0, 0), (0, TILE - 4))),
        ],
        axis=1,
    )
    weights = lax.all_gather(rest, "fsdp", axis=0, tiled=True)

    bounds = active_chunks(segment_ids, valid)
    mix = mixing(width, count, me)
    onehot = offset_rows(count, me)
    segb = jnp.broadcast_to(segment_ids[:, None], (LEN, TILE))
    hidden_mixed = mm(hidden, mix).astype(bf)
    bounds, mix, onehot, segb, hidden_mixed = together([bounds, mix, onehot, segb, hidden_mixed])
    table_mixed = mm(table, mix).astype(bf)
    both_rows = mm(hidden_mixed, query_key).astype(bf)
    value_rows = mm(hidden_mixed, value_full).astype(bf)
    position = mm(table_mixed, query_key).astype(bf)
    spread_rows = mm(onehot[: 2 * LEN], position).astype(bf)
    along_back = mm(onehot[2 * LEN :], position[:, width:]).astype(bf)
    attended_wide, inverse, probs = attend_forward(
        bounds, both_rows, value_rows, spread_rows, segb, segment_ids[None, :]
    )
    mask = jnp.broadcast_to(valid.astype(f4)[:, None], (LEN, TILE))
    result, d_first, d_branch, attended_gradient, activated, d_branch_two, normed_low, d_expanded, rows = middle(
        hidden, attended_wide, weights, wide, mask, cotangent
    )
    grads = weight_grads(
        normed_low, d_expanded, activated, d_branch_two, attended_wide, d_branch, rows
    )
    owned = lax.psum_scatter(grads, "fsdp", scatter_dimension=0, tiled=True).astype(f4)
    query_low, key_low, value_low, along_grad, against_grad = attend_backward(
        bounds,
        both_rows,
        value_rows,
        attended_gradient,
        attended_wide,
        inverse,
        along_back,
        spread_rows,
        probs,
    )
    both = (((0,), (1,)), ((), ()))
    pos_key_low = mm(onehot[2 * LEN :], along_grad, both).astype(bf)
    pos_query_low = mm(onehot[: 2 * LEN], against_grad, both).astype(bf)
    query_mixed, key_mixed = query_key[:, :width], query_key[:, width:]
    grad_query = mm(hidden_mixed, query_low, ROWS_FIRST) + mm(
        table_mixed, pos_query_low, ROWS_FIRST
    )
    grad_key = mm(hidden_mixed, key_low, ROWS_FIRST) + mm(table_mixed, pos_key_low, ROWS_FIRST)
    grad_value = mm(hidden_mixed, value_low, ROWS_FIRST)
    grad_table = mm(pos_query_low, query_mixed, NT) + mm(pos_key_low, key_mixed, NT)
    grad_table = mm(grad_table.astype(bf), mix, NT).astype(bf)
    grad_pack = jnp.concatenate(
        [
            jnp.concatenate([grad_query.astype(bf), grad_key.astype(bf)], axis=1).reshape(
                count, per, 2 * width
            ),
            grad_table.reshape(count, per_t // 2, 2 * width),
        ],
        axis=1,
    )
    grad_value = grad_value.astype(bf).reshape(count, per, width)
    own_pack, own_value = scatter_pair(grad_pack, grad_value, count)
    d_input = (
        mm(query_low, query_mixed, NT) + mm(key_low, key_mixed, NT) + mm(value_low, value_full, NT)
    )
    d_input = d_first + mm(d_input.astype(bf), mix, NT)
    cells = f4(hidden.shape[0] * count * width)
    expand_owned = owned[:, :wide].reshape(per, parts, count, per).transpose(0, 2, 1, 3)
    contract_owned = [owned[:, wide + n * width : wide + (n + 1) * width] for n in range(parts)]
    output_owned = owned[:, 2 * wide : 2 * wide + width]
    last = owned[:, 2 * wide + width : 2 * wide + width + 6]
    return (
        result,
        d_input.astype(bf),
        own_pack[:per, :width],
        own_pack[:per, width:],
        own_value,
        output_owned,
        own_pack[per:].reshape(per_t, width),
        last[:, 0],
        last[:, 1],
        expand_owned.reshape(per, wide),
        jnp.concatenate(contract_owned, axis=0),
        last[:, 2],
        last[:, 3],
        jnp.sqrt(last[0, 4] / cells),
        jnp.sqrt(last[0, 5] / cells),
    )


def solution(mesh):
    in_specs = (
        P("fsdp", None),
        P("fsdp", None),
        P("fsdp", None),
        P("fsdp", None),
        P("fsdp", None),
        P("fsdp", None),
        P("fsdp"),
        P("fsdp"),
        P("fsdp", None),
        P("fsdp", None),
        P("fsdp"),
        P("fsdp"),
        P("fsdp"),
        P("fsdp"),
        P("fsdp", None),
    )
    out_specs = (
        P("fsdp", None),
        P("fsdp", None),
        P("fsdp", None),
        P("fsdp", None),
        P("fsdp", None),
        P("fsdp", None),
        P("fsdp", None),
        P("fsdp"),
        P("fsdp"),
        P("fsdp", None),
        P("fsdp", None),
        P("fsdp"),
        P("fsdp"),
        P(),
        P(),
    )
    return jax.shard_map(shards, mesh=mesh, in_specs=in_specs, out_specs=out_specs, check_vma=False)
```

```python
from functools import partial
import math

import jax
import jax.numpy as jnp
import numpy as np
from jax import lax
from jax.experimental import pallas as pl
from jax.experimental.pallas import tpu as pltpu
from jax.sharding import PartitionSpec as P

bf = jnp.bfloat16
f4 = jnp.float32
HEADS = 12
BUCKETS = 256
LEN = 1024
TILE = 128
CH = 256
NCH = LEN // CH
SCALE = 1.0 / math.sqrt(192.0)
NORM_EPS = 1e-07
MASKED = -1e30
TOK = 256
NEAR = 6
FCH = 768
ROWS_FIRST = (((0,), (0,)), ((), ()))
ROWS_LAST = (((1,), (1,)), ((), ()))
NT = ROWS_LAST
NN = (((1,), (0,)), ((), ()))


def bucket_index(offsets, buckets):
    middle = buckets // 2
    limit = 2 * buckets
    magnitude = np.abs(offsets)
    inside = (offsets < middle) & (offsets > -middle)
    clipped = np.where(inside, middle - 1, magnitude)
    logged = (
        np.ceil(np.log(clipped / middle) / np.log((limit - 1) / middle) * (middle - 1)) + middle
    )
    bucket = np.where(magnitude <= middle, offsets, (logged * np.sign(offsets)).astype(np.int32))
    return np.clip(bucket + buckets, 0, 2 * buckets - 1).astype(np.int32)


def dot(a,b,dims=NN): return lax.dot_general(a,b,dims,preferred_element_type=f4)
def al(x,m): return pl.multiple_of(x,m)
def iotas():
    r=lax.broadcasted_iota(jnp.int32,(TILE,TILE),0); c=lax.broadcasted_iota(jnp.int32,(TILE,TILE),1)
    return r,c


def fwd_kernel(
    b_ref, qa_ref, ka_ref, rk_ref, rq_ref, qb_ref, kb_ref, v_ref, segb_ref, segr_ref,
    att_ref, inv_ref, p_ref,
    xs0, xs1, ys0, ys1, sc0, sc1, mx0, mx1, top, sm, acc,
):
    r, c = iotas()
    eye = (r == c).astype(f4).astype(bf)
    rev = (r + c == TILE - 1).astype(f4).astype(bf)
    early = (r + c) < TILE
    lane = lax.broadcasted_iota(jnp.int32, (CH, TILE), 1)
    left = lane < 64
    lane_t = lax.broadcasted_iota(jnp.int32, (TILE, TILE), 1)
    left_t = lane_t < 64
    step = pl.program_id(0)
    last = pl.num_programs(0) - 1
    fac = SCALE * math.log2(math.e)

    def head(x, h, mask):
        zero = jnp.zeros(x.shape, bf)
        return jnp.where(mask, x, zero) if h == 0 else jnp.where(mask, zero, x)

    def product(ic, slot, xs, ys):
        rows = pl.ds(al(ic * CH, CH), CH)
        w = pl.ds(al((jnp.clip(slot + 3 - ic, 1, NEAR) - 1) * CH, CH), CH)
        out = pl.ds(al(slot * CH, CH), CH)
        q = qa_ref[rows, :]
        k = ka_ref[rows, :]
        for h in range(2):
            xs[h, rows, out] = dot(head(q, h, left), rk_ref[w, :], NT).astype(bf)
            ys[h, rows, out] = dot(head(k, h, left), rq_ref[w, :], NT).astype(bf)

    def skewed(ref, h, row, spot):
        rr = pl.ds(al(row * TILE, TILE), TILE)
        a = ref[h, rr, pl.ds(al((spot + 2) * TILE, TILE), TILE)]
        b = ref[h, rr, pl.ds(al((spot + 1) * TILE, TILE), TILE)]
        return pltpu.roll(jnp.where(early, a, b), 0, 1, stride=1, stride_axis=0)

    def score(ic, jc, xs, ys, sc, mx):
        cols = pl.ds(al(jc * CH, CH), CH)
        segc = segr_ref[:, cols]
        keys = kb_ref[cols, :]
        for s in range(2):
            i = 2 * ic + s
            rows = pl.ds(al(i * TILE, TILE), TILE)
            srow = segb_ref[rows, :]
            q = qb_ref[rows, :]
            for h in range(2):
                turned = [skewed(ys, h, 2 * jc + t, i - t) for t in range(2)]
                lhs = jnp.concatenate([head(q, h, left_t), eye], axis=1)
                rhs = jnp.concatenate([keys, jnp.concatenate(turned, axis=0)], axis=1)
                content = dot(lhs, rhs, NT)
                best = mx[h, rows, :]
                for t in range(2):
                    along = skewed(xs, h, i, 2 * jc + t - s).astype(f4)
                    ok = srow == segc[:, t * TILE : (t + 1) * TILE]
                    val = jnp.where(ok, content[:, t * TILE : (t + 1) * TILE] + along, MASKED)
                    sc[h, rows, pl.ds(al(jc * CH + t * TILE, TILE), TILE)] = val
                    best = jnp.maximum(best, val)
                mx[h, rows, :] = best

    def mix(ic, jc, sc):
        rows = pl.ds(al(ic * CH, CH), CH)
        for h in range(2):
            tot = sm[h]
            peak = top[h]
            for t in range(2):
                cols = pl.ds(al(jc * CH + t * TILE, TILE), TILE)
                e = jnp.exp2((sc[h, rows, cols] - peak) * fac)
                tot = tot + e
                rhs = jnp.concatenate([head(v_ref[cols, :], h, left_t), rev], axis=1)
                res = dot(e.astype(bf), rhs)
                acc[...] += res[:, :TILE]
                p_ref[h, rows, cols] = res[:, TILE:].astype(bf)
            sm[h] = tot

    def open_scores(ic, mx):
        rows = pl.ds(al(ic * CH, CH), CH)
        for h in range(2):
            mx[h, rows, :] = jnp.full((CH, TILE), MASKED, f4)

    def open_mix(ic, mx):
        rows = pl.ds(al(ic * CH, CH), CH)
        for h in range(2):
            peak = jnp.max(mx[h, rows, :], axis=1, keepdims=True)
            top[h] = jnp.broadcast_to(peak, (CH, TILE))
            sm[h] = jnp.zeros((CH, TILE), f4)
        acc[...] = jnp.zeros((CH, TILE), f4)

    def close_mix(ic):
        rows = pl.ds(al(ic * CH, CH), CH)
        inv = [1.0 / jnp.sum(sm[h], axis=1, keepdims=True) for h in range(2)]
        pair = jnp.where(
            left, jnp.broadcast_to(inv[0], (CH, TILE)), jnp.broadcast_to(inv[1], (CH, TILE))
        )
        inv_ref[rows, :] = pair
        att_ref[rows, :] = acc[...] * pair

    def sweep(before, body, after):
        def chunk(ic, _):
            lo = b_ref[ic]
            hi = b_ref[NCH + ic]
            before(ic, lo)

            def block(jc, _):
                body(ic, jc)
                return 0

            lax.fori_loop(lo, hi, block, 0)
            after(ic)
            return 0

        lax.fori_loop(0, NCH, chunk, 0)

    def fused(xs_new, ys_new, xs, ys, sc_new, mx_new, sc, mx):
        def before(ic, lo):
            product(ic, lo, xs_new, ys_new)
            open_scores(ic, mx_new)
            open_mix(ic, mx)

        def body(ic, jc):
            product(ic, jc + 1, xs_new, ys_new)
            mix(ic, jc, sc)
            score(ic, jc, xs, ys, sc_new, mx_new)

        sweep(before, body, close_mix)

    @pl.when(step == 0)
    def _():
        sweep(
            lambda ic, lo: product(ic, lo, xs0, ys0),
            lambda ic, jc: product(ic, jc + 1, xs0, ys0),
            lambda ic: None,
        )

    @pl.when((step > 0) & (step < last) & (step % 2 == 1))
    def _():
        fused(xs1, ys1, xs0, ys0, sc1, mx1, sc0, mx0)

    @pl.when((step > 0) & (step < last) & (step % 2 == 0))
    def _():
        fused(xs0, ys0, xs1, ys1, sc0, mx0, sc1, mx1)

    @pl.when(step == last)
    def _():
        sweep(lambda ic, lo: open_mix(ic, mx0), lambda ic, jc: mix(ic, jc, sc0), close_mix)


def attend_forward(bounds, both, v, spread, segb, segr):
    pairs = v.shape[1] // TILE

    def col(n, lag, at=0, every=2):
        return pl.BlockSpec(
            (n, TILE), lambda s, *_: (0, at + every * jnp.clip(s - lag, 0, pairs - 1))
        )

    def wide(lag):
        return pl.BlockSpec((2, LEN, LEN), lambda s, *_: (jnp.clip(s - lag, 0, pairs - 1), 0, 0))

    window = pltpu.VMEM((2, LEN, LEN + CH), bf)
    return pl.pallas_call(
        fwd_kernel,
        grid_spec=pltpu.PrefetchScalarGridSpec(
            num_scalar_prefetch=1,
            grid=(pairs + 2,),
            in_specs=[
                col(LEN, 0),
                col(LEN, 0, 1),
                col(NEAR * CH, 0, 1),
                col(NEAR * CH, 0),
                col(LEN, 1),
                col(LEN, 1, 1),
                col(LEN, 2, 0, 1),
                pl.BlockSpec((LEN, TILE), lambda s, *_: (0, 0)),
                pl.BlockSpec((1, LEN), lambda s, *_: (0, 0)),
            ],
            out_specs=[col(LEN, 2, 0, 1), col(LEN, 2, 0, 1), wide(2)],
            scratch_shapes=[window] * 4
            + [pltpu.VMEM((2, LEN, LEN), f4)] * 2
            + [pltpu.VMEM((2, LEN, TILE), f4)] * 2
            + [pltpu.VMEM((2, CH, TILE), f4)] * 2
            + [pltpu.VMEM((CH, TILE), f4)],
        ),
        out_shape=[
            jax.ShapeDtypeStruct(v.shape, f4),
            jax.ShapeDtypeStruct(v.shape, f4),
            jax.ShapeDtypeStruct((2 * pairs, LEN, LEN), bf),
        ],
        compiler_params=pltpu.CompilerParams(vmem_limit_bytes=60 << 20),
        name="attend_forward",
    )(bounds, both, both, spread, spread, both, both, v, segb, segr)


def bwd_kernel(
    b_ref, q_ref, k_ref, v_ref, da_ref, att_ref, inv_ref, p_ref, rk_ref, rq_ref,
    dqk_ref, dv_ref, g_ref,
    ws0, ws1, wt0, wt1, dq0, dq1, dkt0, dkt1, dvt0, dvt1, qt0, qt1, kt0, kt1,
    gk0, gk1, gq0, gq1, dat, vr, kr, rkr, dq2, dk2, corr, norm,
):
    r, c = iotas()
    rev = (r + c == TILE - 1).astype(f4).astype(bf)
    late = c >= r
    early = c <= r
    left = lax.broadcasted_iota(jnp.int32, (CH, TILE), 1) < 64
    upper = lax.broadcasted_iota(jnp.int32, (TILE, CH), 0) < 64
    step = pl.program_id(0)
    last = pl.num_programs(0) - 1

    def head(x, h):
        zero = jnp.zeros(x.shape, x.dtype)
        return jnp.where(left, x, zero) if h == 0 else jnp.where(left, zero, x)

    def chunk_of(i):
        return pl.ds(al(i * CH, CH), CH)

    def tile_of(i):
        return pl.ds(al(i * TILE, TILE), TILE)

    def clear(*refs):
        for ref in refs:
            ref[...] = jnp.zeros(ref.shape, ref.dtype)

    def prepare(qt, kt):
        da = (da_ref[...].astype(f4) * inv_ref[...]).astype(bf)
        for t in range(LEN // TILE):
            rows = slice(t * TILE, (t + 1) * TILE)
            vr[rows, :] = dot(rev, v_ref[rows, :]).astype(bf)
            turned = dot(rev, k_ref[rows, :]).astype(bf)
            kr[rows, :] = turned
            kt[:, rows] = turned.T
            qt[:, rows] = q_ref[rows, :].T
            dat[:, rows] = da[rows].T

    def turn_table():
        for t in range(NEAR * CH // TILE):
            rows = slice(t * TILE, (t + 1) * TILE)
            rkr[rows, :] = dot(rev, rk_ref[rows, :]).astype(bf)

    def pads(ic, lo, hi, ws, wt):
        zero = jnp.zeros((CH, CH), bf)
        for h in range(2):
            for ref in (ws, wt):
                ref[h, chunk_of(ic), chunk_of(lo)] = zero
                ref[h, chunk_of(ic), chunk_of(hi + 1)] = zero

    def open_grad(ic, dq):
        rows = chunk_of(ic)
        x = att_ref[rows, :] * da_ref[rows, :].astype(f4)
        pair = inv_ref[rows, :]
        turned = pltpu.roll(pair, 64, 1)
        for h in range(2):
            total = jnp.sum(head(x, h), axis=1, keepdims=True)
            corr[h] = jnp.broadcast_to(total, (CH, TILE))
            norm[h] = jnp.where(left, pair, turned) if h == 0 else jnp.where(left, turned, pair)
        dq[rows, :] = jnp.zeros((CH, TILE), f4)

    def both_heads(first, second):
        return jnp.where(left, first, second)

    def grad_start(ic, jc):
        rows, cols = chunk_of(ic), chunk_of(jc)
        da = da_ref[rows, :]
        values = vr[cols, :]
        return [dot(head(da, h), values, NT) for h in range(2)]

    def grad_scores(ic, jc, dps):
        rows, cols = chunk_of(ic), chunk_of(jc)
        parts = []
        for h in range(2):
            p = p_ref[h, rows, cols]
            d, iv = corr[h], norm[h]
            parts.append(
                [
                    (
                        p[:, t * TILE : (t + 1) * TILE].astype(f4)
                        * ((dps[h][:, t * TILE : (t + 1) * TILE] - d) * iv)
                    ).astype(bf)
                    for t in range(2)
                ]
            )
        return parts

    def grad_skew(ic, jc, parts, ws, wt):
        for h in range(2):
            for t in range(2):
                for s in range(2):
                    sr = slice(s * TILE, (s + 1) * TILE)
                    ws[h, tile_of(2 * ic + s), tile_of(2 * jc + 2 + t)] = pltpu.roll(
                        parts[h][t][sr], 0, 1, stride=1, stride_axis=0
                    )
                    wt[h, tile_of(2 * jc + t), tile_of(2 * ic + 2 + s)] = pltpu.roll(
                        parts[h][t][sr].T, 1, 1, stride=1, stride_axis=0
                    )

    def grad_values(ic, jc, dvt):
        rows, cols = chunk_of(ic), chunk_of(jc)
        for h in range(2):
            half = slice(h * 64, (h + 1) * 64)
            dvt[half, cols] += dot(dat[half, rows], p_ref[h, rows, cols])

    def grad_out(ic, jc, parts, dq, dkt, qt):
        rows, cols = chunk_of(ic), chunk_of(jc)
        keys = kr[cols, :]
        whole = [jnp.concatenate(parts[h], axis=1) for h in range(2)]
        dq[rows, :] += both_heads(dot(whole[0], keys), dot(whole[1], keys))
        for h in range(2):
            half = slice(h * 64, (h + 1) * 64)
            dkt[half, cols] += dot(qt[half, rows], whole[h])

    def fold(ic, slot, first, ws, wt, qt, kt, gk, gq):
        rows = chunk_of(ic)
        w = chunk_of(jnp.clip(slot + 3 - ic, 1, NEAR) - 1)
        for ref, mask, table, out, turned, g in (
            (ws, late, rkr, dq2, qt, gk),
            (wt, early, rq_ref, dk2, kt, gq),
        ):
            rels = table[w, :]
            outs = []
            for h in range(2):
                band = []
                for s in range(2):
                    line = []
                    for b in range(2):
                        spot = 2 * slot + s + b
                        x = ref[h, tile_of(2 * ic + s), tile_of(spot)]
                        y = ref[h, tile_of(2 * ic + s), tile_of(spot + 1)]
                        line.append(jnp.where(mask, x, y))
                    band.append(jnp.concatenate(line, axis=1))
                band = jnp.concatenate(band, axis=0)
                outs.append(dot(band, rels))
                half = slice(h * 64, (h + 1) * 64)
                g[half, w] += dot(turned[half, rows], band)
            if first:
                out[rows, :] = both_heads(*outs)
            else:
                out[rows, :] += both_heads(*outs)

    def close(ic, dq, dkt, dvt):
        rows = chunk_of(ic)
        dqk_ref[rows, :TILE] = ((dq[rows, :] + dq2[rows, :]) * SCALE).astype(bf)
        for t in range(2):
            tr = tile_of(2 * ic + t)
            x = ((dkt[:, tr].T + dk2[tr, :]) * SCALE).astype(bf)
            dqk_ref[tr, TILE:] = dot(rev, x).astype(bf)
            dv_ref[tr, :] = dot(rev, dvt[:, tr].T.astype(bf)).astype(bf)
        dkt[:, rows] = jnp.zeros((TILE, CH), f4)
        dvt[:, rows] = jnp.zeros((TILE, CH), f4)

    def flush(gk, gq):
        g_ref[:TILE, :] = (gq[...] * SCALE).astype(bf)
        for t in range(NEAR * CH // TILE):
            cols = slice(t * TILE, (t + 1) * TILE)
            g_ref[TILE:, cols] = dot((gk[:, cols] * SCALE).astype(bf), rev).astype(bf)

    def sweep(before, body, idle):
        def chunk(ic, _):
            lo = b_ref[2 * NCH + ic]
            hi = b_ref[3 * NCH + ic]

            @pl.when(hi > lo)
            def _():
                before(ic, lo, hi)

            @pl.when(hi <= lo)
            def _():
                idle(ic)

            def block(jc, _):
                body(ic, jc)
                return 0

            lax.fori_loop(lo, hi, block, 0)
            return 0

        lax.fori_loop(0, NCH, chunk, 0)

    def no_fold(ic):
        dq2[chunk_of(ic), :] = jnp.zeros((CH, TILE), f4)
        dk2[chunk_of(ic), :] = jnp.zeros((CH, TILE), f4)

    def no_grad(ic, dq):
        dq[chunk_of(ic), :] = jnp.zeros((CH, TILE), f4)

    def fused(new, old):
        ws, wt, dq, dkt, dvt, qt, kt, gk_next, gq_next = new
        ws_, wt_, dq_, dkt_, dvt_, qt_, kt_, gk, gq = old
        prepare(qt, kt)
        turn_table()

        def before(ic, lo, hi):
            @pl.when(step < 2)
            def _():
                pads(ic, lo, hi, ws, wt)

            fold(ic, lo, True, ws_, wt_, qt_, kt_, gk, gq)
            open_grad(ic, dq)

        def body(ic, jc):
            dps = grad_start(ic, jc)
            fold(ic, jc + 1, False, ws_, wt_, qt_, kt_, gk, gq)
            grad_values(ic, jc, dvt)
            parts = grad_scores(ic, jc, dps)
            grad_skew(ic, jc, parts, ws, wt)
            grad_out(ic, jc, parts, dq, dkt, qt)

        def idle(ic):
            no_fold(ic)
            no_grad(ic, dq)

        sweep(before, body, idle)

        def finish(ic, _):
            close(ic, dq_, dkt_, dvt_)
            return 0

        lax.fori_loop(0, NCH, finish, 0)
        flush(gk, gq)
        clear(gk, gq)

    set0 = (ws0, wt0, dq0, dkt0, dvt0, qt0, kt0, gk0, gq0)
    set1 = (ws1, wt1, dq1, dkt1, dvt1, qt1, kt1, gk1, gq1)

    @pl.when(step == 0)
    def _():
        clear(dkt0, dkt1, dvt0, dvt1, gk0, gk1, gq0, gq1)
        prepare(qt0, kt0)

        def before(ic, lo, hi):
            pads(ic, lo, hi, ws0, wt0)
            open_grad(ic, dq0)

        def body(ic, jc):
            parts = grad_scores(ic, jc, grad_start(ic, jc))
            grad_values(ic, jc, dvt0)
            grad_skew(ic, jc, parts, ws0, wt0)
            grad_out(ic, jc, parts, dq0, dkt0, qt0)

        sweep(before, body, lambda ic: no_grad(ic, dq0))

    @pl.when((step > 0) & (step < last) & (step % 2 == 1))
    def _():
        fused(set1, set0)

    @pl.when((step > 0) & (step < last) & (step % 2 == 0))
    def _():
        fused(set0, set1)

    @pl.when(step == last)
    def _():
        turn_table()
        sweep(
            lambda ic, lo, hi: fold(ic, lo, True, ws1, wt1, qt1, kt1, gk1, gq1),
            lambda ic, jc: fold(ic, jc + 1, False, ws1, wt1, qt1, kt1, gk1, gq1),
            no_fold,
        )

        def finish(ic, _):
            close(ic, dq1, dkt1, dvt1)
            return 0

        lax.fori_loop(0, NCH, finish, 0)
        flush(gk1, gq1)


def attend_backward(bounds, both, v, da, att, inv, spread, p):
    pairs = v.shape[1] // TILE

    def col(n, lag, at=0, every=1):
        return pl.BlockSpec(
            (n, TILE), lambda s, *_: (0, at + every * jnp.clip(s - lag, 0, pairs - 1))
        )

    def out(at):
        return lambda s, *_: (jnp.clip(s - 1, 0, pairs - 1), 0)[:: 1 - 2 * at]

    def twice(shape, dtype):
        return [pltpu.VMEM(shape, dtype)] * 2

    return pl.pallas_call(
        bwd_kernel,
        grid_spec=pltpu.PrefetchScalarGridSpec(
            num_scalar_prefetch=1,
            grid=(pairs + 1,),
            in_specs=[
                col(LEN, 0, 0, 2),
                col(LEN, 0, 1, 2),
                col(LEN, 0),
                col(LEN, 0),
                col(LEN, 0),
                col(LEN, 0),
                pl.BlockSpec((2, LEN, LEN), lambda s, *_: (jnp.minimum(s, pairs - 1), 0, 0)),
                col(NEAR * CH, 1, 1, 2),
                col(NEAR * CH, 1, 0, 2),
            ],
            out_specs=[
                pl.BlockSpec((LEN, 2 * TILE), out(1)),
                col(LEN, 1),
                pl.BlockSpec((2 * TILE, NEAR * CH), out(0)),
            ],
            scratch_shapes=twice((2, LEN, LEN + 2 * CH), bf)
            + twice((2, LEN, LEN + 2 * CH), bf)
            + twice((LEN, TILE), f4)
            + twice((TILE, LEN), f4)
            + twice((TILE, LEN), f4)
            + twice((TILE, LEN), bf)
            + twice((TILE, LEN), bf)
            + twice((TILE, NEAR * CH), f4)
            + twice((TILE, NEAR * CH), f4)
            + [pltpu.VMEM((TILE, LEN), bf)]
            + [pltpu.VMEM((LEN, TILE), bf)] * 2
            + [pltpu.VMEM((NEAR * CH, TILE), bf)]
            + [pltpu.VMEM((LEN, TILE), f4)] * 2
            + [pltpu.VMEM((2, CH, TILE), f4)] * 2,
        ),
        out_shape=[
            jax.ShapeDtypeStruct(both.shape, bf),
            jax.ShapeDtypeStruct(v.shape, bf),
            jax.ShapeDtypeStruct((both.shape[1], NEAR * CH), bf),
        ],
        compiler_params=pltpu.CompilerParams(vmem_limit_bytes=60 << 20),
        name="attend_backward",
    )(bounds, both, both, v, da, att, inv, p, spread, spread)


def gelu_pair(u):
    size = jnp.abs(u)
    bell = jnp.exp2(u * u * (-0.5 * math.log2(math.e)))
    t = 1.0 / (1.0 + (0.3275911 / math.sqrt(2.0)) * size)
    poly = 0.5 * 1.061405429
    for c in (-1.453152027, 1.421413741, -0.284496736, 0.254829592):
        poly = poly * t + 0.5 * c
    tail = poly * t * bell
    phi = jnp.where(u < 0.0, tail, 1.0 - tail)
    return u * phi, phi + u * bell * (1.0 / math.sqrt(2.0 * math.pi))


def middle_kernel(
    hid_ref, att_ref, wo_ref, we_ref, wc_ref, vec_ref, mask_ref, cot_ref,
    out_ref, dfirst_ref, dbranch_ref, datt_ref, act_ref, dtwo_ref, low_ref, dexp_ref, sums_ref,
    pre, slope, acc, norm_,
):
    width = hid_ref.shape[1]
    chunks = we_ref.shape[1] // FCH
    vectors = vec_ref[...].astype(f4).T
    gain_one = vectors[0:1, :]
    shift_one = vectors[1:2, :]
    gain_two = vectors[2:3, :]
    shift_two = vectors[3:4, :]
    inv = 1.0 / width
    first = hid_ref[...].astype(f4) + dot(att_ref[...].astype(bf), wo_ref[...])
    cen = first - jnp.sum(first, axis=1, keepdims=True) * inv
    rstd_one = lax.rsqrt(jnp.sum(cen * cen, axis=1, keepdims=True) * inv + NORM_EPS)
    n_one = cen * rstd_one
    norm_[...] = n_one
    normed = n_one * gain_one + shift_one
    low_ref[...] = normed.astype(bf)
    acc[...] = jnp.zeros(acc.shape, f4)

    def cols(c):
        return slice(c * FCH, (c + 1) * FCH)

    def expand(c):
        pre[c % 2] = dot(low_ref[...], we_ref[:, cols(c)])

    def bend(c):
        value, grad = gelu_pair(pre[c % 2])
        act_ref[:, cols(c)] = value.astype(bf)
        slope[:, cols(c)] = grad.astype(bf)

    def contract(c):
        acc[...] += dot(act_ref[:, cols(c)], wc_ref[:, cols(c)])

    expand(0)
    expand(1)
    bend(0)

    def steady(c, _):
        expand(c + 1)
        bend(c)
        contract(c - 1)
        return 0

    for c in range(1, chunks - 1):
        steady(c, 0)
    bend(chunks - 1)
    contract(chunks - 2)
    contract(chunks - 1)
    branch = acc[...]
    mask = mask_ref[:, 0:1]
    normed = norm_[...] * gain_one + shift_one
    second = normed + branch
    row_res = jnp.sum(mask * second * second, axis=0, keepdims=True)
    row_sub = jnp.sum(mask * branch * branch, axis=0, keepdims=True)
    cen = second - jnp.sum(second, axis=1, keepdims=True) * inv
    rstd = lax.rsqrt(jnp.sum(cen * cen, axis=1, keepdims=True) * inv + NORM_EPS)
    n_two = cen * rstd
    out_ref[...] = (n_two * gain_two + shift_two).astype(bf)
    up = cot_ref[...].astype(f4) * mask
    row_g2 = jnp.sum(up * n_two, axis=0, keepdims=True)
    row_s2 = jnp.sum(up, axis=0, keepdims=True)
    g = up * gain_two
    d_second = (
        g
        - jnp.sum(g, axis=1, keepdims=True) * inv
        - n_two * (jnp.sum(g * n_two, axis=1, keepdims=True) * inv)
    ) * rstd
    dtwo_ref[...] = d_second.astype(bf)
    acc[...] = d_second

    def back(c):
        grad = dot(dtwo_ref[...], wc_ref[:, cols(c)], NT) * slope[:, cols(c)].astype(f4)
        dexp_ref[:, cols(c)] = grad.astype(bf)

    def into(c):
        acc[...] += dot(dexp_ref[:, cols(c)], we_ref[:, cols(c)], NT)

    back(0)

    def steady_back(c, _):
        back(c)
        into(c - 1)
        return 0

    for c in range(1, chunks):
        steady_back(c, 0)
    into(chunks - 1)
    up = acc[...]
    n_one = norm_[...]
    row_g1 = jnp.sum(up * n_one, axis=0, keepdims=True)
    row_s1 = jnp.sum(up, axis=0, keepdims=True)
    g = up * gain_one
    d_first = (
        g
        - jnp.sum(g, axis=1, keepdims=True) * inv
        - n_one * (jnp.sum(g * n_one, axis=1, keepdims=True) * inv)
    ) * rstd_one
    dfirst_ref[...] = d_first
    low = d_first.astype(bf)
    dbranch_ref[...] = low
    datt_ref[...] = dot(low, wo_ref[...], NT).astype(bf)
    rows = jnp.concatenate(
        [row_g1, row_s1, row_g2, row_s2, row_res, row_sub, jnp.zeros((2, width), f4)], axis=0
    )

    @pl.when(pl.program_id(0) == 0)
    def _():
        sums_ref[...] = rows

    @pl.when(pl.program_id(0) > 0)
    def _():
        sums_ref[...] += rows


def middle(hidden, attended, weights, wide, mask, cotangent):
    tokens, width = hidden.shape
    tok = lambda n: pl.BlockSpec((TOK, n), lambda i: (i, 0))
    once = lambda n, at: pl.BlockSpec(
        (width, n), lambda i: (0, at // n), pipeline_mode=pl.Buffered(1)
    )
    shape = lambda n, dtype: jax.ShapeDtypeStruct((tokens, n), dtype)
    return pl.pallas_call(
        middle_kernel,
        grid=(tokens // TOK,),
        in_specs=[
            tok(width),
            tok(width),
            once(width, 2 * wide),
            once(wide, 0),
            once(wide, wide),
            once(TILE, 2 * wide + width),
            tok(TILE),
            tok(width),
        ],
        out_specs=[
            tok(width),
            tok(width),
            tok(width),
            tok(width),
            tok(wide),
            tok(width),
            tok(width),
            tok(wide),
            pl.BlockSpec((8, width), lambda i: (0, 0)),
        ],
        out_shape=[
            shape(width, bf),
            shape(width, f4),
            shape(width, bf),
            shape(width, bf),
            shape(wide, bf),
            shape(width, bf),
            shape(width, bf),
            shape(wide, bf),
            jax.ShapeDtypeStruct((8, width), f4),
        ],
        scratch_shapes=[
            pltpu.VMEM((2, TOK, FCH), f4),
            pltpu.VMEM((TOK, wide), bf),
            pltpu.VMEM((TOK, width), f4),
            pltpu.VMEM((TOK, width), f4),
        ],
        compiler_params=pltpu.CompilerParams(vmem_limit_bytes=60 << 20),
        name="middle",
    )(hidden, attended, weights, weights, weights, weights, mask, cotangent)


def weight_kernel(
    low_ref, dexp_ref, act_ref, dtwo_ref, att_ref, dbranch_ref, sums_ref, out_ref, turned
):
    step = pl.program_id(0)
    width = low_ref.shape[1]
    parts = (pl.num_programs(0) - 2) // 2

    @pl.when(step == 0)
    def _():
        turned[...] = low_ref[...].T

    @pl.when(step < parts)
    def _():
        out_ref[...] = dot(turned[...], dexp_ref[...]).astype(bf)

    @pl.when((step >= parts) & (step < 2 * parts))
    def _():
        out_ref[...] = dot(act_ref[...].T, dtwo_ref[...]).astype(bf)

    @pl.when(step == 2 * parts)
    def _():
        out_ref[...] = dot(att_ref[...].astype(bf).T, dbranch_ref[...]).astype(bf)

    @pl.when(step == 2 * parts + 1)
    def _():
        rows = sums_ref[...]
        total = jnp.broadcast_to(jnp.sum(rows[4:6], axis=1, keepdims=True), (2, width))
        full = jnp.concatenate([rows[:4], total, jnp.zeros((TILE - 6, width), f4)], axis=0)
        out_ref[:, :TILE] = full.T.astype(bf)


def weight_grads(low, dexp, act, dtwo, att, dbranch, sums):
    tokens, width = low.shape
    wide = dexp.shape[1]
    parts = wide // width
    full = lambda: pl.BlockSpec((tokens, width), lambda j: (0, 0), pipeline_mode=pl.Buffered(1))
    return pl.pallas_call(
        weight_kernel,
        grid=(2 * parts + 2,),
        in_specs=[
            full(),
            pl.BlockSpec((tokens, width), lambda j: (0, jnp.minimum(j, parts - 1))),
            pl.BlockSpec((tokens, width), lambda j: (0, jnp.clip(j - parts, 0, parts - 1))),
            full(),
            full(),
            full(),
            pl.BlockSpec((8, width), lambda j: (0, 0)),
        ],
        out_specs=pl.BlockSpec((width, width), lambda j: (0, j)),
        out_shape=jax.ShapeDtypeStruct((width, 2 * wide + width + TILE), bf),
        scratch_shapes=[pltpu.VMEM((width, tokens), bf)],
        compiler_params=pltpu.CompilerParams(vmem_limit_bytes=60 << 20),
        name="weight_grads",
    )(low, dexp, act, dtwo, att, dbranch, sums)


def lane_pieces(size, count, parts, per, forward):
    found = [[] for _ in range(size // TILE)]
    for device in range(count):
        for part in range(parts):
            source = (device * parts + part) * per
            target = part * count * per + device * per
            if not forward:
                source, target = target, source
            done = 0
            while done < per:
                at, to = source + done, target + done
                span = min(per - done, TILE - at % TILE, TILE - to % TILE)
                found[to // TILE].append((at // TILE, at % TILE, to % TILE, span))
                done += span
    return found


def permute_lanes(load, store, rows, pieces):
    lane = lax.broadcasted_iota(jnp.int32, (rows, TILE), 1)
    for block, group in enumerate(pieces):
        total = jnp.zeros((rows, TILE), f4)
        for at, offset, spot, span in group:
            moved = load(at)
            if spot != offset:
                moved = pltpu.roll(moved, (spot - offset) % TILE, 1)
            total = jnp.where((lane >= spot) & (lane < spot + span), moved, total)
        store(block, total)


def lanes(block):
    return slice(block * TILE, (block + 1) * TILE)


def pack_kernel(count, expand_ref, contract_ref, output_ref, small_ref, out_ref):
    per, wide = expand_ref.shape
    width = output_ref.shape[1]
    parts = wide // width

    def store(block, value):
        out_ref[:, lanes(block)] = value.astype(bf)

    permute_lanes(
        lambda at: expand_ref[:, lanes(at)].astype(f4),
        store,
        per,
        lane_pieces(wide, count, parts, per, True),
    )
    rows = contract_ref[...].astype(f4)
    for part in range(parts):
        at = wide + part * width
        out_ref[:, at : at + width] = rows[part * per : (part + 1) * per].astype(bf)
    out_ref[:, 2 * wide : 2 * wide + width] = output_ref[...]
    out_ref[:, 2 * wide + width :] = small_ref[...]


def pack_weights(count, expand, contract, output, small):
    per, wide = expand.shape
    return pl.pallas_call(
        partial(pack_kernel, count),
        out_shape=jax.ShapeDtypeStruct((per, 2 * wide + output.shape[1] + TILE), bf),
        name="pack_weights",
    )(expand, contract, output, small)


def finish_kernel(count, own_ref, expand_ref, contract_ref, output_ref, small_ref):
    per, wide = expand_ref.shape
    width = output_ref.shape[1]
    parts = wide // width

    def store(block, value):
        expand_ref[:, lanes(block)] = value

    permute_lanes(
        lambda at: own_ref[:, lanes(at)].astype(f4),
        store,
        per,
        lane_pieces(wide, count, parts, per, False),
    )
    for part in range(parts):
        at = wide + part * width
        contract_ref[part * per : (part + 1) * per, :] = own_ref[:, at : at + width].astype(f4)
    output_ref[...] = own_ref[:, 2 * wide : 2 * wide + width].astype(f4)
    small_ref[...] = own_ref[:, 2 * wide + width :].astype(f4)


def finish_grads(count, own, wide, width):
    per = own.shape[0]
    shape = lambda a, b: jax.ShapeDtypeStruct((a, b), f4)
    return pl.pallas_call(
        partial(finish_kernel, count),
        out_shape=[
            shape(per, wide),
            shape(per * (wide // width), width),
            shape(per, width),
            shape(per, TILE),
        ],
        name="finish_grads",
    )(own)


def digits(count):
    found = [(1, 2)]
    stride = 2
    while stride < count:
        radix = 4 if count // stride >= 4 else 2
        found.append((stride, radix))
        stride *= radix
    return found


def place(relative, count):
    spot = relative * 0
    for stride, radix in digits(count):
        spot = spot * radix + ((relative >> (stride.bit_length() - 1)) & (radix - 1))
    return spot


def mixing(size, count, me):
    per = size // count
    row = np.arange(size)
    target = place(jnp.asarray(row // per, jnp.int32) ^ me, count) * per + (row % per)
    spots = lax.broadcasted_iota(jnp.int32, (size, size), 1)
    return (target[:, None] == spots).astype(bf)


def near_index():
    index = bucket_index(LEN - np.arange(2 * LEN), BUCKETS).reshape(-1, CH)
    assert (index[:2] == index[0, 0]).all() and (index[-2:] == index[-1, -1]).all()
    return index[1:-1].reshape(-1)


def offset_rows(count, me):
    index = near_index()
    size = 2 * BUCKETS
    per = size // count
    target = place(jnp.asarray(index // per, jnp.int32) ^ me, count) * per + (index % per)
    spots = lax.broadcasted_iota(jnp.int32, (index.shape[0], size), 1)
    return (target[:, None] == spots).astype(bf)


def swap(value, offset, count):
    return lax.ppermute(value, "fsdp", [(i, i ^ offset) for i in range(count)])


def together(values):
    return list(lax.optimization_barrier(tuple(values)))


def gather_pair(first, second, count, held):
    middle = digits(count)[1:]
    one, two = first[None], second[None]
    later = None
    for (stride_a, radix_a), (stride_b, radix_b) in zip(middle[::-1], middle):
        got_a = [one]
        got_b = [two]
        for step in range(1, max(radix_a, radix_b)):
            if step < radix_a:
                got_a.append(swap(one, step * stride_a, count))
            if step < radix_b:
                got_b.append(swap(two, step * stride_b, count))
        one, two, *held = together(
            [jnp.concatenate(got_a, axis=0), jnp.concatenate(got_b, axis=0), *held]
        )
        if later is None:
            later, held = held, []
    radices = [radix for _, radix in middle[::-1]]
    two = two.reshape(*radices, *second.shape)
    turn = tuple(range(len(middle)))[::-1]
    two = two.transpose(turn + (len(middle), len(middle) + 1)).reshape(-1, *second.shape)
    return (one, swap(one, 1, count)), (two, swap(two, 1, count)), later


def scatter_pair(first, second, count):
    middle = digits(count)[1:]
    radices = [radix for _, radix in middle]
    shape_a, shape_b = first.shape[1:], second.shape[1:]
    half_a = first.reshape(2, -1, *shape_a)
    half_b = second.reshape(2, -1, *shape_b)
    one, two = together(
        [
            half_a[0].astype(f4) + swap(half_a[1], 1, count).astype(f4),
            half_b[0].astype(f4) + swap(half_b[1], 1, count).astype(f4),
        ]
    )
    one = one.astype(bf).reshape(*radices, *shape_a)
    two = two.astype(bf).reshape(*radices, *shape_b)
    for step, ((stride_a, radix_a), (stride_b, radix_b)) in enumerate(zip(middle, middle[::-1])):
        last = two.ndim - 3
        got_a = []
        got_b = []
        for hop in range(1, max(radix_a, radix_b)):
            if hop < radix_a:
                got_a.append(swap(one[hop], hop * stride_a, count))
            if hop < radix_b:
                got_b.append(
                    swap(lax.index_in_dim(two, hop, last, keepdims=False), hop * stride_b, count)
                )
        sum_a = one[0].astype(f4)
        sum_b = lax.index_in_dim(two, 0, last, keepdims=False).astype(f4)
        got = together(got_a + got_b)
        for piece in got[: len(got_a)]:
            sum_a = sum_a + piece.astype(f4)
        for piece in got[len(got_a) :]:
            sum_b = sum_b + piece.astype(f4)
        if step == len(middle) - 1:
            return sum_a, sum_b
        one, two = sum_a.astype(bf), sum_b.astype(bf)


def active_chunks(segment, valid):
    rows = segment.reshape(NCH, CH)
    ok = valid.reshape(NCH, CH) > 0
    first = rows[:, 0]
    last = rows[:, -1]
    over = (first[None, :] <= last[:, None]) & (last[None, :] >= first[:, None])
    real = jnp.max(jnp.where(ok, rows, -1), axis=1)
    back = (first[None, :] <= real[:, None]) & (last[None, :] >= first[:, None])
    back = back | back.T
    place_ = jnp.arange(NCH)[None, :]

    def limits(mask):
        lo = jnp.min(jnp.where(mask, place_, NCH), axis=1)
        hi = jnp.max(jnp.where(mask, place_ + 1, 0), axis=1)
        return jnp.where(hi > 0, lo, 0), hi

    return jnp.concatenate(limits(over) + limits(back)).astype(jnp.int32)


def weave(first, second):
    cut = lambda x: x.reshape(x.shape[0], -1, 1, TILE)
    return jnp.concatenate([cut(first), cut(second)], axis=2).reshape(first.shape[0], -1)


def mm(left, right, dims=NN):
    return lax.dot_general(left, right, dims, preferred_element_type=f4)


def shards(
    hidden,
    query_weight,
    key_weight,
    value_weight,
    output_weight,
    relative_table,
    first_gain,
    first_shift,
    expand_weight,
    contract_weight,
    second_gain,
    second_shift,
    segment_ids,
    valid,
    cotangent,
):
    count = lax.axis_size("fsdp")
    me = lax.axis_index("fsdp")
    width = hidden.shape[1]
    wide = expand_weight.shape[1]
    per = query_weight.shape[0]
    per_t = relative_table.shape[0]
    per_c = contract_weight.shape[0]
    parts = wide // width

    pair_a, pair_b, held = gather_pair(
        weave(query_weight, key_weight),
        jnp.concatenate([value_weight, relative_table], axis=0),
        count,
        [
            expand_weight,
            contract_weight,
            output_weight,
            first_gain,
            first_shift,
            second_gain,
            second_shift,
        ],
    )
    expand_weight, contract_weight, output_weight = held[:3]
    query_key = jnp.concatenate(pair_a, axis=0).reshape(count * per, 2 * width)
    value_full = jnp.concatenate([x[:, :per] for x in pair_b], axis=0)
    value_full = value_full.reshape(count * per, width)
    table = jnp.concatenate([x[:, per:] for x in pair_b], axis=0).reshape(count * per_t, width)

    small = jnp.stack(held[3:], axis=1)
    small = jnp.pad(small, ((0, 0), (0, TILE - 4)))
    rest = pack_weights(count, expand_weight, contract_weight, output_weight, small)
    weights = lax.all_gather(rest, "fsdp", axis=0, tiled=True)

    bounds = active_chunks(segment_ids, valid)
    mix = mixing(width, count, me)
    onehot = offset_rows(count, me)
    segb = jnp.broadcast_to(segment_ids[:, None], (LEN, TILE))
    hidden_mixed = mm(hidden, mix).astype(bf)
    bounds, mix, onehot, segb, hidden_mixed = together([bounds, mix, onehot, segb, hidden_mixed])
    table_mixed = mm(table, mix).astype(bf)
    both_rows = mm(hidden_mixed, query_key).astype(bf)
    value_rows = mm(hidden_mixed, value_full).astype(bf)
    position = mm(table_mixed, query_key).astype(bf)
    spread_rows = mm(onehot, position).astype(bf)
    attended_wide, inverse, probs = attend_forward(
        bounds, both_rows, value_rows, spread_rows, segb, segment_ids[None, :]
    )
    mask = jnp.broadcast_to(valid.astype(f4)[:, None], (LEN, TILE))
    result, d_first, d_branch, attended_gradient, activated, d_branch_two, normed_low, d_expanded, rows = middle(
        hidden, attended_wide, weights, wide, mask, cotangent
    )
    grads = weight_grads(
        normed_low, d_expanded, activated, d_branch_two, attended_wide, d_branch, rows
    )
    owned = lax.psum_scatter(grads, "fsdp", scatter_dimension=0, tiled=True)
    both_low, value_low, offset_grad = attend_backward(
        bounds,
        both_rows,
        value_rows,
        attended_gradient,
        attended_wide,
        inverse,
        spread_rows,
        probs,
    )
    position_low = mm(offset_grad, onehot).astype(bf)
    grad_pack = mm(hidden_mixed, both_low, ROWS_FIRST) + mm(
        table_mixed, position_low, (((0,), (1,)), ((), ()))
    )
    grad_pack = grad_pack.astype(bf).reshape(count, per, 2 * width)
    grad_value = mm(hidden_mixed, value_low, ROWS_FIRST)
    grad_table = mm(position_low, query_key, (((0,), (1,)), ((), ())))
    grad_table = mm(grad_table.astype(bf), mix, NT).astype(bf)
    grad_value = jnp.concatenate(
        [
            grad_value.astype(bf).reshape(count, per, width),
            grad_table.reshape(count, per_t, width),
        ],
        axis=1,
    )
    own_pack, own_value = scatter_pair(grad_pack, grad_value, count)
    d_input = mm(both_low, query_key, NT) + mm(value_low, value_full, NT)
    d_input = d_first + mm(d_input.astype(bf), mix, NT)
    cells = f4(hidden.shape[0] * count * width)
    expand_owned, contract_owned, output_owned, last = finish_grads(count, owned, wide, width)
    own_pack = own_pack.reshape(per, -1, 2, TILE)
    return (
        result,
        d_input.astype(bf),
        own_pack[:, :, 0].reshape(per, width),
        own_pack[:, :, 1].reshape(per, width),
        own_value[:per],
        output_owned,
        own_value[per:],
        last[:, 0],
        last[:, 1],
        expand_owned,
        contract_owned,
        last[:, 2],
        last[:, 3],
        jnp.sqrt(last[0, 4] / cells),
        jnp.sqrt(last[0, 5] / cells),
    )


def solution(mesh):
    in_specs = (
        P("fsdp", None),
        P("fsdp", None),
        P("fsdp", None),
        P("fsdp", None),
        P("fsdp", None),
        P("fsdp", None),
        P("fsdp"),
        P("fsdp"),
        P("fsdp", None),
        P("fsdp", None),
        P("fsdp"),
        P("fsdp"),
        P("fsdp"),
        P("fsdp"),
        P("fsdp", None),
    )
    out_specs = (
        P("fsdp", None),
        P("fsdp", None),
        P("fsdp", None),
        P("fsdp", None),
        P("fsdp", None),
        P("fsdp", None),
        P("fsdp", None),
        P("fsdp"),
        P("fsdp"),
        P("fsdp", None),
        P("fsdp", None),
        P("fsdp"),
        P("fsdp"),
        P(),
        P(),
    )
    return jax.shard_map(shards, mesh=mesh, in_specs=in_specs, out_specs=out_specs, check_vma=False)
```

```python
from functools import partial
import math

import jax
import jax.numpy as jnp
import numpy as np
from jax import lax
from jax.experimental import pallas as pl
from jax.experimental.pallas import tpu as pltpu
from jax.sharding import PartitionSpec as P

bf = jnp.bfloat16
f4 = jnp.float32
HEADS = 12
BUCKETS = 256
LEN = 1024
TILE = 128
CH = 256
NCH = LEN // CH
SCALE = 1.0 / math.sqrt(192.0)
NORM_EPS = 1e-07
MASKED = -1e30
TOK = 256
NEAR = 6
FCH = 768
ROWS_FIRST = (((0,), (0,)), ((), ()))
ROWS_LAST = (((1,), (1,)), ((), ()))
NT = ROWS_LAST
NN = (((1,), (0,)), ((), ()))


def bucket_index(offsets, buckets):
    middle = buckets // 2
    limit = 2 * buckets
    magnitude = np.abs(offsets)
    inside = (offsets < middle) & (offsets > -middle)
    clipped = np.where(inside, middle - 1, magnitude)
    logged = (
        np.ceil(np.log(clipped / middle) / np.log((limit - 1) / middle) * (middle - 1)) + middle
    )
    bucket = np.where(magnitude <= middle, offsets, (logged * np.sign(offsets)).astype(np.int32))
    return np.clip(bucket + buckets, 0, 2 * buckets - 1).astype(np.int32)


def dot(a,b,dims=NN): return lax.dot_general(a,b,dims,preferred_element_type=f4)
def al(x,m): return pl.multiple_of(x,m)
def iotas():
    r=lax.broadcasted_iota(jnp.int32,(TILE,TILE),0); c=lax.broadcasted_iota(jnp.int32,(TILE,TILE),1)
    return r,c


def fwd_kernel(
    b_ref, qa_ref, ka_ref, rk_ref, rq_ref, qb_ref, kb_ref, v_ref, segr_ref,
    att_ref, inv_ref, p_ref,
    xs0, xs1, ys0, ys1, sc0, sc1, mx0, mx1, top, sm, acc, segb,
):
    r, c = iotas()
    eye = (r == c).astype(f4).astype(bf)
    rev = (r + c == TILE - 1).astype(f4).astype(bf)
    early = (r + c) < TILE
    lane = lax.broadcasted_iota(jnp.int32, (CH, TILE), 1)
    left = lane < 64
    lane_t = lax.broadcasted_iota(jnp.int32, (TILE, TILE), 1)
    left_t = lane_t < 64
    step = pl.program_id(0)
    last = pl.num_programs(0) - 1
    fac = SCALE * math.log2(math.e)

    def head(x, h, mask):
        zero = jnp.zeros(x.shape, bf)
        return jnp.where(mask, x, zero) if h == 0 else jnp.where(mask, zero, x)

    def product(ic, slot, xs, ys):
        rows = pl.ds(al(ic * CH, CH), CH)
        w = pl.ds(al((jnp.clip(slot + 3 - ic, 1, NEAR) - 1) * CH, CH), CH)
        out = pl.ds(al(slot * CH, CH), CH)
        q = qa_ref[rows, :]
        k = ka_ref[rows, :]
        for h in range(2):
            xs[h, rows, out] = dot(head(q, h, left), rk_ref[w, :], NT).astype(bf)
            ys[h, rows, out] = dot(head(k, h, left), rq_ref[w, :], NT).astype(bf)

    def skewed(ref, h, row, spot):
        rr = pl.ds(al(row * TILE, TILE), TILE)
        a = ref[h, rr, pl.ds(al((spot + 2) * TILE, TILE), TILE)]
        b = ref[h, rr, pl.ds(al((spot + 1) * TILE, TILE), TILE)]
        return pltpu.roll(jnp.where(early, a, b), 0, 1, stride=1, stride_axis=0)

    def score(ic, jc, s, xs, ys, sc, mx):
        cols = pl.ds(al(jc * CH, CH), CH)
        segc = segr_ref[:, cols].astype(f4)
        keys = kb_ref[cols, :]
        i = 2 * ic + s
        rows = pl.ds(al(i * TILE, TILE), TILE)
        srow = segb[rows, :]
        q = qb_ref[rows, :]
        for h in range(2):
            turned = [skewed(ys, h, 2 * jc + t, i - t) for t in range(2)]
            lhs = jnp.concatenate([head(q, h, left_t), eye], axis=1)
            rhs = jnp.concatenate([keys, jnp.concatenate(turned, axis=0)], axis=1)
            content = dot(lhs, rhs, NT)
            best = mx[h, rows, :]
            for t in range(2):
                along = skewed(xs, h, i, 2 * jc + t - s).astype(f4)
                ok = srow == segc[:, t * TILE : (t + 1) * TILE]
                val = jnp.where(ok, content[:, t * TILE : (t + 1) * TILE] + along, MASKED)
                sc[h, rows, pl.ds(al(jc * CH + t * TILE, TILE), TILE)] = val
                best = jnp.maximum(best, val)
            mx[h, rows, :] = best

    def mix(ic, jc, h, sc):
        rows = pl.ds(al(ic * CH, CH), CH)
        tot = sm[h]
        peak = top[h]
        for t in range(2):
            cols = pl.ds(al(jc * CH + t * TILE, TILE), TILE)
            e = jnp.exp2((sc[h, rows, cols] - peak) * fac)
            tot = tot + e
            rhs = jnp.concatenate([head(v_ref[cols, :], h, left_t), rev], axis=1)
            res = dot(e.astype(bf), rhs)
            acc[...] += res[:, :TILE]
            p_ref[h, rows, cols] = res[:, TILE:].astype(bf)
        sm[h] = tot

    def open_scores(ic, mx):
        rows = pl.ds(al(ic * CH, CH), CH)
        for h in range(2):
            mx[h, rows, :] = jnp.full((CH, TILE), MASKED, f4)

    def open_mix(ic, mx):
        rows = pl.ds(al(ic * CH, CH), CH)
        for h in range(2):
            peak = jnp.max(mx[h, rows, :], axis=1, keepdims=True)
            top[h] = jnp.broadcast_to(peak, (CH, TILE))
            sm[h] = jnp.zeros((CH, TILE), f4)
        acc[...] = jnp.zeros((CH, TILE), f4)

    def close_mix(ic):
        rows = pl.ds(al(ic * CH, CH), CH)
        inv = [1.0 / jnp.sum(sm[h], axis=1, keepdims=True) for h in range(2)]
        pair = jnp.where(
            left, jnp.broadcast_to(inv[0], (CH, TILE)), jnp.broadcast_to(inv[1], (CH, TILE))
        )
        inv_ref[rows, :] = pair
        att_ref[rows, :] = acc[...] * pair

    def sweep(before, body, after):
        def chunk(ic, _):
            lo = b_ref[ic]
            hi = b_ref[NCH + ic]
            before(ic, lo)

            def block(jc, _):
                body(ic, jc)
                return 0

            lax.fori_loop(lo, hi, block, 0)
            after(ic)
            return 0

        lax.fori_loop(0, NCH, chunk, 0)

    def fused(xs_new, ys_new, xs, ys, sc_new, mx_new, sc, mx):
        def before(ic, lo):
            product(ic, lo, xs_new, ys_new)
            open_scores(ic, mx_new)
            open_mix(ic, mx)

        def body(ic, jc):
            product(ic, jc + 1, xs_new, ys_new)
            for part in range(2):
                mix(ic, jc, part, sc)
                score(ic, jc, part, xs, ys, sc_new, mx_new)

        sweep(before, body, close_mix)

    @pl.when(step == 0)
    def _():
        for t in range(LEN // TILE):
            cols = slice(t * TILE, (t + 1) * TILE)
            row = jnp.broadcast_to(segr_ref[:, cols].astype(f4), (TILE, TILE))
            segb[cols, :] = row.T
        sweep(
            lambda ic, lo: product(ic, lo, xs0, ys0),
            lambda ic, jc: product(ic, jc + 1, xs0, ys0),
            lambda ic: None,
        )

    @pl.when((step > 0) & (step < last) & (step % 2 == 1))
    def _():
        fused(xs1, ys1, xs0, ys0, sc1, mx1, sc0, mx0)

    @pl.when((step > 0) & (step < last) & (step % 2 == 0))
    def _():
        fused(xs0, ys0, xs1, ys1, sc0, mx0, sc1, mx1)

    @pl.when(step == last)
    def _():
        def body(ic, jc):
            mix(ic, jc, 0, sc0)
            mix(ic, jc, 1, sc0)

        sweep(lambda ic, lo: open_mix(ic, mx0), body, close_mix)


def attend_forward(bounds, both, v, spread, segr):
    pairs = v.shape[1] // TILE

    def col(n, lag, at=0, every=2):
        return pl.BlockSpec(
            (n, TILE), lambda s, *_: (0, at + every * jnp.clip(s - lag, 0, pairs - 1))
        )

    def wide(lag):
        return pl.BlockSpec((2, LEN, LEN), lambda s, *_: (jnp.clip(s - lag, 0, pairs - 1), 0, 0))

    window = pltpu.VMEM((2, LEN, LEN + CH), bf)
    return pl.pallas_call(
        fwd_kernel,
        grid_spec=pltpu.PrefetchScalarGridSpec(
            num_scalar_prefetch=1,
            grid=(pairs + 2,),
            in_specs=[
                col(LEN, 0),
                col(LEN, 0, 1),
                col(NEAR * CH, 0, 1),
                col(NEAR * CH, 0),
                col(LEN, 1),
                col(LEN, 1, 1),
                col(LEN, 2, 0, 1),
                pl.BlockSpec((1, LEN), lambda s, *_: (0, 0)),
            ],
            out_specs=[col(LEN, 2, 0, 1), col(LEN, 2, 0, 1), wide(2)],
            scratch_shapes=[window] * 4
            + [pltpu.VMEM((2, LEN, LEN), f4)] * 2
            + [pltpu.VMEM((2, LEN, TILE), f4)] * 2
            + [pltpu.VMEM((2, CH, TILE), f4)] * 2
            + [pltpu.VMEM((CH, TILE), f4)]
            + [pltpu.VMEM((LEN, TILE), f4)],
        ),
        out_shape=[
            jax.ShapeDtypeStruct(v.shape, f4),
            jax.ShapeDtypeStruct(v.shape, f4),
            jax.ShapeDtypeStruct((2 * pairs, LEN, LEN), bf),
        ],
        compiler_params=pltpu.CompilerParams(vmem_limit_bytes=60 << 20),
        name="attend_forward",
    )(bounds, both, both, spread, spread, both, both, v, segr)


def bwd_kernel(
    b_ref, q_ref, k_ref, v_ref, da_ref, att_ref, inv_ref, p_ref, rk_ref, rq_ref,
    dqk_ref, dv_ref, g_ref,
    ws0, ws1, wt0, wt1, dq0, dq1, dkt0, dkt1, dvt0, dvt1, qt0, qt1, kt0, kt1,
    gk0, gk1, gq0, gq1, dat, vr, kr, rkr, dq2, dk2, corr, norm,
):
    r, c = iotas()
    rev = (r + c == TILE - 1).astype(f4).astype(bf)
    late = c >= r
    early = c <= r
    left = lax.broadcasted_iota(jnp.int32, (CH, TILE), 1) < 64
    upper = lax.broadcasted_iota(jnp.int32, (TILE, CH), 0) < 64
    step = pl.program_id(0)
    last = pl.num_programs(0) - 1

    def head(x, h):
        zero = jnp.zeros(x.shape, x.dtype)
        return jnp.where(left, x, zero) if h == 0 else jnp.where(left, zero, x)

    def chunk_of(i):
        return pl.ds(al(i * CH, CH), CH)

    def tile_of(i):
        return pl.ds(al(i * TILE, TILE), TILE)

    def clear(*refs):
        for ref in refs:
            ref[...] = jnp.zeros(ref.shape, ref.dtype)

    def prepare(qt, kt):
        da = (da_ref[...].astype(f4) * inv_ref[...]).astype(bf)
        for t in range(LEN // TILE):
            rows = slice(t * TILE, (t + 1) * TILE)
            vr[rows, :] = dot(rev, v_ref[rows, :]).astype(bf)
            turned = dot(rev, k_ref[rows, :]).astype(bf)
            kr[rows, :] = turned
            kt[:, rows] = turned.T
            qt[:, rows] = q_ref[rows, :].T
            dat[:, rows] = da[rows].T

    def turn_table():
        for t in range(NEAR * CH // TILE):
            rows = slice(t * TILE, (t + 1) * TILE)
            rkr[rows, :] = dot(rev, rk_ref[rows, :]).astype(bf)

    def pads(ic, lo, hi, ws, wt):
        zero = jnp.zeros((CH, CH), bf)
        for h in range(2):
            for ref in (ws, wt):
                ref[h, chunk_of(ic), chunk_of(lo)] = zero
                ref[h, chunk_of(ic), chunk_of(hi + 1)] = zero

    def open_grad(ic, dq):
        rows = chunk_of(ic)
        x = att_ref[rows, :] * da_ref[rows, :].astype(f4)
        pair = inv_ref[rows, :]
        turned = pltpu.roll(pair, 64, 1)
        for h in range(2):
            total = jnp.sum(head(x, h), axis=1, keepdims=True)
            corr[h] = jnp.broadcast_to(total, (CH, TILE))
            norm[h] = jnp.where(left, pair, turned) if h == 0 else jnp.where(left, turned, pair)
        dq[rows, :] = jnp.zeros((CH, TILE), f4)

    def both_heads(first, second):
        return jnp.where(left, first, second)

    def grad_start(ic, jc):
        rows, cols = chunk_of(ic), chunk_of(jc)
        da = da_ref[rows, :]
        values = vr[cols, :]
        return [dot(head(da, h), values, NT) for h in range(2)]

    def grad_scores(ic, jc, dps):
        rows, cols = chunk_of(ic), chunk_of(jc)
        parts = []
        for h in range(2):
            p = p_ref[h, rows, cols]
            d, iv = corr[h], norm[h]
            parts.append(
                [
                    (
                        p[:, t * TILE : (t + 1) * TILE].astype(f4)
                        * ((dps[h][:, t * TILE : (t + 1) * TILE] - d) * iv)
                    ).astype(bf)
                    for t in range(2)
                ]
            )
        return parts

    def grad_skew(ic, jc, parts, ws, wt):
        for h in range(2):
            for t in range(2):
                for s in range(2):
                    sr = slice(s * TILE, (s + 1) * TILE)
                    ws[h, tile_of(2 * ic + s), tile_of(2 * jc + 2 + t)] = pltpu.roll(
                        parts[h][t][sr], 0, 1, stride=1, stride_axis=0
                    )
                    wt[h, tile_of(2 * jc + t), tile_of(2 * ic + 2 + s)] = pltpu.roll(
                        parts[h][t][sr].T, 1, 1, stride=1, stride_axis=0
                    )

    def grad_values(ic, jc, dvt):
        rows, cols = chunk_of(ic), chunk_of(jc)
        for h in range(2):
            half = slice(h * 64, (h + 1) * 64)
            dvt[half, cols] += dot(dat[half, rows], p_ref[h, rows, cols])

    def grad_out(ic, jc, parts, dq, dkt, qt):
        rows, cols = chunk_of(ic), chunk_of(jc)
        keys = kr[cols, :]
        whole = [jnp.concatenate(parts[h], axis=1) for h in range(2)]
        dq[rows, :] += both_heads(dot(whole[0], keys), dot(whole[1], keys))
        for h in range(2):
            half = slice(h * 64, (h + 1) * 64)
            dkt[half, cols] += dot(qt[half, rows], whole[h])

    def fold(ic, slot, first, ws, wt, qt, kt, gk, gq):
        rows = chunk_of(ic)
        w = chunk_of(jnp.clip(slot + 3 - ic, 1, NEAR) - 1)
        for ref, mask, table, out, turned, g in (
            (ws, late, rkr, dq2, qt, gk),
            (wt, early, rq_ref, dk2, kt, gq),
        ):
            rels = table[w, :]
            outs = []
            for h in range(2):
                band = []
                for s in range(2):
                    line = []
                    for b in range(2):
                        spot = 2 * slot + s + b
                        x = ref[h, tile_of(2 * ic + s), tile_of(spot)]
                        y = ref[h, tile_of(2 * ic + s), tile_of(spot + 1)]
                        line.append(jnp.where(mask, x, y))
                    band.append(jnp.concatenate(line, axis=1))
                band = jnp.concatenate(band, axis=0)
                outs.append(dot(band, rels))
                half = slice(h * 64, (h + 1) * 64)
                g[half, w] += dot(turned[half, rows], band)
            if first:
                out[rows, :] = both_heads(*outs)
            else:
                out[rows, :] += both_heads(*outs)

    def close(ic, dq, dkt, dvt):
        rows = chunk_of(ic)
        dqk_ref[rows, :TILE] = ((dq[rows, :] + dq2[rows, :]) * SCALE).astype(bf)
        for t in range(2):
            tr = tile_of(2 * ic + t)
            x = ((dkt[:, tr].T + dk2[tr, :]) * SCALE).astype(bf)
            dqk_ref[tr, TILE:] = dot(rev, x).astype(bf)
            dv_ref[tr, :] = dot(rev, dvt[:, tr].T.astype(bf)).astype(bf)
        dkt[:, rows] = jnp.zeros((TILE, CH), f4)
        dvt[:, rows] = jnp.zeros((TILE, CH), f4)

    def flush(gk, gq):
        g_ref[:TILE, :] = (gq[...] * SCALE).astype(bf)
        for t in range(NEAR * CH // TILE):
            cols = slice(t * TILE, (t + 1) * TILE)
            g_ref[TILE:, cols] = dot((gk[:, cols] * SCALE).astype(bf), rev).astype(bf)

    def sweep(before, body, idle):
        def chunk(ic, _):
            lo = b_ref[2 * NCH + ic]
            hi = b_ref[3 * NCH + ic]

            @pl.when(hi > lo)
            def _():
                before(ic, lo, hi)

            @pl.when(hi <= lo)
            def _():
                idle(ic)

            def block(jc, _):
                body(ic, jc)
                return 0

            lax.fori_loop(lo, hi, block, 0)
            return 0

        lax.fori_loop(0, NCH, chunk, 0)

    def no_fold(ic):
        dq2[chunk_of(ic), :] = jnp.zeros((CH, TILE), f4)
        dk2[chunk_of(ic), :] = jnp.zeros((CH, TILE), f4)

    def no_grad(ic, dq):
        dq[chunk_of(ic), :] = jnp.zeros((CH, TILE), f4)

    def fused(new, old):
        ws, wt, dq, dkt, dvt, qt, kt, gk_next, gq_next = new
        ws_, wt_, dq_, dkt_, dvt_, qt_, kt_, gk, gq = old
        prepare(qt, kt)
        turn_table()

        def before(ic, lo, hi):
            @pl.when(step < 2)
            def _():
                pads(ic, lo, hi, ws, wt)

            fold(ic, lo, True, ws_, wt_, qt_, kt_, gk, gq)
            open_grad(ic, dq)

        def body(ic, jc):
            dps = grad_start(ic, jc)
            fold(ic, jc + 1, False, ws_, wt_, qt_, kt_, gk, gq)
            grad_values(ic, jc, dvt)
            parts = grad_scores(ic, jc, dps)
            grad_skew(ic, jc, parts, ws, wt)
            grad_out(ic, jc, parts, dq, dkt, qt)

        def idle(ic):
            no_fold(ic)
            no_grad(ic, dq)

        sweep(before, body, idle)

        def finish(ic, _):
            close(ic, dq_, dkt_, dvt_)
            return 0

        lax.fori_loop(0, NCH, finish, 0)
        flush(gk, gq)
        clear(gk, gq)

    set0 = (ws0, wt0, dq0, dkt0, dvt0, qt0, kt0, gk0, gq0)
    set1 = (ws1, wt1, dq1, dkt1, dvt1, qt1, kt1, gk1, gq1)

    @pl.when(step == 0)
    def _():
        clear(dkt0, dkt1, dvt0, dvt1, gk0, gk1, gq0, gq1)
        prepare(qt0, kt0)

        def before(ic, lo, hi):
            pads(ic, lo, hi, ws0, wt0)
            open_grad(ic, dq0)

        def body(ic, jc):
            parts = grad_scores(ic, jc, grad_start(ic, jc))
            grad_values(ic, jc, dvt0)
            grad_skew(ic, jc, parts, ws0, wt0)
            grad_out(ic, jc, parts, dq0, dkt0, qt0)

        sweep(before, body, lambda ic: no_grad(ic, dq0))

    @pl.when((step > 0) & (step < last) & (step % 2 == 1))
    def _():
        fused(set1, set0)

    @pl.when((step > 0) & (step < last) & (step % 2 == 0))
    def _():
        fused(set0, set1)

    @pl.when(step == last)
    def _():
        turn_table()
        sweep(
            lambda ic, lo, hi: fold(ic, lo, True, ws1, wt1, qt1, kt1, gk1, gq1),
            lambda ic, jc: fold(ic, jc + 1, False, ws1, wt1, qt1, kt1, gk1, gq1),
            no_fold,
        )

        def finish(ic, _):
            close(ic, dq1, dkt1, dvt1)
            return 0

        lax.fori_loop(0, NCH, finish, 0)
        flush(gk1, gq1)


def attend_backward(bounds, both, v, da, att, inv, spread, p):
    pairs = v.shape[1] // TILE

    def col(n, lag, at=0, every=1):
        return pl.BlockSpec(
            (n, TILE), lambda s, *_: (0, at + every * jnp.clip(s - lag, 0, pairs - 1))
        )

    def out(at):
        return lambda s, *_: (jnp.clip(s - 1, 0, pairs - 1), 0)[:: 1 - 2 * at]

    def twice(shape, dtype):
        return [pltpu.VMEM(shape, dtype)] * 2

    return pl.pallas_call(
        bwd_kernel,
        grid_spec=pltpu.PrefetchScalarGridSpec(
            num_scalar_prefetch=1,
            grid=(pairs + 1,),
            in_specs=[
                col(LEN, 0, 0, 2),
                col(LEN, 0, 1, 2),
                col(LEN, 0),
                col(LEN, 0),
                col(LEN, 0),
                col(LEN, 0),
                pl.BlockSpec((2, LEN, LEN), lambda s, *_: (jnp.minimum(s, pairs - 1), 0, 0)),
                col(NEAR * CH, 1, 1, 2),
                col(NEAR * CH, 1, 0, 2),
            ],
            out_specs=[
                pl.BlockSpec((LEN, 2 * TILE), out(1)),
                col(LEN, 1),
                pl.BlockSpec((2 * TILE, NEAR * CH), out(0)),
            ],
            scratch_shapes=twice((2, LEN, LEN + 2 * CH), bf)
            + twice((2, LEN, LEN + 2 * CH), bf)
            + twice((LEN, TILE), f4)
            + twice((TILE, LEN), f4)
            + twice((TILE, LEN), f4)
            + twice((TILE, LEN), bf)
            + twice((TILE, LEN), bf)
            + twice((TILE, NEAR * CH), f4)
            + twice((TILE, NEAR * CH), f4)
            + [pltpu.VMEM((TILE, LEN), bf)]
            + [pltpu.VMEM((LEN, TILE), bf)] * 2
            + [pltpu.VMEM((NEAR * CH, TILE), bf)]
            + [pltpu.VMEM((LEN, TILE), f4)] * 2
            + [pltpu.VMEM((2, CH, TILE), f4)] * 2,
        ),
        out_shape=[
            jax.ShapeDtypeStruct(both.shape, bf),
            jax.ShapeDtypeStruct(v.shape, bf),
            jax.ShapeDtypeStruct((both.shape[1], NEAR * CH), bf),
        ],
        compiler_params=pltpu.CompilerParams(vmem_limit_bytes=60 << 20),
        name="attend_backward",
    )(bounds, both, both, v, da, att, inv, p, spread, spread)


def gelu_pair(u):
    size = jnp.abs(u)
    bell = jnp.exp2(u * u * (-0.5 * math.log2(math.e)))
    t = 1.0 / (1.0 + (0.3275911 / math.sqrt(2.0)) * size)
    poly = 0.5 * 1.061405429
    for c in (-1.453152027, 1.421413741, -0.284496736, 0.254829592):
        poly = poly * t + 0.5 * c
    tail = poly * t * bell
    phi = jnp.where(u < 0.0, tail, 1.0 - tail)
    return u * phi, phi + u * bell * (1.0 / math.sqrt(2.0 * math.pi))


def middle_kernel(
    hid_ref, att_ref, wo_ref, we_ref, wc_ref, vec_ref, mask_ref, cot_ref,
    out_ref, dfirst_ref, datt_ref, grad_ref,
    pre, slope, acc, norm_, act, dexp, low, dtwo, dbranch, attended, turned, sums,
):
    step = pl.program_id(0)
    blocks = act.shape[0] // TOK
    parts = act.shape[1] // low.shape[1]

    @pl.when(step < blocks)
    def _():
        rows = pl.ds(al(step * TOK, TOK), TOK)
        views = [ref.at[rows] for ref in (act, dexp, low, dtwo, dbranch, attended)]
        token_block(
            step, hid_ref, att_ref, wo_ref, we_ref, wc_ref, vec_ref, mask_ref, cot_ref,
            out_ref, dfirst_ref, datt_ref, pre, slope, acc, norm_, sums, *views,
        )

    @pl.when(step >= blocks)
    def _():
        weight_block(
            step - blocks, parts, act, dexp, low, dtwo, dbranch, attended, turned, sums, grad_ref
        )


def token_block(
    step, hid_ref, att_ref, wo_ref, we_ref, wc_ref, vec_ref, mask_ref, cot_ref,
    out_ref, dfirst_ref, datt_ref, pre, slope, acc, norm_, sums,
    act_ref, dexp_ref, low_ref, dtwo_ref, dbranch_ref, attb_ref,
):
    width = hid_ref.shape[1]
    chunks = we_ref.shape[1] // FCH
    vectors = vec_ref[...].astype(f4).T
    gain_one = vectors[0:1, :]
    shift_one = vectors[1:2, :]
    gain_two = vectors[2:3, :]
    shift_two = vectors[3:4, :]
    inv = 1.0 / width
    attb_ref[...] = att_ref[...].astype(bf)
    first = hid_ref[...].astype(f4) + dot(attb_ref[...], wo_ref[...])
    cen = first - jnp.sum(first, axis=1, keepdims=True) * inv
    rstd_one = lax.rsqrt(jnp.sum(cen * cen, axis=1, keepdims=True) * inv + NORM_EPS)
    n_one = cen * rstd_one
    norm_[...] = n_one
    normed = n_one * gain_one + shift_one
    low_ref[...] = normed.astype(bf)
    acc[...] = jnp.zeros(acc.shape, f4)

    def cols(c):
        return slice(c * FCH, (c + 1) * FCH)

    def expand(c):
        pre[c % 2] = dot(low_ref[...], we_ref[:, cols(c)])

    def bend(c):
        value, grad = gelu_pair(pre[c % 2])
        act_ref[:, cols(c)] = value.astype(bf)
        slope[:, cols(c)] = grad.astype(bf)

    def contract(c):
        acc[...] += dot(act_ref[:, cols(c)], wc_ref[:, cols(c)])

    expand(0)
    expand(1)
    bend(0)

    def steady(c, _):
        expand(c + 1)
        bend(c)
        contract(c - 1)
        return 0

    for c in range(1, chunks - 1):
        steady(c, 0)
    bend(chunks - 1)
    contract(chunks - 2)
    contract(chunks - 1)
    branch = acc[...]
    turned = [
        jnp.broadcast_to(mask_ref[:, t : t + TILE].astype(f4), (TILE, TILE)).T
        for t in range(0, TOK, TILE)
    ]
    mask = jnp.concatenate(turned, axis=0)[:, 0:1]
    normed = norm_[...] * gain_one + shift_one
    second = normed + branch
    row_res = jnp.sum(mask * second * second, axis=0, keepdims=True)
    row_sub = jnp.sum(mask * branch * branch, axis=0, keepdims=True)
    cen = second - jnp.sum(second, axis=1, keepdims=True) * inv
    rstd = lax.rsqrt(jnp.sum(cen * cen, axis=1, keepdims=True) * inv + NORM_EPS)
    n_two = cen * rstd
    out_ref[...] = (n_two * gain_two + shift_two).astype(bf)
    up = cot_ref[...].astype(f4) * mask
    row_g2 = jnp.sum(up * n_two, axis=0, keepdims=True)
    row_s2 = jnp.sum(up, axis=0, keepdims=True)
    g = up * gain_two
    d_second = (
        g
        - jnp.sum(g, axis=1, keepdims=True) * inv
        - n_two * (jnp.sum(g * n_two, axis=1, keepdims=True) * inv)
    ) * rstd
    dtwo_ref[...] = d_second.astype(bf)
    acc[...] = d_second

    def back(c):
        grad = dot(dtwo_ref[...], wc_ref[:, cols(c)], NT) * slope[:, cols(c)].astype(f4)
        dexp_ref[:, cols(c)] = grad.astype(bf)

    def into(c):
        acc[...] += dot(dexp_ref[:, cols(c)], we_ref[:, cols(c)], NT)

    back(0)

    def steady_back(c, _):
        back(c)
        into(c - 1)
        return 0

    for c in range(1, chunks):
        steady_back(c, 0)
    into(chunks - 1)
    up = acc[...]
    n_one = norm_[...]
    row_g1 = jnp.sum(up * n_one, axis=0, keepdims=True)
    row_s1 = jnp.sum(up, axis=0, keepdims=True)
    g = up * gain_one
    d_first = (
        g
        - jnp.sum(g, axis=1, keepdims=True) * inv
        - n_one * (jnp.sum(g * n_one, axis=1, keepdims=True) * inv)
    ) * rstd_one
    dfirst_ref[...] = d_first
    low = d_first.astype(bf)
    dbranch_ref[...] = low
    datt_ref[...] = dot(low, wo_ref[...], NT).astype(bf)
    rows = jnp.concatenate(
        [row_g1, row_s1, row_g2, row_s2, row_res, row_sub, jnp.zeros((2, width), f4)], axis=0
    )

    @pl.when(step == 0)
    def _():
        sums[...] = rows

    @pl.when(step > 0)
    def _():
        sums[...] += rows


def weight_block(
    step, parts, act, dexp, low, dtwo, dbranch, attended, turned, sums, out_ref
):
    width = low.shape[1]

    @pl.when(step == 0)
    def _():
        turned[...] = low[...].T

    @pl.when(step < parts)
    def _():
        cols = pl.ds(al(step * width, width), width)
        out_ref[...] = dot(turned[...], dexp[:, cols]).astype(bf)

    @pl.when((step >= parts) & (step < 2 * parts))
    def _():
        cols = pl.ds(al((step - parts) * width, width), width)
        out_ref[...] = dot(act[:, cols].T, dtwo[...]).astype(bf)

    @pl.when(step == 2 * parts)
    def _():
        out_ref[...] = dot(attended[...].T, dbranch[...]).astype(bf)

    @pl.when(step == 2 * parts + 1)
    def _():
        rows = sums[...]
        total = jnp.broadcast_to(jnp.sum(rows[4:6], axis=1, keepdims=True), (2, width))
        full = jnp.concatenate([rows[:4], total, jnp.zeros((TILE - 6, width), f4)], axis=0)
        out_ref[:, :TILE] = full.T.astype(bf)


def middle(hidden, attended, weights, wide, mask, cotangent):
    tokens, width = hidden.shape
    blocks = tokens // TOK
    parts = wide // width
    tok = lambda n: pl.BlockSpec((TOK, n), lambda i: (jnp.minimum(i, blocks - 1), 0))
    once = lambda n, at: pl.BlockSpec(
        (width, n), lambda i: (0, at // n), pipeline_mode=pl.Buffered(1)
    )
    shape = lambda n, dtype: jax.ShapeDtypeStruct((tokens, n), dtype)
    whole = lambda n: pltpu.VMEM((tokens, n), bf)
    return pl.pallas_call(
        middle_kernel,
        grid=(blocks + 2 * parts + 2,),
        in_specs=[
            tok(width),
            tok(width),
            once(width, 2 * wide),
            once(wide, 0),
            once(wide, wide),
            once(TILE, 2 * wide + width),
            pl.BlockSpec((1, TOK), lambda i: (0, jnp.minimum(i, blocks - 1))),
            tok(width),
        ],
        out_specs=[
            tok(width),
            tok(width),
            tok(width),
            pl.BlockSpec((width, width), lambda i: (0, jnp.maximum(i - blocks, 0))),
        ],
        out_shape=[
            shape(width, bf),
            shape(width, f4),
            shape(width, bf),
            jax.ShapeDtypeStruct((width, 2 * wide + width + TILE), bf),
        ],
        scratch_shapes=[
            pltpu.VMEM((2, TOK, FCH), f4),
            pltpu.VMEM((TOK, wide), bf),
            pltpu.VMEM((TOK, width), f4),
            pltpu.VMEM((TOK, width), f4),
            whole(wide),
            whole(wide),
            whole(width),
            whole(width),
            whole(width),
            whole(width),
            pltpu.VMEM((width, tokens), bf),
            pltpu.VMEM((8, width), f4),
        ],
        compiler_params=pltpu.CompilerParams(vmem_limit_bytes=60 << 20),
        name="middle",
    )(hidden, attended, weights, weights, weights, weights, mask, cotangent)


def lane_pieces(size, count, parts, per, forward):
    found = [[] for _ in range(size // TILE)]
    for device in range(count):
        for part in range(parts):
            source = (device * parts + part) * per
            target = part * count * per + device * per
            if not forward:
                source, target = target, source
            done = 0
            while done < per:
                at, to = source + done, target + done
                span = min(per - done, TILE - at % TILE, TILE - to % TILE)
                found[to // TILE].append((at // TILE, at % TILE, to % TILE, span))
                done += span
    return found


def permute_lanes(load, store, rows, pieces):
    lane = lax.broadcasted_iota(jnp.int32, (rows, TILE), 1)
    for block, group in enumerate(pieces):
        total = jnp.zeros((rows, TILE), f4)
        for at, offset, spot, span in group:
            moved = load(at)
            if spot != offset:
                moved = pltpu.roll(moved, (spot - offset) % TILE, 1)
            total = jnp.where((lane >= spot) & (lane < spot + span), moved, total)
        store(block, total)


def lanes(block):
    return slice(block * TILE, (block + 1) * TILE)


def pack_kernel(count, expand_ref, contract_ref, output_ref, small_ref, out_ref):
    per, wide = expand_ref.shape
    width = output_ref.shape[1]
    parts = wide // width

    def store(block, value):
        out_ref[:, lanes(block)] = value.astype(bf)

    permute_lanes(
        lambda at: expand_ref[:, lanes(at)].astype(f4),
        store,
        per,
        lane_pieces(wide, count, parts, per, True),
    )
    rows = contract_ref[...].astype(f4)
    for part in range(parts):
        at = wide + part * width
        out_ref[:, at : at + width] = rows[part * per : (part + 1) * per].astype(bf)
    out_ref[:, 2 * wide : 2 * wide + width] = output_ref[...]
    out_ref[:, 2 * wide + width :] = small_ref[...]


def pack_weights(count, expand, contract, output, small):
    per, wide = expand.shape
    return pl.pallas_call(
        partial(pack_kernel, count),
        out_shape=jax.ShapeDtypeStruct((per, 2 * wide + output.shape[1] + TILE), bf),
        name="pack_weights",
    )(expand, contract, output, small)


def finish_kernel(count, own_ref, expand_ref, contract_ref, output_ref, small_ref):
    per, wide = expand_ref.shape
    width = output_ref.shape[1]
    parts = wide // width

    def store(block, value):
        expand_ref[:, lanes(block)] = value

    permute_lanes(
        lambda at: own_ref[:, lanes(at)].astype(f4),
        store,
        per,
        lane_pieces(wide, count, parts, per, False),
    )
    for part in range(parts):
        at = wide + part * width
        contract_ref[part * per : (part + 1) * per, :] = own_ref[:, at : at + width].astype(f4)
    output_ref[...] = own_ref[:, 2 * wide : 2 * wide + width].astype(f4)
    small_ref[...] = own_ref[:, 2 * wide + width :].astype(f4)


def finish_grads(count, own, wide, width):
    per = own.shape[0]
    shape = lambda a, b: jax.ShapeDtypeStruct((a, b), f4)
    return pl.pallas_call(
        partial(finish_kernel, count),
        out_shape=[
            shape(per, wide),
            shape(per * (wide // width), width),
            shape(per, width),
            shape(per, TILE),
        ],
        name="finish_grads",
    )(own)


def digits(count):
    found = [(1, 2)]
    stride = 2
    while stride < count:
        radix = 4 if count // stride >= 4 else 2
        found.append((stride, radix))
        stride *= radix
    return found


def place(relative, count):
    spot = relative * 0
    for stride, radix in digits(count):
        spot = spot * radix + ((relative >> (stride.bit_length() - 1)) & (radix - 1))
    return spot


def mixing(size, count, me):
    per = size // count
    row = np.arange(size)
    target = place(jnp.asarray(row // per, jnp.int32) ^ me, count) * per + (row % per)
    spots = lax.broadcasted_iota(jnp.int32, (size, size), 1)
    return (target[:, None] == spots).astype(bf)


def near_index():
    index = bucket_index(LEN - np.arange(2 * LEN), BUCKETS).reshape(-1, CH)
    assert (index[:2] == index[0, 0]).all() and (index[-2:] == index[-1, -1]).all()
    return index[1:-1].reshape(-1)


def offset_rows(count, me):
    index = near_index()
    size = 2 * BUCKETS
    per = size // count
    target = place(jnp.asarray(index // per, jnp.int32) ^ me, count) * per + (index % per)
    spots = lax.broadcasted_iota(jnp.int32, (index.shape[0], size), 1)
    return (target[:, None] == spots).astype(bf)


def swap(value, offset, count):
    return lax.ppermute(value, "fsdp", [(i, i ^ offset) for i in range(count)])


def together(values):
    return list(lax.optimization_barrier(tuple(values)))


def gather_pair(first, second, count, beside):
    middle = digits(count)[1:]
    one, two = first[None], second[None]
    for (stride_a, radix_a), (stride_b, radix_b) in zip(middle[::-1], middle):
        got_a = [one]
        got_b = [two]
        for step in range(1, max(radix_a, radix_b)):
            if step < radix_a:
                got_a.append(swap(one, step * stride_a, count))
            if step < radix_b:
                got_b.append(swap(two, step * stride_b, count))
        one, two, *beside = together(
            [jnp.concatenate(got_a, axis=0), jnp.concatenate(got_b, axis=0), *beside]
        )
    radices = [radix for _, radix in middle[::-1]]
    two = two.reshape(*radices, *second.shape)
    turn = tuple(range(len(middle)))[::-1]
    two = two.transpose(turn + (len(middle), len(middle) + 1)).reshape(-1, *second.shape)
    return (one, swap(one, 1, count)), (two, swap(two, 1, count)), beside


def scatter_pair(first, second, count, beside):
    middle = digits(count)[1:]
    radices = [radix for _, radix in middle]
    shape_a, shape_b = first.shape[1:], second.shape[1:]
    half_a = first.reshape(2, -1, *shape_a)
    half_b = second.reshape(2, -1, *shape_b)
    one, two = together(
        [
            half_a[0].astype(f4) + swap(half_a[1], 1, count).astype(f4),
            half_b[0].astype(f4) + swap(half_b[1], 1, count).astype(f4),
        ]
    )
    one = one.astype(bf).reshape(*radices, *shape_a)
    two = two.astype(bf).reshape(*radices, *shape_b)
    for step, ((stride_a, radix_a), (stride_b, radix_b)) in enumerate(zip(middle, middle[::-1])):
        last = two.ndim - 3
        got_a = []
        got_b = []
        for hop in range(1, max(radix_a, radix_b)):
            if hop < radix_a:
                got_a.append(swap(one[hop], hop * stride_a, count))
            if hop < radix_b:
                got_b.append(
                    swap(lax.index_in_dim(two, hop, last, keepdims=False), hop * stride_b, count)
                )
        sum_a = one[0].astype(f4)
        sum_b = lax.index_in_dim(two, 0, last, keepdims=False).astype(f4)
        if step == 0:
            *got, beside = together(got_a + got_b + [beside])
        else:
            got = together(got_a + got_b)
        for piece in got[: len(got_a)]:
            sum_a = sum_a + piece.astype(f4)
        for piece in got[len(got_a) :]:
            sum_b = sum_b + piece.astype(f4)
        if step == len(middle) - 1:
            return sum_a, sum_b, beside
        one, two = sum_a.astype(bf), sum_b.astype(bf)


def active_chunks(segment, valid):
    rows = segment.reshape(NCH, CH)
    ok = valid.reshape(NCH, CH) > 0
    first = rows[:, 0]
    last = rows[:, -1]
    over = (first[None, :] <= last[:, None]) & (last[None, :] >= first[:, None])
    real = jnp.max(jnp.where(ok, rows, -1), axis=1)
    back = (first[None, :] <= real[:, None]) & (last[None, :] >= first[:, None])
    back = back | back.T
    place_ = jnp.arange(NCH)[None, :]

    def limits(mask):
        lo = jnp.min(jnp.where(mask, place_, NCH), axis=1)
        hi = jnp.max(jnp.where(mask, place_ + 1, 0), axis=1)
        return jnp.where(hi > 0, lo, 0), hi

    return jnp.concatenate(limits(over) + limits(back)).astype(jnp.int32)


def weave(first, second):
    cut = lambda x: x.reshape(x.shape[0], -1, 1, TILE)
    return jnp.concatenate([cut(first), cut(second)], axis=2).reshape(first.shape[0], -1)


def mm(left, right, dims=NN):
    return lax.dot_general(left, right, dims, preferred_element_type=f4)


def shards(
    hidden,
    query_weight,
    key_weight,
    value_weight,
    output_weight,
    relative_table,
    first_gain,
    first_shift,
    expand_weight,
    contract_weight,
    second_gain,
    second_shift,
    segment_ids,
    valid,
    cotangent,
):
    count = lax.axis_size("fsdp")
    me = lax.axis_index("fsdp")
    width = hidden.shape[1]
    wide = expand_weight.shape[1]
    per = query_weight.shape[0]
    per_t = relative_table.shape[0]
    per_c = contract_weight.shape[0]
    parts = wide // width

    first, second, *held = together(
        [
            weave(query_weight, key_weight),
            jnp.concatenate([value_weight, relative_table], axis=0),
            expand_weight,
            contract_weight,
            output_weight,
            first_gain,
            first_shift,
            second_gain,
            second_shift,
        ]
    )
    expand_weight, contract_weight, output_weight = held[:3]
    small = jnp.pad(jnp.stack(held[3:], axis=1), ((0, 0), (0, TILE - 4)))
    rest = pack_weights(count, expand_weight, contract_weight, output_weight, small)
    mix = mixing(width, count, me)
    pair_a, pair_b, (rest, mix, hidden_mixed, onehot, bounds) = gather_pair(
        first,
        second,
        count,
        [
            rest,
            mix,
            mm(hidden, mix).astype(bf),
            offset_rows(count, me),
            active_chunks(segment_ids, valid),
        ],
    )
    query_key = jnp.concatenate(pair_a, axis=0).reshape(count * per, 2 * width)
    value_full = jnp.concatenate([x[:, :per] for x in pair_b], axis=0)
    value_full = value_full.reshape(count * per, width)
    table = jnp.concatenate([x[:, per:] for x in pair_b], axis=0).reshape(count * per_t, width)

    weights = lax.all_gather(rest, "fsdp", axis=0, tiled=True)

    table_mixed = mm(table, mix).astype(bf)
    both_rows = mm(hidden_mixed, query_key).astype(bf)
    value_rows = mm(hidden_mixed, value_full).astype(bf)
    (position,) = together([mm(table_mixed, query_key).astype(bf)])
    spread_rows = mm(onehot, position).astype(bf)
    attended_wide, inverse, probs = attend_forward(
        bounds, both_rows, value_rows, spread_rows, segment_ids[None, :]
    )
    result, d_first, attended_gradient, grads = middle(
        hidden, attended_wide, weights, wide, valid[None, :], cotangent
    )
    owned = lax.psum_scatter(grads, "fsdp", scatter_dimension=0, tiled=True)
    both_low, value_low, offset_grad = attend_backward(
        bounds,
        both_rows,
        value_rows,
        attended_gradient,
        attended_wide,
        inverse,
        spread_rows,
        probs,
    )
    position_low = mm(offset_grad, onehot).astype(bf)
    grad_pack = mm(hidden_mixed, both_low, ROWS_FIRST) + mm(
        table_mixed, position_low, (((0,), (1,)), ((), ()))
    )
    grad_pack = grad_pack.astype(bf).reshape(count, per, 2 * width)
    grad_value = mm(hidden_mixed, value_low, ROWS_FIRST)
    grad_table = mm(position_low, query_key, (((0,), (1,)), ((), ())))
    grad_table = mm(grad_table.astype(bf), mix, NT).astype(bf)
    grad_value = jnp.concatenate(
        [
            grad_value.astype(bf).reshape(count, per, width),
            grad_table.reshape(count, per_t, width),
        ],
        axis=1,
    )
    d_input = mm(both_low, query_key, NT) + mm(value_low, value_full, NT)
    own_pack, own_value, d_input = scatter_pair(grad_pack, grad_value, count, d_input.astype(bf))
    d_input = d_first + mm(d_input, mix, NT)
    cells = f4(hidden.shape[0] * count * width)
    expand_owned, contract_owned, output_owned, last = finish_grads(count, owned, wide, width)
    own_pack = own_pack.reshape(per, -1, 2, TILE)
    return (
        result,
        d_input.astype(bf),
        own_pack[:, :, 0].reshape(per, width),
        own_pack[:, :, 1].reshape(per, width),
        own_value[:per],
        output_owned,
        own_value[per:],
        last[:, 0],
        last[:, 1],
        expand_owned,
        contract_owned,
        last[:, 2],
        last[:, 3],
        jnp.sqrt(last[0, 4] / cells),
        jnp.sqrt(last[0, 5] / cells),
    )


def solution(mesh):
    in_specs = (
        P("fsdp", None),
        P("fsdp", None),
        P("fsdp", None),
        P("fsdp", None),
        P("fsdp", None),
        P("fsdp", None),
        P("fsdp"),
        P("fsdp"),
        P("fsdp", None),
        P("fsdp", None),
        P("fsdp"),
        P("fsdp"),
        P("fsdp"),
        P("fsdp"),
        P("fsdp", None),
    )
    out_specs = (
        P("fsdp", None),
        P("fsdp", None),
        P("fsdp", None),
        P("fsdp", None),
        P("fsdp", None),
        P("fsdp", None),
        P("fsdp", None),
        P("fsdp"),
        P("fsdp"),
        P("fsdp", None),
        P("fsdp", None),
        P("fsdp"),
        P("fsdp"),
        P(),
        P(),
    )
    return jax.shard_map(shards, mesh=mesh, in_specs=in_specs, out_specs=out_specs, check_vma=False)
```

```python
from functools import partial
import math

import jax
import jax.numpy as jnp
import numpy as np
from jax import lax
from jax.experimental import pallas as pl
from jax.experimental.pallas import tpu as pltpu
from jax.sharding import PartitionSpec as P

bf = jnp.bfloat16
f4 = jnp.float32
HEADS = 12
BUCKETS = 256
LEN = 1024
TILE = 128
CH = 256
NCH = LEN // CH
SCALE = 1.0 / math.sqrt(192.0)
NORM_EPS = 1e-07
MASKED = -1e30
TOK = 256
NEAR = 6
FCH = 768
ROWS_FIRST = (((0,), (0,)), ((), ()))
ROWS_LAST = (((1,), (1,)), ((), ()))
NT = ROWS_LAST
NN = (((1,), (0,)), ((), ()))


def bucket_index(offsets, buckets):
    middle = buckets // 2
    limit = 2 * buckets
    magnitude = np.abs(offsets)
    inside = (offsets < middle) & (offsets > -middle)
    clipped = np.where(inside, middle - 1, magnitude)
    logged = (
        np.ceil(np.log(clipped / middle) / np.log((limit - 1) / middle) * (middle - 1)) + middle
    )
    bucket = np.where(magnitude <= middle, offsets, (logged * np.sign(offsets)).astype(np.int32))
    return np.clip(bucket + buckets, 0, 2 * buckets - 1).astype(np.int32)


def dot(a,b,dims=NN): return lax.dot_general(a,b,dims,preferred_element_type=f4)
def al(x,m): return pl.multiple_of(x,m)
def iotas():
    r=lax.broadcasted_iota(jnp.int32,(TILE,TILE),0); c=lax.broadcasted_iota(jnp.int32,(TILE,TILE),1)
    return r,c


def fwd_kernel(
    b_ref, qa_ref, ka_ref, rk_ref, rq_ref, qb_ref, kb_ref, v_ref, segr_ref,
    att_ref, inv_ref, p_ref,
    xs0, xs1, ys0, ys1, sc0, sc1, mx0, mx1, top, sm, acc, segb,
):
    r, c = iotas()
    eye = (r == c).astype(f4).astype(bf)
    rev = (r + c == TILE - 1).astype(f4).astype(bf)
    early = (r + c) < TILE
    lane = lax.broadcasted_iota(jnp.int32, (CH, TILE), 1)
    left = lane < 64
    lane_t = lax.broadcasted_iota(jnp.int32, (TILE, TILE), 1)
    left_t = lane_t < 64
    step = pl.program_id(0)
    last = pl.num_programs(0) - 1
    fac = SCALE * math.log2(math.e)

    def head(x, h, mask):
        zero = jnp.zeros(x.shape, bf)
        return jnp.where(mask, x, zero) if h == 0 else jnp.where(mask, zero, x)

    def product(ic, slot, xs, ys):
        rows = pl.ds(al(ic * CH, CH), CH)
        w = pl.ds(al((jnp.clip(slot + 3 - ic, 1, NEAR) - 1) * CH, CH), CH)
        out = pl.ds(al(slot * CH, CH), CH)
        q = qa_ref[rows, :]
        k = ka_ref[rows, :]
        for h in range(2):
            xs[h, rows, out] = dot(head(q, h, left), rk_ref[w, :], NT).astype(bf)
            ys[h, rows, out] = dot(head(k, h, left), rq_ref[w, :], NT).astype(bf)

    def skewed(ref, h, row, spot):
        rr = pl.ds(al(row * TILE, TILE), TILE)
        a = ref[h, rr, pl.ds(al((spot + 2) * TILE, TILE), TILE)]
        b = ref[h, rr, pl.ds(al((spot + 1) * TILE, TILE), TILE)]
        return pltpu.roll(jnp.where(early, a, b), 0, 1, stride=1, stride_axis=0)

    def score(ic, jc, s, xs, ys, sc, mx):
        cols = pl.ds(al(jc * CH, CH), CH)
        segc = segr_ref[:, cols].astype(f4)
        keys = kb_ref[cols, :]
        i = 2 * ic + s
        rows = pl.ds(al(i * TILE, TILE), TILE)
        srow = segb[rows, :]
        q = qb_ref[rows, :]
        for h in range(2):
            turned = [skewed(ys, h, 2 * jc + t, i - t) for t in range(2)]
            lhs = jnp.concatenate([head(q, h, left_t), eye], axis=1)
            rhs = jnp.concatenate([keys, jnp.concatenate(turned, axis=0)], axis=1)
            content = dot(lhs, rhs, NT)
            best = mx[h, rows, :]
            for t in range(2):
                along = skewed(xs, h, i, 2 * jc + t - s).astype(f4)
                ok = srow == segc[:, t * TILE : (t + 1) * TILE]
                val = jnp.where(ok, content[:, t * TILE : (t + 1) * TILE] + along, MASKED)
                sc[h, rows, pl.ds(al(jc * CH + t * TILE, TILE), TILE)] = val
                best = jnp.maximum(best, val)
            mx[h, rows, :] = best

    def mix(ic, jc, h, sc):
        rows = pl.ds(al(ic * CH, CH), CH)
        tot = sm[h]
        peak = top[h]
        for t in range(2):
            cols = pl.ds(al(jc * CH + t * TILE, TILE), TILE)
            e = jnp.exp2((sc[h, rows, cols] - peak) * fac)
            tot = tot + e
            rhs = jnp.concatenate([head(v_ref[cols, :], h, left_t), rev], axis=1)
            res = dot(e.astype(bf), rhs)
            acc[...] += res[:, :TILE]
            p_ref[h, rows, cols] = res[:, TILE:].astype(bf)
        sm[h] = tot

    def open_scores(ic, mx):
        rows = pl.ds(al(ic * CH, CH), CH)
        for h in range(2):
            mx[h, rows, :] = jnp.full((CH, TILE), MASKED, f4)

    def open_mix(ic, mx):
        rows = pl.ds(al(ic * CH, CH), CH)
        for h in range(2):
            peak = jnp.max(mx[h, rows, :], axis=1, keepdims=True)
            top[h] = jnp.broadcast_to(peak, (CH, TILE))
            sm[h] = jnp.zeros((CH, TILE), f4)
        acc[...] = jnp.zeros((CH, TILE), f4)

    def close_mix(ic):
        rows = pl.ds(al(ic * CH, CH), CH)
        inv = [1.0 / jnp.sum(sm[h], axis=1, keepdims=True) for h in range(2)]
        pair = jnp.where(
            left, jnp.broadcast_to(inv[0], (CH, TILE)), jnp.broadcast_to(inv[1], (CH, TILE))
        )
        inv_ref[rows, :] = pair
        att_ref[rows, :] = acc[...] * pair

    def sweep(before, body, after):
        def chunk(ic, _):
            lo = b_ref[ic]
            hi = b_ref[NCH + ic]
            before(ic, lo)

            def block(jc, _):
                body(ic, jc)
                return 0

            lax.fori_loop(lo, hi, block, 0)
            after(ic)
            return 0

        lax.fori_loop(0, NCH, chunk, 0)

    def fused(xs_new, ys_new, xs, ys, sc_new, mx_new, sc, mx):
        def before(ic, lo):
            product(ic, lo, xs_new, ys_new)
            open_scores(ic, mx_new)
            open_mix(ic, mx)

        def body(ic, jc):
            product(ic, jc + 1, xs_new, ys_new)
            for part in range(2):
                mix(ic, jc, part, sc)
                score(ic, jc, part, xs, ys, sc_new, mx_new)

        sweep(before, body, close_mix)

    @pl.when(step == 0)
    def _():
        for t in range(LEN // TILE):
            cols = slice(t * TILE, (t + 1) * TILE)
            row = jnp.broadcast_to(segr_ref[:, cols].astype(f4), (TILE, TILE))
            segb[cols, :] = row.T
        sweep(
            lambda ic, lo: product(ic, lo, xs0, ys0),
            lambda ic, jc: product(ic, jc + 1, xs0, ys0),
            lambda ic: None,
        )

    @pl.when((step > 0) & (step < last) & (step % 2 == 1))
    def _():
        fused(xs1, ys1, xs0, ys0, sc1, mx1, sc0, mx0)

    @pl.when((step > 0) & (step < last) & (step % 2 == 0))
    def _():
        fused(xs0, ys0, xs1, ys1, sc0, mx0, sc1, mx1)

    @pl.when(step == last)
    def _():
        def body(ic, jc):
            mix(ic, jc, 0, sc0)
            mix(ic, jc, 1, sc0)

        sweep(lambda ic, lo: open_mix(ic, mx0), body, close_mix)


def attend_forward(bounds, both, v, spread, segr):
    pairs = v.shape[1] // TILE

    def col(n, lag, at=0, every=2):
        return pl.BlockSpec(
            (n, TILE), lambda s, *_: (0, at + every * jnp.clip(s - lag, 0, pairs - 1))
        )

    def wide(lag):
        return pl.BlockSpec((2, LEN, LEN), lambda s, *_: (jnp.clip(s - lag, 0, pairs - 1), 0, 0))

    window = pltpu.VMEM((2, LEN, LEN + CH), bf)
    return pl.pallas_call(
        fwd_kernel,
        grid_spec=pltpu.PrefetchScalarGridSpec(
            num_scalar_prefetch=1,
            grid=(pairs + 2,),
            in_specs=[
                col(LEN, 0),
                col(LEN, 0, 1),
                col(NEAR * CH, 0, 1),
                col(NEAR * CH, 0),
                col(LEN, 1),
                col(LEN, 1, 1),
                col(LEN, 2, 0, 1),
                pl.BlockSpec((1, LEN), lambda s, *_: (0, 0)),
            ],
            out_specs=[col(LEN, 2, 0, 1), col(LEN, 2, 0, 1), wide(2)],
            scratch_shapes=[window] * 4
            + [pltpu.VMEM((2, LEN, LEN), f4)] * 2
            + [pltpu.VMEM((2, LEN, TILE), f4)] * 2
            + [pltpu.VMEM((2, CH, TILE), f4)] * 2
            + [pltpu.VMEM((CH, TILE), f4)]
            + [pltpu.VMEM((LEN, TILE), f4)],
        ),
        out_shape=[
            jax.ShapeDtypeStruct(v.shape, f4),
            jax.ShapeDtypeStruct(v.shape, f4),
            jax.ShapeDtypeStruct((2 * pairs, LEN, LEN), bf),
        ],
        compiler_params=pltpu.CompilerParams(vmem_limit_bytes=60 << 20),
        name="attend_forward",
    )(bounds, both, both, spread, spread, both, both, v, segr)


def bwd_kernel(
    b_ref, q_ref, k_ref, v_ref, da_ref, att_ref, inv_ref, p_ref, rk_ref, rq_ref,
    dqk_ref, dv_ref, g_ref,
    ws0, ws1, wt0, wt1, dq0, dq1, dkt0, dkt1, dvt0, dvt1, qt0, qt1, kt0, kt1,
    gk0, gk1, gq0, gq1, dat, vr, kr, rkr, dq2, dk2, corr, norm,
):
    r, c = iotas()
    rev = (r + c == TILE - 1).astype(f4).astype(bf)
    late = c >= r
    early = c <= r
    left = lax.broadcasted_iota(jnp.int32, (CH, TILE), 1) < 64
    upper = lax.broadcasted_iota(jnp.int32, (TILE, CH), 0) < 64
    step = pl.program_id(0)
    last = pl.num_programs(0) - 1

    def head(x, h):
        zero = jnp.zeros(x.shape, x.dtype)
        return jnp.where(left, x, zero) if h == 0 else jnp.where(left, zero, x)

    def chunk_of(i):
        return pl.ds(al(i * CH, CH), CH)

    def tile_of(i):
        return pl.ds(al(i * TILE, TILE), TILE)

    def clear(*refs):
        for ref in refs:
            ref[...] = jnp.zeros(ref.shape, ref.dtype)

    def prepare(qt, kt):
        da = (da_ref[...].astype(f4) * inv_ref[...]).astype(bf)
        for t in range(LEN // TILE):
            rows = slice(t * TILE, (t + 1) * TILE)
            vr[rows, :] = dot(rev, v_ref[rows, :]).astype(bf)
            turned = dot(rev, k_ref[rows, :]).astype(bf)
            kr[rows, :] = turned
            kt[:, rows] = turned.T
            qt[:, rows] = q_ref[rows, :].T
            dat[:, rows] = da[rows].T

    def turn_table():
        for t in range(NEAR * CH // TILE):
            rows = slice(t * TILE, (t + 1) * TILE)
            rkr[rows, :] = dot(rev, rk_ref[rows, :]).astype(bf)

    def pads(ic, lo, hi, ws, wt):
        zero = jnp.zeros((CH, CH), bf)
        for h in range(2):
            for ref in (ws, wt):
                ref[h, chunk_of(ic), chunk_of(lo)] = zero
                ref[h, chunk_of(ic), chunk_of(hi + 1)] = zero

    def open_grad(ic, dq):
        rows = chunk_of(ic)
        x = att_ref[rows, :] * da_ref[rows, :].astype(f4)
        pair = inv_ref[rows, :]
        turned = pltpu.roll(pair, 64, 1)
        for h in range(2):
            total = jnp.sum(head(x, h), axis=1, keepdims=True)
            corr[h] = jnp.broadcast_to(total, (CH, TILE))
            norm[h] = jnp.where(left, pair, turned) if h == 0 else jnp.where(left, turned, pair)
        dq[rows, :] = jnp.zeros((CH, TILE), f4)

    def both_heads(first, second):
        return jnp.where(left, first, second)

    def grad_start(ic, jc):
        rows, cols = chunk_of(ic), chunk_of(jc)
        da = da_ref[rows, :]
        values = vr[cols, :]
        return [dot(head(da, h), values, NT) for h in range(2)]

    def grad_scores(ic, jc, dps):
        rows, cols = chunk_of(ic), chunk_of(jc)
        parts = []
        for h in range(2):
            p = p_ref[h, rows, cols]
            d, iv = corr[h], norm[h]
            parts.append(
                [
                    (
                        p[:, t * TILE : (t + 1) * TILE].astype(f4)
                        * ((dps[h][:, t * TILE : (t + 1) * TILE] - d) * iv)
                    ).astype(bf)
                    for t in range(2)
                ]
            )
        return parts

    def grad_skew(ic, jc, parts, ws, wt):
        for h in range(2):
            for t in range(2):
                for s in range(2):
                    sr = slice(s * TILE, (s + 1) * TILE)
                    ws[h, tile_of(2 * ic + s), tile_of(2 * jc + 2 + t)] = pltpu.roll(
                        parts[h][t][sr], 0, 1, stride=1, stride_axis=0
                    )
                    wt[h, tile_of(2 * jc + t), tile_of(2 * ic + 2 + s)] = pltpu.roll(
                        parts[h][t][sr].T, 1, 1, stride=1, stride_axis=0
                    )

    def grad_values(ic, jc, dvt):
        rows, cols = chunk_of(ic), chunk_of(jc)
        for h in range(2):
            half = slice(h * 64, (h + 1) * 64)
            dvt[half, cols] += dot(dat[half, rows], p_ref[h, rows, cols])

    def grad_out(ic, jc, parts, dq, dkt, qt):
        rows, cols = chunk_of(ic), chunk_of(jc)
        keys = kr[cols, :]
        whole = [jnp.concatenate(parts[h], axis=1) for h in range(2)]
        dq[rows, :] += both_heads(dot(whole[0], keys), dot(whole[1], keys))
        for h in range(2):
            half = slice(h * 64, (h + 1) * 64)
            dkt[half, cols] += dot(qt[half, rows], whole[h])

    def fold(ic, slot, first, ws, wt, qt, kt, gk, gq):
        rows = chunk_of(ic)
        w = chunk_of(jnp.clip(slot + 3 - ic, 1, NEAR) - 1)
        for ref, mask, table, out, turned, g in (
            (ws, late, rkr, dq2, qt, gk),
            (wt, early, rq_ref, dk2, kt, gq),
        ):
            rels = table[w, :]
            outs = []
            for h in range(2):
                band = []
                for s in range(2):
                    line = []
                    for b in range(2):
                        spot = 2 * slot + s + b
                        x = ref[h, tile_of(2 * ic + s), tile_of(spot)]
                        y = ref[h, tile_of(2 * ic + s), tile_of(spot + 1)]
                        line.append(jnp.where(mask, x, y))
                    band.append(jnp.concatenate(line, axis=1))
                band = jnp.concatenate(band, axis=0)
                outs.append(dot(band, rels))
                half = slice(h * 64, (h + 1) * 64)
                g[half, w] += dot(turned[half, rows], band)
            if first:
                out[rows, :] = both_heads(*outs)
            else:
                out[rows, :] += both_heads(*outs)

    def close(ic, dq, dkt, dvt):
        rows = chunk_of(ic)
        dqk_ref[rows, :TILE] = ((dq[rows, :] + dq2[rows, :]) * SCALE).astype(bf)
        for t in range(2):
            tr = tile_of(2 * ic + t)
            x = ((dkt[:, tr].T + dk2[tr, :]) * SCALE).astype(bf)
            dqk_ref[tr, TILE:] = dot(rev, x).astype(bf)
            dv_ref[tr, :] = dot(rev, dvt[:, tr].T.astype(bf)).astype(bf)
        dkt[:, rows] = jnp.zeros((TILE, CH), f4)
        dvt[:, rows] = jnp.zeros((TILE, CH), f4)

    def flush(gk, gq):
        g_ref[:TILE, :] = (gq[...] * SCALE).astype(bf)
        for t in range(NEAR * CH // TILE):
            cols = slice(t * TILE, (t + 1) * TILE)
            g_ref[TILE:, cols] = dot((gk[:, cols] * SCALE).astype(bf), rev).astype(bf)

    def sweep(before, body, idle):
        def chunk(ic, _):
            lo = b_ref[2 * NCH + ic]
            hi = b_ref[3 * NCH + ic]

            @pl.when(hi > lo)
            def _():
                before(ic, lo, hi)

            @pl.when(hi <= lo)
            def _():
                idle(ic)

            def block(jc, _):
                body(ic, jc)
                return 0

            lax.fori_loop(lo, hi, block, 0)
            return 0

        lax.fori_loop(0, NCH, chunk, 0)

    def no_fold(ic):
        dq2[chunk_of(ic), :] = jnp.zeros((CH, TILE), f4)
        dk2[chunk_of(ic), :] = jnp.zeros((CH, TILE), f4)

    def no_grad(ic, dq):
        dq[chunk_of(ic), :] = jnp.zeros((CH, TILE), f4)

    def fused(new, old):
        ws, wt, dq, dkt, dvt, qt, kt, gk_next, gq_next = new
        ws_, wt_, dq_, dkt_, dvt_, qt_, kt_, gk, gq = old
        prepare(qt, kt)
        turn_table()

        def before(ic, lo, hi):
            @pl.when(step < 2)
            def _():
                pads(ic, lo, hi, ws, wt)

            fold(ic, lo, True, ws_, wt_, qt_, kt_, gk, gq)
            open_grad(ic, dq)

        def body(ic, jc):
            dps = grad_start(ic, jc)
            fold(ic, jc + 1, False, ws_, wt_, qt_, kt_, gk, gq)
            grad_values(ic, jc, dvt)
            parts = grad_scores(ic, jc, dps)
            grad_skew(ic, jc, parts, ws, wt)
            grad_out(ic, jc, parts, dq, dkt, qt)

        def idle(ic):
            no_fold(ic)
            no_grad(ic, dq)

        sweep(before, body, idle)

        def finish(ic, _):
            close(ic, dq_, dkt_, dvt_)
            return 0

        lax.fori_loop(0, NCH, finish, 0)
        flush(gk, gq)
        clear(gk, gq)

    set0 = (ws0, wt0, dq0, dkt0, dvt0, qt0, kt0, gk0, gq0)
    set1 = (ws1, wt1, dq1, dkt1, dvt1, qt1, kt1, gk1, gq1)

    @pl.when(step == 0)
    def _():
        clear(dkt0, dkt1, dvt0, dvt1, gk0, gk1, gq0, gq1)
        prepare(qt0, kt0)

        def before(ic, lo, hi):
            pads(ic, lo, hi, ws0, wt0)
            open_grad(ic, dq0)

        def body(ic, jc):
            parts = grad_scores(ic, jc, grad_start(ic, jc))
            grad_values(ic, jc, dvt0)
            grad_skew(ic, jc, parts, ws0, wt0)
            grad_out(ic, jc, parts, dq0, dkt0, qt0)

        sweep(before, body, lambda ic: no_grad(ic, dq0))

    @pl.when((step > 0) & (step < last) & (step % 2 == 1))
    def _():
        fused(set1, set0)

    @pl.when((step > 0) & (step < last) & (step % 2 == 0))
    def _():
        fused(set0, set1)

    @pl.when(step == last)
    def _():
        turn_table()
        sweep(
            lambda ic, lo, hi: fold(ic, lo, True, ws1, wt1, qt1, kt1, gk1, gq1),
            lambda ic, jc: fold(ic, jc + 1, False, ws1, wt1, qt1, kt1, gk1, gq1),
            no_fold,
        )

        def finish(ic, _):
            close(ic, dq1, dkt1, dvt1)
            return 0

        lax.fori_loop(0, NCH, finish, 0)
        flush(gk1, gq1)


def attend_backward(bounds, both, v, da, att, inv, spread, p):
    pairs = v.shape[1] // TILE

    def col(n, lag, at=0, every=1):
        return pl.BlockSpec(
            (n, TILE), lambda s, *_: (0, at + every * jnp.clip(s - lag, 0, pairs - 1))
        )

    def out(at):
        return lambda s, *_: (jnp.clip(s - 1, 0, pairs - 1), 0)[:: 1 - 2 * at]

    def twice(shape, dtype):
        return [pltpu.VMEM(shape, dtype)] * 2

    return pl.pallas_call(
        bwd_kernel,
        grid_spec=pltpu.PrefetchScalarGridSpec(
            num_scalar_prefetch=1,
            grid=(pairs + 1,),
            in_specs=[
                col(LEN, 0, 0, 2),
                col(LEN, 0, 1, 2),
                col(LEN, 0),
                col(LEN, 0),
                col(LEN, 0),
                col(LEN, 0),
                pl.BlockSpec((2, LEN, LEN), lambda s, *_: (jnp.minimum(s, pairs - 1), 0, 0)),
                col(NEAR * CH, 1, 1, 2),
                col(NEAR * CH, 1, 0, 2),
            ],
            out_specs=[
                pl.BlockSpec((LEN, 2 * TILE), out(1)),
                col(LEN, 1),
                pl.BlockSpec((2 * TILE, NEAR * CH), out(0)),
            ],
            scratch_shapes=twice((2, LEN, LEN + 2 * CH), bf)
            + twice((2, LEN, LEN + 2 * CH), bf)
            + twice((LEN, TILE), f4)
            + twice((TILE, LEN), f4)
            + twice((TILE, LEN), f4)
            + twice((TILE, LEN), bf)
            + twice((TILE, LEN), bf)
            + twice((TILE, NEAR * CH), f4)
            + twice((TILE, NEAR * CH), f4)
            + [pltpu.VMEM((TILE, LEN), bf)]
            + [pltpu.VMEM((LEN, TILE), bf)] * 2
            + [pltpu.VMEM((NEAR * CH, TILE), bf)]
            + [pltpu.VMEM((LEN, TILE), f4)] * 2
            + [pltpu.VMEM((2, CH, TILE), f4)] * 2,
        ),
        out_shape=[
            jax.ShapeDtypeStruct(both.shape, bf),
            jax.ShapeDtypeStruct(v.shape, bf),
            jax.ShapeDtypeStruct((both.shape[1], NEAR * CH), bf),
        ],
        compiler_params=pltpu.CompilerParams(vmem_limit_bytes=60 << 20),
        name="attend_backward",
    )(bounds, both, both, v, da, att, inv, p, spread, spread)


def gelu_pair(u):
    size = jnp.abs(u)
    bell = jnp.exp2(u * u * (-0.5 * math.log2(math.e)))
    t = 1.0 / (1.0 + (0.3275911 / math.sqrt(2.0)) * size)
    poly = 0.5 * 1.061405429
    for c in (-1.453152027, 1.421413741, -0.284496736, 0.254829592):
        poly = poly * t + 0.5 * c
    tail = poly * t * bell
    phi = jnp.where(u < 0.0, tail, 1.0 - tail)
    return u * phi, phi + u * bell * (1.0 / math.sqrt(2.0 * math.pi))


def middle_kernel(
    hid_ref, att_ref, wo_ref, we_ref, wc_ref, vec_ref, mask_ref, cot_ref,
    out_ref, dfirst_ref, datt_ref, grad_ref,
    pre, slope, acc, norm_, act, dexp, low, dtwo, dbranch, attended, turned, sums,
):
    step = pl.program_id(0)
    blocks = act.shape[0] // TOK
    parts = act.shape[1] // low.shape[1]

    @pl.when(step < blocks)
    def _():
        rows = pl.ds(al(step * TOK, TOK), TOK)
        views = [ref.at[rows] for ref in (act, dexp, low, dtwo, dbranch, attended)]
        token_block(
            step, hid_ref, att_ref, wo_ref, we_ref, wc_ref, vec_ref, mask_ref, cot_ref,
            out_ref, dfirst_ref, datt_ref, pre, slope, acc, norm_, sums, *views,
        )

    @pl.when(step >= blocks)
    def _():
        weight_block(
            step - blocks, parts, act, dexp, low, dtwo, dbranch, attended, turned, sums, grad_ref
        )


def token_block(
    step, hid_ref, att_ref, wo_ref, we_ref, wc_ref, vec_ref, mask_ref, cot_ref,
    out_ref, dfirst_ref, datt_ref, pre, slope, acc, norm_, sums,
    act_ref, dexp_ref, low_ref, dtwo_ref, dbranch_ref, attb_ref,
):
    width = hid_ref.shape[1]
    chunks = we_ref.shape[1] // FCH
    vectors = vec_ref[...].astype(f4).T
    gain_one = vectors[0:1, :]
    shift_one = vectors[1:2, :]
    gain_two = vectors[2:3, :]
    shift_two = vectors[3:4, :]
    inv = 1.0 / width
    attb_ref[...] = att_ref[...].astype(bf)
    first = hid_ref[...].astype(f4) + dot(attb_ref[...], wo_ref[...])
    cen = first - jnp.sum(first, axis=1, keepdims=True) * inv
    rstd_one = lax.rsqrt(jnp.sum(cen * cen, axis=1, keepdims=True) * inv + NORM_EPS)
    n_one = cen * rstd_one
    norm_[...] = n_one
    normed = n_one * gain_one + shift_one
    low_ref[...] = normed.astype(bf)
    acc[...] = jnp.zeros(acc.shape, f4)

    def cols(c):
        return slice(c * FCH, (c + 1) * FCH)

    def expand(c):
        pre[c % 2] = dot(low_ref[...], we_ref[:, cols(c)])

    def bend(c):
        value, grad = gelu_pair(pre[c % 2])
        act_ref[:, cols(c)] = value.astype(bf)
        slope[:, cols(c)] = grad.astype(bf)

    def contract(c):
        acc[...] += dot(act_ref[:, cols(c)], wc_ref[:, cols(c)])

    expand(0)
    expand(1)
    bend(0)

    def steady(c, _):
        expand(c + 1)
        bend(c)
        contract(c - 1)
        return 0

    for c in range(1, chunks - 1):
        steady(c, 0)
    bend(chunks - 1)
    contract(chunks - 2)
    contract(chunks - 1)
    branch = acc[...]
    turned = [
        jnp.broadcast_to(mask_ref[:, t : t + TILE].astype(f4), (TILE, TILE)).T
        for t in range(0, TOK, TILE)
    ]
    mask = jnp.concatenate(turned, axis=0)[:, 0:1]
    normed = norm_[...] * gain_one + shift_one
    second = normed + branch
    row_res = jnp.sum(mask * second * second, axis=0, keepdims=True)
    row_sub = jnp.sum(mask * branch * branch, axis=0, keepdims=True)
    cen = second - jnp.sum(second, axis=1, keepdims=True) * inv
    rstd = lax.rsqrt(jnp.sum(cen * cen, axis=1, keepdims=True) * inv + NORM_EPS)
    n_two = cen * rstd
    out_ref[...] = (n_two * gain_two + shift_two).astype(bf)
    up = cot_ref[...].astype(f4) * mask
    row_g2 = jnp.sum(up * n_two, axis=0, keepdims=True)
    row_s2 = jnp.sum(up, axis=0, keepdims=True)
    g = up * gain_two
    d_second = (
        g
        - jnp.sum(g, axis=1, keepdims=True) * inv
        - n_two * (jnp.sum(g * n_two, axis=1, keepdims=True) * inv)
    ) * rstd
    dtwo_ref[...] = d_second.astype(bf)
    acc[...] = d_second

    def back(c):
        grad = dot(dtwo_ref[...], wc_ref[:, cols(c)], NT) * slope[:, cols(c)].astype(f4)
        dexp_ref[:, cols(c)] = grad.astype(bf)

    def into(c):
        acc[...] += dot(dexp_ref[:, cols(c)], we_ref[:, cols(c)], NT)

    back(0)

    def steady_back(c, _):
        back(c)
        into(c - 1)
        return 0

    for c in range(1, chunks):
        steady_back(c, 0)
    into(chunks - 1)
    up = acc[...]
    n_one = norm_[...]
    row_g1 = jnp.sum(up * n_one, axis=0, keepdims=True)
    row_s1 = jnp.sum(up, axis=0, keepdims=True)
    g = up * gain_one
    d_first = (
        g
        - jnp.sum(g, axis=1, keepdims=True) * inv
        - n_one * (jnp.sum(g * n_one, axis=1, keepdims=True) * inv)
    ) * rstd_one
    dfirst_ref[...] = d_first
    low = d_first.astype(bf)
    dbranch_ref[...] = low
    datt_ref[...] = dot(low, wo_ref[...], NT).astype(bf)
    rows = jnp.concatenate(
        [row_g1, row_s1, row_g2, row_s2, row_res, row_sub, jnp.zeros((2, width), f4)], axis=0
    )

    @pl.when(step == 0)
    def _():
        sums[...] = rows

    @pl.when(step > 0)
    def _():
        sums[...] += rows


def weight_block(
    step, parts, act, dexp, low, dtwo, dbranch, attended, turned, sums, out_ref
):
    width = low.shape[1]

    @pl.when(step == 0)
    def _():
        turned[...] = low[...].T

    @pl.when(step < parts)
    def _():
        cols = pl.ds(al(step * width, width), width)
        out_ref[...] = dot(turned[...], dexp[:, cols]).astype(bf)

    @pl.when((step >= parts) & (step < 2 * parts))
    def _():
        cols = pl.ds(al((step - parts) * width, width), width)
        out_ref[...] = dot(act[:, cols].T, dtwo[...]).astype(bf)

    @pl.when(step == 2 * parts)
    def _():
        out_ref[...] = dot(attended[...].T, dbranch[...]).astype(bf)

    @pl.when(step == 2 * parts + 1)
    def _():
        rows = sums[...]
        total = jnp.broadcast_to(jnp.sum(rows[4:6], axis=1, keepdims=True), (2, width))
        full = jnp.concatenate([rows[:4], total, jnp.zeros((TILE - 6, width), f4)], axis=0)
        out_ref[:, :TILE] = full.T.astype(bf)


def middle(hidden, attended, weights, wide, mask, cotangent):
    tokens, width = hidden.shape
    blocks = tokens // TOK
    parts = wide // width
    tok = lambda n: pl.BlockSpec((TOK, n), lambda i: (jnp.minimum(i, blocks - 1), 0))
    once = lambda n, at: pl.BlockSpec(
        (width, n), lambda i: (0, at // n), pipeline_mode=pl.Buffered(1)
    )
    shape = lambda n, dtype: jax.ShapeDtypeStruct((tokens, n), dtype)
    whole = lambda n: pltpu.VMEM((tokens, n), bf)
    return pl.pallas_call(
        middle_kernel,
        grid=(blocks + 2 * parts + 2,),
        in_specs=[
            tok(width),
            tok(width),
            once(width, 2 * wide),
            once(wide, 0),
            once(wide, wide),
            once(TILE, 2 * wide + width),
            pl.BlockSpec((1, TOK), lambda i: (0, jnp.minimum(i, blocks - 1))),
            tok(width),
        ],
        out_specs=[
            tok(width),
            tok(width),
            tok(width),
            pl.BlockSpec((width, width), lambda i: (0, jnp.maximum(i - blocks, 0))),
        ],
        out_shape=[
            shape(width, bf),
            shape(width, f4),
            shape(width, bf),
            jax.ShapeDtypeStruct((width, 2 * wide + width + TILE), bf),
        ],
        scratch_shapes=[
            pltpu.VMEM((2, TOK, FCH), f4),
            pltpu.VMEM((TOK, wide), bf),
            pltpu.VMEM((TOK, width), f4),
            pltpu.VMEM((TOK, width), f4),
            whole(wide),
            whole(wide),
            whole(width),
            whole(width),
            whole(width),
            whole(width),
            pltpu.VMEM((width, tokens), bf),
            pltpu.VMEM((8, width), f4),
        ],
        compiler_params=pltpu.CompilerParams(vmem_limit_bytes=60 << 20),
        name="middle",
    )(hidden, attended, weights, weights, weights, weights, mask, cotangent)


def lane_pieces(size, count, parts, per, forward):
    found = [[] for _ in range(size // TILE)]
    for device in range(count):
        for part in range(parts):
            source = (device * parts + part) * per
            target = part * count * per + device * per
            if not forward:
                source, target = target, source
            done = 0
            while done < per:
                at, to = source + done, target + done
                span = min(per - done, TILE - at % TILE, TILE - to % TILE)
                found[to // TILE].append((at // TILE, at % TILE, to % TILE, span))
                done += span
    return found


def permute_lanes(load, store, rows, pieces):
    lane = lax.broadcasted_iota(jnp.int32, (rows, TILE), 1)
    for block, group in enumerate(pieces):
        total = jnp.zeros((rows, TILE), f4)
        for at, offset, spot, span in group:
            moved = load(at)
            if spot != offset:
                moved = pltpu.roll(moved, (spot - offset) % TILE, 1)
            total = jnp.where((lane >= spot) & (lane < spot + span), moved, total)
        store(block, total)


def lanes(block):
    return slice(block * TILE, (block + 1) * TILE)


def pack_kernel(
    count, query_ref, key_ref, value_ref, table_ref, expand_ref, contract_ref, output_ref,
    small_ref, first_ref, second_ref, out_ref,
):
    per, wide = expand_ref.shape
    width = output_ref.shape[1]
    parts = wide // width
    for block in range(width // TILE):
        first_ref[:, lanes(2 * block)] = query_ref[:, lanes(block)]
        first_ref[:, lanes(2 * block + 1)] = key_ref[:, lanes(block)]
    rows = jnp.concatenate([value_ref[...].astype(f4), table_ref[...].astype(f4)], axis=0)
    second_ref[...] = rows.astype(bf)

    def store(block, value):
        out_ref[:, lanes(block)] = value.astype(bf)

    permute_lanes(
        lambda at: expand_ref[:, lanes(at)].astype(f4),
        store,
        per,
        lane_pieces(wide, count, parts, per, True),
    )
    rows = contract_ref[...].astype(f4)
    for part in range(parts):
        at = wide + part * width
        out_ref[:, at : at + width] = rows[part * per : (part + 1) * per].astype(bf)
    out_ref[:, 2 * wide : 2 * wide + width] = output_ref[...]
    out_ref[:, 2 * wide + width :] = small_ref[...]


def pack_weights(count, query, key, value, table, expand, contract, output, small):
    per, wide = expand.shape
    width = output.shape[1]
    shape = lambda a, b: jax.ShapeDtypeStruct((a, b), bf)
    return pl.pallas_call(
        partial(pack_kernel, count),
        out_shape=[
            shape(per, 2 * width),
            shape(per + table.shape[0], width),
            shape(per, 2 * wide + width + TILE),
        ],
        name="pack_weights",
    )(query, key, value, table, expand, contract, output, small)


def finish_kernel(count, cells, own_ref, expand_ref, contract_ref, output_ref, *rest):
    per, wide = expand_ref.shape
    width = output_ref.shape[1]
    parts = wide // width

    def store(block, value):
        expand_ref[:, lanes(block)] = value

    permute_lanes(
        lambda at: own_ref[:, lanes(at)].astype(f4),
        store,
        per,
        lane_pieces(wide, count, parts, per, False),
    )
    for part in range(parts):
        at = wide + part * width
        contract_ref[part * per : (part + 1) * per, :] = own_ref[:, at : at + width].astype(f4)
    output_ref[...] = own_ref[:, 2 * wide : 2 * wide + width].astype(f4)
    turned = own_ref[:, 2 * wide + width :].astype(f4).T
    for number, ref in enumerate(rest[:4]):
        ref[...] = turned[number : number + 1, :]
    for number, ref in enumerate(rest[4:]):
        ref[...] = jnp.sqrt(turned[4 + number : 5 + number, :1] * (1.0 / cells))


def finish_grads(count, cells, own, wide, width):
    per = own.shape[0]
    shape = lambda a, b: jax.ShapeDtypeStruct((a, b), f4)
    return pl.pallas_call(
        partial(finish_kernel, count, cells),
        out_shape=[
            shape(per, wide),
            shape(per * (wide // width), width),
            shape(per, width),
            *[shape(1, per)] * 4,
            *[shape(1, 1)] * 2,
        ],
        name="finish_grads",
    )(own)


def digits(count):
    found = [(1, 2)]
    stride = 2
    while stride < count:
        radix = 4 if count // stride >= 4 else 2
        found.append((stride, radix))
        stride *= radix
    return found


def place(relative, count):
    spot = relative * 0
    for stride, radix in digits(count):
        spot = spot * radix + ((relative >> (stride.bit_length() - 1)) & (radix - 1))
    return spot


def mixing(size, count, me):
    per = size // count
    row = np.arange(size)
    target = place(jnp.asarray(row // per, jnp.int32) ^ me, count) * per + (row % per)
    spots = lax.broadcasted_iota(jnp.int32, (size, size), 1)
    return (target[:, None] == spots).astype(bf)


def near_index():
    index = bucket_index(LEN - np.arange(2 * LEN), BUCKETS).reshape(-1, CH)
    assert (index[:2] == index[0, 0]).all() and (index[-2:] == index[-1, -1]).all()
    return index[1:-1].reshape(-1)


def offset_rows(count, me):
    index = near_index()
    size = 2 * BUCKETS
    per = size // count
    target = place(jnp.asarray(index // per, jnp.int32) ^ me, count) * per + (index % per)
    spots = lax.broadcasted_iota(jnp.int32, (index.shape[0], size), 1)
    return (target[:, None] == spots).astype(bf)


def swap(value, offset, count):
    return lax.ppermute(value, "fsdp", [(i, i ^ offset) for i in range(count)])


def together(values):
    return list(lax.optimization_barrier(tuple(values)))


def gather_pair(first, second, count, beside, work):
    middle = digits(count)[1:]
    one, two = first[None], second[None]
    later = None
    for (stride_a, radix_a), (stride_b, radix_b) in zip(middle[::-1], middle):
        got_a = [one]
        got_b = [two]
        for step in range(1, max(radix_a, radix_b)):
            if step < radix_a:
                got_a.append(swap(one, step * stride_a, count))
            if step < radix_b:
                got_b.append(swap(two, step * stride_b, count))
        one, two, *beside = together(
            [jnp.concatenate(got_a, axis=0), jnp.concatenate(got_b, axis=0), *beside]
        )
        if later is None:
            later, beside = beside[0], work(beside[1])
    radices = [radix for _, radix in middle[::-1]]
    two = two.reshape(*radices, *second.shape)
    turn = tuple(range(len(middle)))[::-1]
    two = two.transpose(turn + (len(middle), len(middle) + 1)).reshape(-1, *second.shape)
    return (one, swap(one, 1, count)), (two, swap(two, 1, count)), later, beside


def scatter_pair(first, second, count, beside):
    middle = digits(count)[1:]
    radices = [radix for _, radix in middle]
    shape_a, shape_b = first.shape[1:], second.shape[1:]
    half_a = first.reshape(2, -1, *shape_a)
    half_b = second.reshape(2, -1, *shape_b)
    one, two = together(
        [
            half_a[0].astype(f4) + swap(half_a[1], 1, count).astype(f4),
            half_b[0].astype(f4) + swap(half_b[1], 1, count).astype(f4),
        ]
    )
    one = one.astype(bf).reshape(*radices, *shape_a)
    two = two.astype(bf).reshape(*radices, *shape_b)
    for step, ((stride_a, radix_a), (stride_b, radix_b)) in enumerate(zip(middle, middle[::-1])):
        last = two.ndim - 3
        got_a = []
        got_b = []
        for hop in range(1, max(radix_a, radix_b)):
            if hop < radix_a:
                got_a.append(swap(one[hop], hop * stride_a, count))
            if hop < radix_b:
                got_b.append(
                    swap(lax.index_in_dim(two, hop, last, keepdims=False), hop * stride_b, count)
                )
        sum_a = one[0].astype(f4)
        sum_b = lax.index_in_dim(two, 0, last, keepdims=False).astype(f4)
        if step == 0:
            *got, beside = together(got_a + got_b + [beside])
        else:
            got = together(got_a + got_b)
        for piece in got[: len(got_a)]:
            sum_a = sum_a + piece.astype(f4)
        for piece in got[len(got_a) :]:
            sum_b = sum_b + piece.astype(f4)
        if step == len(middle) - 1:
            return sum_a, sum_b, beside
        one, two = sum_a.astype(bf), sum_b.astype(bf)


def active_chunks(segment, valid):
    rows = segment.reshape(NCH, CH)
    ok = valid.reshape(NCH, CH) > 0
    first = rows[:, 0]
    last = rows[:, -1]
    over = (first[None, :] <= last[:, None]) & (last[None, :] >= first[:, None])
    real = jnp.max(jnp.where(ok, rows, -1), axis=1)
    back = (first[None, :] <= real[:, None]) & (last[None, :] >= first[:, None])
    back = back | back.T
    place_ = jnp.arange(NCH)[None, :]

    def limits(mask):
        lo = jnp.min(jnp.where(mask, place_, NCH), axis=1)
        hi = jnp.max(jnp.where(mask, place_ + 1, 0), axis=1)
        return jnp.where(hi > 0, lo, 0), hi

    return jnp.concatenate(limits(over) + limits(back)).astype(jnp.int32)


def mm(left, right, dims=NN):
    return lax.dot_general(left, right, dims, preferred_element_type=f4)


def shards(
    hidden,
    query_weight,
    key_weight,
    value_weight,
    output_weight,
    relative_table,
    first_gain,
    first_shift,
    expand_weight,
    contract_weight,
    second_gain,
    second_shift,
    segment_ids,
    valid,
    cotangent,
):
    count = lax.axis_size("fsdp")
    me = lax.axis_index("fsdp")
    width = hidden.shape[1]
    wide = expand_weight.shape[1]
    per = query_weight.shape[0]
    per_t = relative_table.shape[0]
    per_c = contract_weight.shape[0]
    parts = wide // width

    small = jnp.stack([first_gain, first_shift, second_gain, second_shift], axis=1)
    small = jnp.pad(small, ((0, 0), (0, TILE - 4)))
    first, second, rest = pack_weights(
        count,
        query_weight,
        key_weight,
        value_weight,
        relative_table,
        expand_weight,
        contract_weight,
        output_weight,
        small,
    )

    def aside(number):
        mix = mixing(width, count, number)
        return [
            mix,
            mm(hidden, mix).astype(bf),
            offset_rows(count, number),
            active_chunks(segment_ids, valid),
        ]

    pair_a, pair_b, rest, (mix, hidden_mixed, onehot, bounds) = gather_pair(
        first, second, count, [rest, me], aside
    )
    query_key = jnp.concatenate(pair_a, axis=0).reshape(count * per, 2 * width)
    value_full = jnp.concatenate([x[:, :per] for x in pair_b], axis=0)
    value_full = value_full.reshape(count * per, width)
    table = jnp.concatenate([x[:, per:] for x in pair_b], axis=0).reshape(count * per_t, width)

    weights = lax.all_gather(rest, "fsdp", axis=0, tiled=True)

    table_mixed = mm(table, mix).astype(bf)
    both_rows = mm(hidden_mixed, query_key).astype(bf)
    value_rows = mm(hidden_mixed, value_full).astype(bf)
    (position,) = together([mm(table_mixed, query_key).astype(bf)])
    spread_rows = mm(onehot, position).astype(bf)
    attended_wide, inverse, probs = attend_forward(
        bounds, both_rows, value_rows, spread_rows, segment_ids[None, :]
    )
    result, d_first, attended_gradient, grads = middle(
        hidden, attended_wide, weights, wide, valid[None, :], cotangent
    )
    owned = lax.psum_scatter(grads, "fsdp", scatter_dimension=0, tiled=True)
    both_low, value_low, offset_grad = attend_backward(
        bounds,
        both_rows,
        value_rows,
        attended_gradient,
        attended_wide,
        inverse,
        spread_rows,
        probs,
    )
    position_low = mm(offset_grad, onehot).astype(bf)
    grad_pack = mm(hidden_mixed, both_low, ROWS_FIRST) + mm(
        table_mixed, position_low, (((0,), (1,)), ((), ()))
    )
    grad_pack = grad_pack.astype(bf).reshape(count, per, 2 * width)
    grad_value = mm(hidden_mixed, value_low, ROWS_FIRST)
    grad_table = mm(position_low, query_key, (((0,), (1,)), ((), ())))
    grad_table = mm(grad_table.astype(bf), mix, NT).astype(bf)
    grad_value = jnp.concatenate(
        [
            grad_value.astype(bf).reshape(count, per, width),
            grad_table.reshape(count, per_t, width),
        ],
        axis=1,
    )
    d_input = mm(both_low, query_key, NT) + mm(value_low, value_full, NT)
    own_pack, own_value, d_input = scatter_pair(grad_pack, grad_value, count, d_input.astype(bf))
    d_input = d_first + mm(d_input, mix, NT)
    cells = float(hidden.shape[0] * count * width)
    expand_owned, contract_owned, output_owned, *last = finish_grads(
        count, cells, owned, wide, width
    )
    own_pack = own_pack.reshape(per, -1, 2, TILE)
    return (
        result,
        d_input.astype(bf),
        own_pack[:, :, 0].reshape(per, width),
        own_pack[:, :, 1].reshape(per, width),
        own_value[:per],
        output_owned,
        own_value[per:],
        last[0].reshape(per),
        last[1].reshape(per),
        expand_owned,
        contract_owned,
        last[2].reshape(per),
        last[3].reshape(per),
        last[4].reshape(()),
        last[5].reshape(()),
    )


def solution(mesh):
    in_specs = (
        P("fsdp", None),
        P("fsdp", None),
        P("fsdp", None),
        P("fsdp", None),
        P("fsdp", None),
        P("fsdp", None),
        P("fsdp"),
        P("fsdp"),
        P("fsdp", None),
        P("fsdp", None),
        P("fsdp"),
        P("fsdp"),
        P("fsdp"),
        P("fsdp"),
        P("fsdp", None),
    )
    out_specs = (
        P("fsdp", None),
        P("fsdp", None),
        P("fsdp", None),
        P("fsdp", None),
        P("fsdp", None),
        P("fsdp", None),
        P("fsdp", None),
        P("fsdp"),
        P("fsdp"),
        P("fsdp", None),
        P("fsdp", None),
        P("fsdp"),
        P("fsdp"),
        P(),
        P(),
    )
    return jax.shard_map(shards, mesh=mesh, in_specs=in_specs, out_specs=out_specs, check_vma=False)
```

```python
from functools import partial
import math

import jax
import jax.numpy as jnp
import numpy as np
from jax import lax
from jax.experimental import pallas as pl
from jax.experimental.pallas import tpu as pltpu
from jax.sharding import PartitionSpec as P

bf = jnp.bfloat16
f4 = jnp.float32
HEADS = 12
BUCKETS = 256
LEN = 1024
TILE = 128
CH = 256
NCH = LEN // CH
SCALE = 1.0 / math.sqrt(192.0)
NORM_EPS = 1e-07
MASKED = -1e30
TOK = 256
NEAR = 6
FCH = 768
ROWS_FIRST = (((0,), (0,)), ((), ()))
ROWS_LAST = (((1,), (1,)), ((), ()))
NT = ROWS_LAST
NN = (((1,), (0,)), ((), ()))


def bucket_index(offsets, buckets):
    middle = buckets // 2
    limit = 2 * buckets
    magnitude = np.abs(offsets)
    inside = (offsets < middle) & (offsets > -middle)
    clipped = np.where(inside, middle - 1, magnitude)
    logged = (
        np.ceil(np.log(clipped / middle) / np.log((limit - 1) / middle) * (middle - 1)) + middle
    )
    bucket = np.where(magnitude <= middle, offsets, (logged * np.sign(offsets)).astype(np.int32))
    return np.clip(bucket + buckets, 0, 2 * buckets - 1).astype(np.int32)


def dot(a,b,dims=NN): return lax.dot_general(a,b,dims,preferred_element_type=f4)
def al(x,m): return pl.multiple_of(x,m)
def iotas():
    r=lax.broadcasted_iota(jnp.int32,(TILE,TILE),0); c=lax.broadcasted_iota(jnp.int32,(TILE,TILE),1)
    return r,c


def fwd_kernel(
    b_ref, qa_ref, ka_ref, rk_ref, rq_ref, qb_ref, kb_ref, v_ref, segr_ref,
    att_ref, inv_ref, p_ref,
    xs0, xs1, ys0, ys1, sc0, sc1, mx0, mx1, top, sm, acc, segb,
):
    r, c = iotas()
    eye = (r == c).astype(f4).astype(bf)
    rev = (r + c == TILE - 1).astype(f4).astype(bf)
    early = (r + c) < TILE
    lane = lax.broadcasted_iota(jnp.int32, (CH, TILE), 1)
    left = lane < 64
    lane_t = lax.broadcasted_iota(jnp.int32, (TILE, TILE), 1)
    left_t = lane_t < 64
    step = pl.program_id(0)
    last = pl.num_programs(0) - 1
    fac = SCALE * math.log2(math.e)

    def head(x, h, mask):
        zero = jnp.zeros(x.shape, bf)
        return jnp.where(mask, x, zero) if h == 0 else jnp.where(mask, zero, x)

    def product(ic, slot, xs, ys):
        rows = pl.ds(al(ic * CH, CH), CH)
        w = pl.ds(al((jnp.clip(slot + 3 - ic, 1, NEAR) - 1) * CH, CH), CH)
        out = pl.ds(al(slot * CH, CH), CH)
        q = qa_ref[rows, :]
        k = ka_ref[rows, :]
        for h in range(2):
            xs[h, rows, out] = dot(head(q, h, left), rk_ref[w, :], NT).astype(bf)
            ys[h, rows, out] = dot(head(k, h, left), rq_ref[w, :], NT).astype(bf)

    def skewed(ref, h, row, spot):
        rr = pl.ds(al(row * TILE, TILE), TILE)
        a = ref[h, rr, pl.ds(al((spot + 2) * TILE, TILE), TILE)]
        b = ref[h, rr, pl.ds(al((spot + 1) * TILE, TILE), TILE)]
        return pltpu.roll(jnp.where(early, a, b), 0, 1, stride=1, stride_axis=0)

    def score(ic, jc, s, xs, ys, sc, mx):
        cols = pl.ds(al(jc * CH, CH), CH)
        segc = segr_ref[:, cols].astype(f4)
        keys = kb_ref[cols, :]
        i = 2 * ic + s
        rows = pl.ds(al(i * TILE, TILE), TILE)
        srow = segb[rows, :]
        q = qb_ref[rows, :]
        for h in range(2):
            turned = [skewed(ys, h, 2 * jc + t, i - t) for t in range(2)]
            lhs = jnp.concatenate([head(q, h, left_t), eye], axis=1)
            rhs = jnp.concatenate([keys, jnp.concatenate(turned, axis=0)], axis=1)
            content = dot(lhs, rhs, NT)
            best = mx[h, rows, :]
            for t in range(2):
                along = skewed(xs, h, i, 2 * jc + t - s).astype(f4)
                ok = srow == segc[:, t * TILE : (t + 1) * TILE]
                val = jnp.where(ok, content[:, t * TILE : (t + 1) * TILE] + along, MASKED)
                sc[h, rows, pl.ds(al(jc * CH + t * TILE, TILE), TILE)] = val
                best = jnp.maximum(best, val)
            mx[h, rows, :] = best

    def mix(ic, jc, h, sc):
        rows = pl.ds(al(ic * CH, CH), CH)
        tot = sm[h]
        peak = top[h]
        for t in range(2):
            cols = pl.ds(al(jc * CH + t * TILE, TILE), TILE)
            e = jnp.exp2((sc[h, rows, cols] - peak) * fac)
            tot = tot + e
            rhs = jnp.concatenate([head(v_ref[cols, :], h, left_t), rev], axis=1)
            res = dot(e.astype(bf), rhs)
            acc[...] += res[:, :TILE]
            p_ref[h, rows, cols] = res[:, TILE:].astype(bf)
        sm[h] = tot

    def open_scores(ic, mx):
        rows = pl.ds(al(ic * CH, CH), CH)
        for h in range(2):
            mx[h, rows, :] = jnp.full((CH, TILE), MASKED, f4)

    def open_mix(ic, mx):
        rows = pl.ds(al(ic * CH, CH), CH)
        for h in range(2):
            peak = jnp.max(mx[h, rows, :], axis=1, keepdims=True)
            top[h] = jnp.broadcast_to(peak, (CH, TILE))
            sm[h] = jnp.zeros((CH, TILE), f4)
        acc[...] = jnp.zeros((CH, TILE), f4)

    def close_mix(ic):
        rows = pl.ds(al(ic * CH, CH), CH)
        inv = [1.0 / jnp.sum(sm[h], axis=1, keepdims=True) for h in range(2)]
        pair = jnp.where(
            left, jnp.broadcast_to(inv[0], (CH, TILE)), jnp.broadcast_to(inv[1], (CH, TILE))
        )
        inv_ref[rows, :] = pair
        att_ref[rows, :] = acc[...] * pair

    def sweep(before, body, after):
        def chunk(ic, _):
            lo = b_ref[ic]
            hi = b_ref[NCH + ic]
            before(ic, lo)

            def block(jc, _):
                body(ic, jc)
                return 0

            lax.fori_loop(lo, hi, block, 0)
            after(ic)
            return 0

        lax.fori_loop(0, NCH, chunk, 0)

    def fused(xs_new, ys_new, xs, ys, sc_new, mx_new, sc, mx):
        def before(ic, lo):
            product(ic, lo, xs_new, ys_new)
            open_scores(ic, mx_new)
            open_mix(ic, mx)

        def body(ic, jc):
            product(ic, jc + 1, xs_new, ys_new)
            for part in range(2):
                mix(ic, jc, part, sc)
                score(ic, jc, part, xs, ys, sc_new, mx_new)

        sweep(before, body, close_mix)

    @pl.when(step == 0)
    def _():
        for t in range(LEN // TILE):
            cols = slice(t * TILE, (t + 1) * TILE)
            row = jnp.broadcast_to(segr_ref[:, cols].astype(f4), (TILE, TILE))
            segb[cols, :] = row.T
        sweep(
            lambda ic, lo: product(ic, lo, xs0, ys0),
            lambda ic, jc: product(ic, jc + 1, xs0, ys0),
            lambda ic: None,
        )

    @pl.when((step > 0) & (step < last) & (step % 2 == 1))
    def _():
        fused(xs1, ys1, xs0, ys0, sc1, mx1, sc0, mx0)

    @pl.when((step > 0) & (step < last) & (step % 2 == 0))
    def _():
        fused(xs0, ys0, xs1, ys1, sc0, mx0, sc1, mx1)

    @pl.when(step == last)
    def _():
        def body(ic, jc):
            mix(ic, jc, 0, sc0)
            mix(ic, jc, 1, sc0)

        sweep(lambda ic, lo: open_mix(ic, mx0), body, close_mix)


def attend_forward(bounds, both, v, spread, segr):
    pairs = v.shape[1] // TILE

    def col(n, lag, at=0, every=2):
        return pl.BlockSpec(
            (n, TILE), lambda s, *_: (0, at + every * jnp.clip(s - lag, 0, pairs - 1))
        )

    def wide(lag):
        return pl.BlockSpec((2, LEN, LEN), lambda s, *_: (jnp.clip(s - lag, 0, pairs - 1), 0, 0))

    window = pltpu.VMEM((2, LEN, LEN + CH), bf)
    return pl.pallas_call(
        fwd_kernel,
        grid_spec=pltpu.PrefetchScalarGridSpec(
            num_scalar_prefetch=1,
            grid=(pairs + 2,),
            in_specs=[
                col(LEN, 0),
                col(LEN, 0, 1),
                col(NEAR * CH, 0, 1),
                col(NEAR * CH, 0),
                col(LEN, 1),
                col(LEN, 1, 1),
                col(LEN, 2, 0, 1),
                pl.BlockSpec((1, LEN), lambda s, *_: (0, 0)),
            ],
            out_specs=[col(LEN, 2, 0, 1), col(LEN, 2, 0, 1), wide(2)],
            scratch_shapes=[window] * 4
            + [pltpu.VMEM((2, LEN, LEN), f4)] * 2
            + [pltpu.VMEM((2, LEN, TILE), f4)] * 2
            + [pltpu.VMEM((2, CH, TILE), f4)] * 2
            + [pltpu.VMEM((CH, TILE), f4)]
            + [pltpu.VMEM((LEN, TILE), f4)],
        ),
        out_shape=[
            jax.ShapeDtypeStruct(v.shape, f4),
            jax.ShapeDtypeStruct(v.shape, f4),
            jax.ShapeDtypeStruct((2 * pairs, LEN, LEN), bf),
        ],
        compiler_params=pltpu.CompilerParams(vmem_limit_bytes=60 << 20),
        name="attend_forward",
    )(bounds, both, both, spread, spread, both, both, v, segr)


def bwd_kernel(
    b_ref, q_ref, k_ref, v_ref, da_ref, att_ref, inv_ref, p_ref, rk_ref, rq_ref,
    dqk_ref, dv_ref, g_ref,
    ws0, ws1, wt0, wt1, dq0, dq1, dkt0, dkt1, dvt0, dvt1, qt0, qt1, kt0, kt1,
    gk0, gk1, gq0, gq1, dat, vr, kr, rkr, dq2, dk2, corr, norm,
):
    r, c = iotas()
    rev = (r + c == TILE - 1).astype(f4).astype(bf)
    late = c >= r
    early = c <= r
    left = lax.broadcasted_iota(jnp.int32, (CH, TILE), 1) < 64
    upper = lax.broadcasted_iota(jnp.int32, (TILE, CH), 0) < 64
    step = pl.program_id(0)
    last = pl.num_programs(0) - 1

    def head(x, h):
        zero = jnp.zeros(x.shape, x.dtype)
        return jnp.where(left, x, zero) if h == 0 else jnp.where(left, zero, x)

    def chunk_of(i):
        return pl.ds(al(i * CH, CH), CH)

    def tile_of(i):
        return pl.ds(al(i * TILE, TILE), TILE)

    def clear(*refs):
        for ref in refs:
            ref[...] = jnp.zeros(ref.shape, ref.dtype)

    def prepare(qt, kt):
        da = (da_ref[...].astype(f4) * inv_ref[...]).astype(bf)
        for t in range(LEN // TILE):
            rows = slice(t * TILE, (t + 1) * TILE)
            vr[rows, :] = dot(rev, v_ref[rows, :]).astype(bf)
            turned = dot(rev, k_ref[rows, :]).astype(bf)
            kr[rows, :] = turned
            kt[:, rows] = turned.T
            qt[:, rows] = q_ref[rows, :].T
            dat[:, rows] = da[rows].T

    def turn_table():
        for t in range(NEAR * CH // TILE):
            rows = slice(t * TILE, (t + 1) * TILE)
            rkr[rows, :] = dot(rev, rk_ref[rows, :]).astype(bf)

    def pads(ic, lo, hi, ws, wt):
        zero = jnp.zeros((CH, CH), bf)
        for h in range(2):
            for ref in (ws, wt):
                ref[h, chunk_of(ic), chunk_of(lo)] = zero
                ref[h, chunk_of(ic), chunk_of(hi + 1)] = zero

    def open_grad(ic, dq):
        rows = chunk_of(ic)
        x = att_ref[rows, :] * da_ref[rows, :].astype(f4)
        pair = inv_ref[rows, :]
        turned = pltpu.roll(pair, 64, 1)
        for h in range(2):
            total = jnp.sum(head(x, h), axis=1, keepdims=True)
            corr[h] = jnp.broadcast_to(total, (CH, TILE))
            norm[h] = jnp.where(left, pair, turned) if h == 0 else jnp.where(left, turned, pair)
        dq[rows, :] = jnp.zeros((CH, TILE), f4)

    def both_heads(first, second):
        return jnp.where(left, first, second)

    def grad_start(ic, jc):
        rows, cols = chunk_of(ic), chunk_of(jc)
        da = da_ref[rows, :]
        values = vr[cols, :]
        return [dot(head(da, h), values, NT) for h in range(2)]

    def grad_scores(ic, jc, dps):
        rows, cols = chunk_of(ic), chunk_of(jc)
        parts = []
        for h in range(2):
            p = p_ref[h, rows, cols]
            d, iv = corr[h], norm[h]
            parts.append(
                [
                    (
                        p[:, t * TILE : (t + 1) * TILE].astype(f4)
                        * ((dps[h][:, t * TILE : (t + 1) * TILE] - d) * iv)
                    ).astype(bf)
                    for t in range(2)
                ]
            )
        return parts

    def grad_skew(ic, jc, parts, ws, wt):
        for h in range(2):
            for t in range(2):
                for s in range(2):
                    sr = slice(s * TILE, (s + 1) * TILE)
                    ws[h, tile_of(2 * ic + s), tile_of(2 * jc + 2 + t)] = pltpu.roll(
                        parts[h][t][sr], 0, 1, stride=1, stride_axis=0
                    )
                    wt[h, tile_of(2 * jc + t), tile_of(2 * ic + 2 + s)] = pltpu.roll(
                        parts[h][t][sr].T, 1, 1, stride=1, stride_axis=0
                    )

    def grad_values(ic, jc, dvt):
        rows, cols = chunk_of(ic), chunk_of(jc)
        for h in range(2):
            half = slice(h * 64, (h + 1) * 64)
            dvt[half, cols] += dot(dat[half, rows], p_ref[h, rows, cols])

    def grad_out(ic, jc, parts, dq, dkt, qt):
        rows, cols = chunk_of(ic), chunk_of(jc)
        keys = kr[cols, :]
        whole = [jnp.concatenate(parts[h], axis=1) for h in range(2)]
        dq[rows, :] += both_heads(dot(whole[0], keys), dot(whole[1], keys))
        for h in range(2):
            half = slice(h * 64, (h + 1) * 64)
            dkt[half, cols] += dot(qt[half, rows], whole[h])

    def fold(ic, slot, first, ws, wt, qt, kt, gk, gq):
        rows = chunk_of(ic)
        w = chunk_of(jnp.clip(slot + 3 - ic, 1, NEAR) - 1)
        for ref, mask, table, out, turned, g in (
            (ws, late, rkr, dq2, qt, gk),
            (wt, early, rq_ref, dk2, kt, gq),
        ):
            rels = table[w, :]
            outs = []
            for h in range(2):
                band = []
                for s in range(2):
                    line = []
                    for b in range(2):
                        spot = 2 * slot + s + b
                        x = ref[h, tile_of(2 * ic + s), tile_of(spot)]
                        y = ref[h, tile_of(2 * ic + s), tile_of(spot + 1)]
                        line.append(jnp.where(mask, x, y))
                    band.append(jnp.concatenate(line, axis=1))
                band = jnp.concatenate(band, axis=0)
                outs.append(dot(band, rels))
                half = slice(h * 64, (h + 1) * 64)
                g[half, w] += dot(turned[half, rows], band)
            if first:
                out[rows, :] = both_heads(*outs)
            else:
                out[rows, :] += both_heads(*outs)

    def close(ic, dq, dkt, dvt):
        rows = chunk_of(ic)
        dqk_ref[rows, :TILE] = ((dq[rows, :] + dq2[rows, :]) * SCALE).astype(bf)
        for t in range(2):
            tr = tile_of(2 * ic + t)
            x = ((dkt[:, tr].T + dk2[tr, :]) * SCALE).astype(bf)
            dqk_ref[tr, TILE:] = dot(rev, x).astype(bf)
            dv_ref[tr, :] = dot(rev, dvt[:, tr].T.astype(bf)).astype(bf)
        dkt[:, rows] = jnp.zeros((TILE, CH), f4)
        dvt[:, rows] = jnp.zeros((TILE, CH), f4)

    def flush(gk, gq):
        g_ref[:TILE, :] = (gq[...] * SCALE).astype(bf)
        for t in range(NEAR * CH // TILE):
            cols = slice(t * TILE, (t + 1) * TILE)
            g_ref[TILE:, cols] = dot((gk[:, cols] * SCALE).astype(bf), rev).astype(bf)

    def sweep(before, body, idle):
        def chunk(ic, _):
            lo = b_ref[2 * NCH + ic]
            hi = b_ref[3 * NCH + ic]

            @pl.when(hi > lo)
            def _():
                before(ic, lo, hi)

            @pl.when(hi <= lo)
            def _():
                idle(ic)

            def block(jc, _):
                body(ic, jc)
                return 0

            lax.fori_loop(lo, hi, block, 0)
            return 0

        lax.fori_loop(0, NCH, chunk, 0)

    def no_fold(ic):
        dq2[chunk_of(ic), :] = jnp.zeros((CH, TILE), f4)
        dk2[chunk_of(ic), :] = jnp.zeros((CH, TILE), f4)

    def no_grad(ic, dq):
        dq[chunk_of(ic), :] = jnp.zeros((CH, TILE), f4)

    def fused(new, old):
        ws, wt, dq, dkt, dvt, qt, kt, gk_next, gq_next = new
        ws_, wt_, dq_, dkt_, dvt_, qt_, kt_, gk, gq = old
        prepare(qt, kt)
        turn_table()

        def before(ic, lo, hi):
            @pl.when(step < 2)
            def _():
                pads(ic, lo, hi, ws, wt)

            fold(ic, lo, True, ws_, wt_, qt_, kt_, gk, gq)
            open_grad(ic, dq)

        def body(ic, jc):
            dps = grad_start(ic, jc)
            fold(ic, jc + 1, False, ws_, wt_, qt_, kt_, gk, gq)
            grad_values(ic, jc, dvt)
            parts = grad_scores(ic, jc, dps)
            grad_skew(ic, jc, parts, ws, wt)
            grad_out(ic, jc, parts, dq, dkt, qt)

        def idle(ic):
            no_fold(ic)
            no_grad(ic, dq)

        sweep(before, body, idle)

        def finish(ic, _):
            close(ic, dq_, dkt_, dvt_)
            return 0

        lax.fori_loop(0, NCH, finish, 0)
        flush(gk, gq)
        clear(gk, gq)

    set0 = (ws0, wt0, dq0, dkt0, dvt0, qt0, kt0, gk0, gq0)
    set1 = (ws1, wt1, dq1, dkt1, dvt1, qt1, kt1, gk1, gq1)

    @pl.when(step == 0)
    def _():
        clear(dkt0, dkt1, dvt0, dvt1, gk0, gk1, gq0, gq1)
        prepare(qt0, kt0)

        def before(ic, lo, hi):
            pads(ic, lo, hi, ws0, wt0)
            open_grad(ic, dq0)

        def body(ic, jc):
            parts = grad_scores(ic, jc, grad_start(ic, jc))
            grad_values(ic, jc, dvt0)
            grad_skew(ic, jc, parts, ws0, wt0)
            grad_out(ic, jc, parts, dq0, dkt0, qt0)

        sweep(before, body, lambda ic: no_grad(ic, dq0))

    @pl.when((step > 0) & (step < last) & (step % 2 == 1))
    def _():
        fused(set1, set0)

    @pl.when((step > 0) & (step < last) & (step % 2 == 0))
    def _():
        fused(set0, set1)

    @pl.when(step == last)
    def _():
        turn_table()
        sweep(
            lambda ic, lo, hi: fold(ic, lo, True, ws1, wt1, qt1, kt1, gk1, gq1),
            lambda ic, jc: fold(ic, jc + 1, False, ws1, wt1, qt1, kt1, gk1, gq1),
            no_fold,
        )

        def finish(ic, _):
            close(ic, dq1, dkt1, dvt1)
            return 0

        lax.fori_loop(0, NCH, finish, 0)
        flush(gk1, gq1)


def attend_backward(bounds, both, v, da, att, inv, spread, p):
    pairs = v.shape[1] // TILE

    def col(n, lag, at=0, every=1):
        return pl.BlockSpec(
            (n, TILE), lambda s, *_: (0, at + every * jnp.clip(s - lag, 0, pairs - 1))
        )

    def out(at):
        return lambda s, *_: (jnp.clip(s - 1, 0, pairs - 1), 0)[:: 1 - 2 * at]

    def twice(shape, dtype):
        return [pltpu.VMEM(shape, dtype)] * 2

    return pl.pallas_call(
        bwd_kernel,
        grid_spec=pltpu.PrefetchScalarGridSpec(
            num_scalar_prefetch=1,
            grid=(pairs + 1,),
            in_specs=[
                col(LEN, 0, 0, 2),
                col(LEN, 0, 1, 2),
                col(LEN, 0),
                col(LEN, 0),
                col(LEN, 0),
                col(LEN, 0),
                pl.BlockSpec((2, LEN, LEN), lambda s, *_: (jnp.minimum(s, pairs - 1), 0, 0)),
                col(NEAR * CH, 1, 1, 2),
                col(NEAR * CH, 1, 0, 2),
            ],
            out_specs=[
                pl.BlockSpec((LEN, 2 * TILE), out(1)),
                col(LEN, 1),
                pl.BlockSpec((2 * TILE, NEAR * CH), out(0)),
            ],
            scratch_shapes=twice((2, LEN, LEN + 2 * CH), bf)
            + twice((2, LEN, LEN + 2 * CH), bf)
            + twice((LEN, TILE), f4)
            + twice((TILE, LEN), f4)
            + twice((TILE, LEN), f4)
            + twice((TILE, LEN), bf)
            + twice((TILE, LEN), bf)
            + twice((TILE, NEAR * CH), f4)
            + twice((TILE, NEAR * CH), f4)
            + [pltpu.VMEM((TILE, LEN), bf)]
            + [pltpu.VMEM((LEN, TILE), bf)] * 2
            + [pltpu.VMEM((NEAR * CH, TILE), bf)]
            + [pltpu.VMEM((LEN, TILE), f4)] * 2
            + [pltpu.VMEM((2, CH, TILE), f4)] * 2,
        ),
        out_shape=[
            jax.ShapeDtypeStruct(both.shape, bf),
            jax.ShapeDtypeStruct(v.shape, bf),
            jax.ShapeDtypeStruct((both.shape[1], NEAR * CH), bf),
        ],
        compiler_params=pltpu.CompilerParams(vmem_limit_bytes=60 << 20),
        name="attend_backward",
    )(bounds, both, both, v, da, att, inv, p, spread, spread)


def gelu_pair(u):
    size = jnp.abs(u)
    bell = jnp.exp2(u * u * (-0.5 * math.log2(math.e)))
    t = 1.0 / (1.0 + (0.3275911 / math.sqrt(2.0)) * size)
    poly = 0.5 * 1.061405429
    for c in (-1.453152027, 1.421413741, -0.284496736, 0.254829592):
        poly = poly * t + 0.5 * c
    tail = poly * t * bell
    phi = jnp.where(u < 0.0, tail, 1.0 - tail)
    return u * phi, phi + u * bell * (1.0 / math.sqrt(2.0 * math.pi))


def middle_kernel(
    hid_ref, att_ref, wo_ref, we_ref, wc_ref, vec_ref, mask_ref, cot_ref,
    out_ref, dfirst_ref, datt_ref, grad_ref,
    pre, slope, acc, norm_, act, dexp, low, dtwo, dbranch, attended, turned, sums,
):
    step = pl.program_id(0)
    blocks = act.shape[0] // TOK
    parts = act.shape[1] // low.shape[1]

    @pl.when(step < blocks)
    def _():
        rows = pl.ds(al(step * TOK, TOK), TOK)
        views = [ref.at[rows] for ref in (act, dexp, low, dtwo, dbranch, attended)]
        token_block(
            step, hid_ref, att_ref, wo_ref, we_ref, wc_ref, vec_ref, mask_ref, cot_ref,
            out_ref, dfirst_ref, datt_ref, pre, slope, acc, norm_, sums, *views,
        )

    @pl.when(step >= blocks)
    def _():
        weight_block(
            step - blocks, parts, act, dexp, low, dtwo, dbranch, attended, turned, sums, grad_ref
        )


def token_block(
    step, hid_ref, att_ref, wo_ref, we_ref, wc_ref, vec_ref, mask_ref, cot_ref,
    out_ref, dfirst_ref, datt_ref, pre, slope, acc, norm_, sums,
    act_ref, dexp_ref, low_ref, dtwo_ref, dbranch_ref, attb_ref,
):
    width = hid_ref.shape[1]
    chunks = we_ref.shape[1] // FCH
    vectors = vec_ref[...].astype(f4).T
    gain_one = vectors[0:1, :]
    shift_one = vectors[1:2, :]
    gain_two = vectors[2:3, :]
    shift_two = vectors[3:4, :]
    inv = 1.0 / width
    attb_ref[...] = att_ref[...].astype(bf)
    first = hid_ref[...].astype(f4) + dot(attb_ref[...], wo_ref[...])
    cen = first - jnp.sum(first, axis=1, keepdims=True) * inv
    rstd_one = lax.rsqrt(jnp.sum(cen * cen, axis=1, keepdims=True) * inv + NORM_EPS)
    n_one = cen * rstd_one
    norm_[...] = n_one
    normed = n_one * gain_one + shift_one
    low_ref[...] = normed.astype(bf)
    acc[...] = jnp.zeros(acc.shape, f4)

    def cols(c):
        return slice(c * FCH, (c + 1) * FCH)

    def expand(c):
        pre[c % 2] = dot(low_ref[...], we_ref[:, cols(c)])

    def bend(c):
        value, grad = gelu_pair(pre[c % 2])
        act_ref[:, cols(c)] = value.astype(bf)
        slope[:, cols(c)] = grad.astype(bf)

    def contract(c):
        acc[...] += dot(act_ref[:, cols(c)], wc_ref[:, cols(c)])

    expand(0)
    expand(1)
    bend(0)

    def steady(c, _):
        expand(c + 1)
        bend(c)
        contract(c - 1)
        return 0

    for c in range(1, chunks - 1):
        steady(c, 0)
    bend(chunks - 1)
    contract(chunks - 2)
    contract(chunks - 1)
    branch = acc[...]
    turned = [
        jnp.broadcast_to(mask_ref[:, t : t + TILE].astype(f4), (TILE, TILE)).T
        for t in range(0, TOK, TILE)
    ]
    mask = jnp.concatenate(turned, axis=0)[:, 0:1]
    normed = norm_[...] * gain_one + shift_one
    second = normed + branch
    row_res = jnp.sum(mask * second * second, axis=0, keepdims=True)
    row_sub = jnp.sum(mask * branch * branch, axis=0, keepdims=True)
    cen = second - jnp.sum(second, axis=1, keepdims=True) * inv
    rstd = lax.rsqrt(jnp.sum(cen * cen, axis=1, keepdims=True) * inv + NORM_EPS)
    n_two = cen * rstd
    out_ref[...] = (n_two * gain_two + shift_two).astype(bf)
    up = cot_ref[...].astype(f4) * mask
    row_g2 = jnp.sum(up * n_two, axis=0, keepdims=True)
    row_s2 = jnp.sum(up, axis=0, keepdims=True)
    g = up * gain_two
    d_second = (
        g
        - jnp.sum(g, axis=1, keepdims=True) * inv
        - n_two * (jnp.sum(g * n_two, axis=1, keepdims=True) * inv)
    ) * rstd
    dtwo_ref[...] = d_second.astype(bf)
    acc[...] = d_second

    def back(c):
        grad = dot(dtwo_ref[...], wc_ref[:, cols(c)], NT) * slope[:, cols(c)].astype(f4)
        dexp_ref[:, cols(c)] = grad.astype(bf)

    def into(c):
        acc[...] += dot(dexp_ref[:, cols(c)], we_ref[:, cols(c)], NT)

    back(0)

    def steady_back(c, _):
        back(c)
        into(c - 1)
        return 0

    for c in range(1, chunks):
        steady_back(c, 0)
    into(chunks - 1)
    up = acc[...]
    n_one = norm_[...]
    row_g1 = jnp.sum(up * n_one, axis=0, keepdims=True)
    row_s1 = jnp.sum(up, axis=0, keepdims=True)
    g = up * gain_one
    d_first = (
        g
        - jnp.sum(g, axis=1, keepdims=True) * inv
        - n_one * (jnp.sum(g * n_one, axis=1, keepdims=True) * inv)
    ) * rstd_one
    dfirst_ref[...] = d_first
    low = d_first.astype(bf)
    dbranch_ref[...] = low
    datt_ref[...] = dot(low, wo_ref[...], NT).astype(bf)
    rows = jnp.concatenate(
        [row_g1, row_s1, row_g2, row_s2, row_res, row_sub, jnp.zeros((2, width), f4)], axis=0
    )

    @pl.when(step == 0)
    def _():
        sums[...] = rows

    @pl.when(step > 0)
    def _():
        sums[...] += rows


def weight_block(
    step, parts, act, dexp, low, dtwo, dbranch, attended, turned, sums, out_ref
):
    width = low.shape[1]

    @pl.when(step == 0)
    def _():
        turned[...] = low[...].T

    @pl.when(step < parts)
    def _():
        cols = pl.ds(al(step * width, width), width)
        out_ref[...] = dot(turned[...], dexp[:, cols]).astype(bf)

    @pl.when((step >= parts) & (step < 2 * parts))
    def _():
        cols = pl.ds(al((step - parts) * width, width), width)
        out_ref[...] = dot(act[:, cols].T, dtwo[...]).astype(bf)

    @pl.when(step == 2 * parts)
    def _():
        out_ref[...] = dot(attended[...].T, dbranch[...]).astype(bf)

    @pl.when(step == 2 * parts + 1)
    def _():
        rows = sums[...]
        total = jnp.broadcast_to(jnp.sum(rows[4:6], axis=1, keepdims=True), (2, width))
        full = jnp.concatenate([rows[:4], total, jnp.zeros((TILE - 6, width), f4)], axis=0)
        out_ref[:, :TILE] = full.T.astype(bf)


def middle(hidden, attended, weights, wide, mask, cotangent):
    tokens, width = hidden.shape
    blocks = tokens // TOK
    parts = wide // width
    tok = lambda n: pl.BlockSpec((TOK, n), lambda i: (jnp.minimum(i, blocks - 1), 0))
    once = lambda n, at: pl.BlockSpec(
        (width, n), lambda i: (0, at // n), pipeline_mode=pl.Buffered(1)
    )
    shape = lambda n, dtype: jax.ShapeDtypeStruct((tokens, n), dtype)
    whole = lambda n: pltpu.VMEM((tokens, n), bf)
    return pl.pallas_call(
        middle_kernel,
        grid=(blocks + 2 * parts + 2,),
        in_specs=[
            tok(width),
            tok(width),
            once(width, 2 * wide),
            once(wide, 0),
            once(wide, wide),
            once(TILE, 2 * wide + width),
            pl.BlockSpec((1, TOK), lambda i: (0, jnp.minimum(i, blocks - 1))),
            tok(width),
        ],
        out_specs=[
            tok(width),
            tok(width),
            tok(width),
            pl.BlockSpec((width, width), lambda i: (0, jnp.maximum(i - blocks, 0))),
        ],
        out_shape=[
            shape(width, bf),
            shape(width, f4),
            shape(width, bf),
            jax.ShapeDtypeStruct((width, 2 * wide + width + TILE), bf),
        ],
        scratch_shapes=[
            pltpu.VMEM((2, TOK, FCH), f4),
            pltpu.VMEM((TOK, wide), bf),
            pltpu.VMEM((TOK, width), f4),
            pltpu.VMEM((TOK, width), f4),
            whole(wide),
            whole(wide),
            whole(width),
            whole(width),
            whole(width),
            whole(width),
            pltpu.VMEM((width, tokens), bf),
            pltpu.VMEM((8, width), f4),
        ],
        compiler_params=pltpu.CompilerParams(vmem_limit_bytes=60 << 20),
        name="middle",
    )(hidden, attended, weights, weights, weights, weights, mask, cotangent)


def lane_pieces(size, count, parts, per, forward):
    found = [[] for _ in range(size // TILE)]
    for device in range(count):
        for part in range(parts):
            source = (device * parts + part) * per
            target = part * count * per + device * per
            if not forward:
                source, target = target, source
            done = 0
            while done < per:
                at, to = source + done, target + done
                span = min(per - done, TILE - at % TILE, TILE - to % TILE)
                found[to // TILE].append((at // TILE, at % TILE, to % TILE, span))
                done += span
    return found


def permute_lanes(load, store, rows, pieces):
    lane = lax.broadcasted_iota(jnp.int32, (rows, TILE), 1)
    for block, group in enumerate(pieces):
        total = jnp.zeros((rows, TILE), f4)
        for at, offset, spot, span in group:
            moved = load(at)
            if spot != offset:
                moved = pltpu.roll(moved, (spot - offset) % TILE, 1)
            total = jnp.where((lane >= spot) & (lane < spot + span), moved, total)
        store(block, total)


def lanes(block):
    return slice(block * TILE, (block + 1) * TILE)


def pack_kernel(
    count, query_ref, key_ref, table_ref, expand_ref, contract_ref, output_ref,
    small_ref, first_ref, out_ref,
):
    per, wide = expand_ref.shape
    width = output_ref.shape[1]
    parts = wide // width
    half = table_ref.shape[0] // 2
    table = table_ref[...].astype(f4)
    table = jnp.concatenate([table[:half], table[half:]], axis=1)
    for block in range(width // TILE):
        for spot, ref in enumerate((query_ref, key_ref)):
            at = lanes(2 * block + spot)
            rows = jnp.concatenate([ref[:, lanes(block)].astype(f4), table[:, at]], axis=0)
            first_ref[:, at] = rows.astype(bf)

    def store(block, value):
        out_ref[:, lanes(block)] = value.astype(bf)

    permute_lanes(
        lambda at: expand_ref[:, lanes(at)].astype(f4),
        store,
        per,
        lane_pieces(wide, count, parts, per, True),
    )
    rows = contract_ref[...].astype(f4)
    for part in range(parts):
        at = wide + part * width
        out_ref[:, at : at + width] = rows[part * per : (part + 1) * per].astype(bf)
    out_ref[:, 2 * wide : 2 * wide + width] = output_ref[...]
    out_ref[:, 2 * wide + width :] = small_ref[...]


def pack_weights(count, query, key, table, expand, contract, output, small):
    per, wide = expand.shape
    width = output.shape[1]
    shape = lambda a, b: jax.ShapeDtypeStruct((a, b), bf)
    return pl.pallas_call(
        partial(pack_kernel, count),
        out_shape=[
            shape(per + table.shape[0] // 2, 2 * width),
            shape(per, 2 * wide + width + TILE),
        ],
        name="pack_weights",
    )(query, key, table, expand, contract, output, small)


def finish_kernel(count, cells, own_ref, expand_ref, contract_ref, output_ref, *rest):
    per, wide = expand_ref.shape
    width = output_ref.shape[1]
    parts = wide // width

    def store(block, value):
        expand_ref[:, lanes(block)] = value

    permute_lanes(
        lambda at: own_ref[:, lanes(at)].astype(f4),
        store,
        per,
        lane_pieces(wide, count, parts, per, False),
    )
    for part in range(parts):
        at = wide + part * width
        contract_ref[part * per : (part + 1) * per, :] = own_ref[:, at : at + width].astype(f4)
    output_ref[...] = own_ref[:, 2 * wide : 2 * wide + width].astype(f4)
    turned = own_ref[:, 2 * wide + width :].astype(f4).T
    for number, ref in enumerate(rest[:4]):
        ref[...] = turned[number : number + 1, :]
    for number, ref in enumerate(rest[4:]):
        ref[...] = jnp.sqrt(turned[4 + number : 5 + number, :1] * (1.0 / cells))


def finish_grads(count, cells, own, wide, width):
    per = own.shape[0]
    shape = lambda a, b: jax.ShapeDtypeStruct((a, b), f4)
    return pl.pallas_call(
        partial(finish_kernel, count, cells),
        out_shape=[
            shape(per, wide),
            shape(per * (wide // width), width),
            shape(per, width),
            *[shape(1, per)] * 4,
            *[shape(1, 1)] * 2,
        ],
        name="finish_grads",
    )(own)


def digits(count):
    found = [(1, 2)]
    stride = 2
    while stride < count:
        radix = 4 if count // stride >= 4 else 2
        found.append((stride, radix))
        stride *= radix
    return found


def place(relative, count):
    spot = relative * 0
    for stride, radix in digits(count):
        spot = spot * radix + ((relative >> (stride.bit_length() - 1)) & (radix - 1))
    return spot


def mixing(size, count, me):
    per = size // count
    row = np.arange(size)
    target = place(jnp.asarray(row // per, jnp.int32) ^ me, count) * per + (row % per)
    spots = lax.broadcasted_iota(jnp.int32, (size, size), 1)
    return (target[:, None] == spots).astype(bf)


def near_index():
    index = bucket_index(LEN - np.arange(2 * LEN), BUCKETS).reshape(-1, CH)
    assert (index[:2] == index[0, 0]).all() and (index[-2:] == index[-1, -1]).all()
    return index[1:-1].reshape(-1)


def offset_rows(count, me):
    index = near_index()
    size = 2 * BUCKETS
    per = size // count
    target = place(jnp.asarray(index // per, jnp.int32) ^ me, count) * per + (index % per)
    spots = lax.broadcasted_iota(jnp.int32, (index.shape[0], size), 1)
    return (target[:, None] == spots).astype(bf)


def swap(value, offset, count):
    return lax.ppermute(value, "fsdp", [(i, i ^ offset) for i in range(count)])


def together(values):
    return list(lax.optimization_barrier(tuple(values)))


def gather_pair(first, second, count, beside, work):
    middle = digits(count)[1:]
    one, two = first[None], second[None]
    later = None
    for (stride_a, radix_a), (stride_b, radix_b) in zip(middle[::-1], middle):
        got_a = [one]
        got_b = [two]
        for step in range(1, max(radix_a, radix_b)):
            if step < radix_a:
                got_a.append(swap(one, step * stride_a, count))
            if step < radix_b:
                got_b.append(swap(two, step * stride_b, count))
        one, two, *beside = together(
            [jnp.concatenate(got_a, axis=0), jnp.concatenate(got_b, axis=0), *beside]
        )
        if later is None:
            later, beside = beside[0], work(beside[1])
    radices = [radix for _, radix in middle[::-1]]
    two = two.reshape(*radices, *second.shape)
    turn = tuple(range(len(middle)))[::-1]
    two = two.transpose(turn + (len(middle), len(middle) + 1)).reshape(-1, *second.shape)
    return (one, swap(one, 1, count)), (two, swap(two, 1, count)), later, beside


def scatter_pair(first, second, count, beside):
    middle = digits(count)[1:]
    radices = [radix for _, radix in middle]
    shape_a, shape_b = first.shape[1:], second.shape[1:]
    half_a = first.reshape(2, -1, *shape_a)
    half_b = second.reshape(2, -1, *shape_b)
    one, two = together(
        [
            half_a[0].astype(f4) + swap(half_a[1], 1, count).astype(f4),
            half_b[0].astype(f4) + swap(half_b[1], 1, count).astype(f4),
        ]
    )
    one = one.astype(bf).reshape(*radices, *shape_a)
    two = two.astype(bf).reshape(*radices, *shape_b)
    for step, ((stride_a, radix_a), (stride_b, radix_b)) in enumerate(zip(middle, middle[::-1])):
        last = two.ndim - 3
        got_a = []
        got_b = []
        for hop in range(1, max(radix_a, radix_b)):
            if hop < radix_a:
                got_a.append(swap(one[hop], hop * stride_a, count))
            if hop < radix_b:
                got_b.append(
                    swap(lax.index_in_dim(two, hop, last, keepdims=False), hop * stride_b, count)
                )
        sum_a = one[0].astype(f4)
        sum_b = lax.index_in_dim(two, 0, last, keepdims=False).astype(f4)
        if step == 0:
            *got, beside = together(got_a + got_b + [beside])
        else:
            got = together(got_a + got_b)
        for piece in got[: len(got_a)]:
            sum_a = sum_a + piece.astype(f4)
        for piece in got[len(got_a) :]:
            sum_b = sum_b + piece.astype(f4)
        if step == len(middle) - 1:
            return sum_a, sum_b, beside
        one, two = sum_a.astype(bf), sum_b.astype(bf)


def active_chunks(segment, valid):
    rows = segment.reshape(NCH, CH)
    ok = valid.reshape(NCH, CH) > 0
    first = rows[:, 0]
    last = rows[:, -1]
    over = (first[None, :] <= last[:, None]) & (last[None, :] >= first[:, None])
    real = jnp.max(jnp.where(ok, rows, -1), axis=1)
    back = (first[None, :] <= real[:, None]) & (last[None, :] >= first[:, None])
    back = back | back.T
    place_ = jnp.arange(NCH)[None, :]

    def limits(mask):
        lo = jnp.min(jnp.where(mask, place_, NCH), axis=1)
        hi = jnp.max(jnp.where(mask, place_ + 1, 0), axis=1)
        return jnp.where(hi > 0, lo, 0), hi

    return jnp.concatenate(limits(over) + limits(back)).astype(jnp.int32)


def mm(left, right, dims=NN):
    return lax.dot_general(left, right, dims, preferred_element_type=f4)


def shards(
    hidden,
    query_weight,
    key_weight,
    value_weight,
    output_weight,
    relative_table,
    first_gain,
    first_shift,
    expand_weight,
    contract_weight,
    second_gain,
    second_shift,
    segment_ids,
    valid,
    cotangent,
):
    count = lax.axis_size("fsdp")
    me = lax.axis_index("fsdp")
    width = hidden.shape[1]
    wide = expand_weight.shape[1]
    per = query_weight.shape[0]
    per_t = relative_table.shape[0]
    per_c = contract_weight.shape[0]
    parts = wide // width

    small = jnp.stack([first_gain, first_shift, second_gain, second_shift], axis=1)
    small = jnp.pad(small, ((0, 0), (0, TILE - 4)))
    first, rest = pack_weights(
        count,
        query_weight,
        key_weight,
        relative_table,
        expand_weight,
        contract_weight,
        output_weight,
        small,
    )

    def aside(number):
        mix = mixing(width, count, number)
        return [
            mix,
            mm(hidden, mix).astype(bf),
            offset_rows(count, number),
            active_chunks(segment_ids, valid),
        ]

    pair_a, pair_b, rest, (mix, hidden_mixed, onehot, bounds) = gather_pair(
        first, value_weight, count, [rest, me], aside
    )
    query_key = jnp.concatenate([x[:, :per] for x in pair_a], axis=0)
    query_key = query_key.reshape(count * per, 2 * width)
    value_full = jnp.concatenate(pair_b, axis=0).reshape(count * per, width)
    table = [
        jnp.concatenate([x[:, per:, :width], x[:, per:, width:]], axis=1) for x in pair_a
    ]
    table = jnp.concatenate(table, axis=0).reshape(count * per_t, width)
    weights = lax.all_gather(rest, "fsdp", axis=0, tiled=True)

    table_mixed = mm(table, mix).astype(bf)
    both_rows = mm(hidden_mixed, query_key).astype(bf)
    value_rows = mm(hidden_mixed, value_full).astype(bf)
    (position,) = together([mm(table_mixed, query_key).astype(bf)])
    spread_rows = mm(onehot, position).astype(bf)
    attended_wide, inverse, probs = attend_forward(
        bounds, both_rows, value_rows, spread_rows, segment_ids[None, :]
    )
    result, d_first, attended_gradient, grads = middle(
        hidden, attended_wide, weights, wide, valid[None, :], cotangent
    )
    owned = lax.psum_scatter(grads, "fsdp", scatter_dimension=0, tiled=True)
    both_low, value_low, offset_grad = attend_backward(
        bounds,
        both_rows,
        value_rows,
        attended_gradient,
        attended_wide,
        inverse,
        spread_rows,
        probs,
    )
    position_low = mm(offset_grad, onehot).astype(bf)
    grad_pack = mm(hidden_mixed, both_low, ROWS_FIRST) + mm(
        table_mixed, position_low, (((0,), (1,)), ((), ()))
    )
    grad_pack = grad_pack.astype(bf).reshape(count, per, 2 * width)
    grad_value = mm(hidden_mixed, value_low, ROWS_FIRST)
    grad_table = mm(position_low, query_key, (((0,), (1,)), ((), ())))
    grad_table = mm(grad_table.astype(bf), mix, NT).astype(bf)
    grad_value = jnp.concatenate(
        [
            grad_value.astype(bf).reshape(count, per, width),
            grad_table.reshape(count, per_t, width),
        ],
        axis=1,
    )
    d_input = mm(both_low, query_key, NT) + mm(value_low, value_full, NT)
    own_pack, own_value, d_input = scatter_pair(grad_pack, grad_value, count, d_input.astype(bf))
    d_input = d_first + mm(d_input, mix, NT)
    cells = float(hidden.shape[0] * count * width)
    expand_owned, contract_owned, output_owned, *last = finish_grads(
        count, cells, owned, wide, width
    )
    own_pack = own_pack.reshape(per, -1, 2, TILE)
    return (
        result,
        d_input.astype(bf),
        own_pack[:, :, 0].reshape(per, width),
        own_pack[:, :, 1].reshape(per, width),
        own_value[:per],
        output_owned,
        own_value[per:],
        last[0].reshape(per),
        last[1].reshape(per),
        expand_owned,
        contract_owned,
        last[2].reshape(per),
        last[3].reshape(per),
        last[4].reshape(()),
        last[5].reshape(()),
    )


def solution(mesh):
    in_specs = (
        P("fsdp", None),
        P("fsdp", None),
        P("fsdp", None),
        P("fsdp", None),
        P("fsdp", None),
        P("fsdp", None),
        P("fsdp"),
        P("fsdp"),
        P("fsdp", None),
        P("fsdp", None),
        P("fsdp"),
        P("fsdp"),
        P("fsdp"),
        P("fsdp"),
        P("fsdp", None),
    )
    out_specs = (
        P("fsdp", None),
        P("fsdp", None),
        P("fsdp", None),
        P("fsdp", None),
        P("fsdp", None),
        P("fsdp", None),
        P("fsdp", None),
        P("fsdp"),
        P("fsdp"),
        P("fsdp", None),
        P("fsdp", None),
        P("fsdp"),
        P("fsdp"),
        P(),
        P(),
    )
    return jax.shard_map(shards, mesh=mesh, in_specs=in_specs, out_specs=out_specs, check_vma=False)
```

```python
from functools import partial
import math

import jax
import jax.numpy as jnp
import numpy as np
from jax import lax
from jax.experimental import pallas as pl
from jax.experimental.pallas import tpu as pltpu
from jax.sharding import PartitionSpec as P

bf = jnp.bfloat16
f4 = jnp.float32
HEADS = 12
BUCKETS = 256
LEN = 1024
TILE = 128
CH = 256
NCH = LEN // CH
SCALE = 1.0 / math.sqrt(192.0)
NORM_EPS = 1e-07
MASKED = -1e30
TOK = 256
NEAR = 6
FCH = 768
ROWS_FIRST = (((0,), (0,)), ((), ()))
ROWS_LAST = (((1,), (1,)), ((), ()))
NT = ROWS_LAST
NN = (((1,), (0,)), ((), ()))


def bucket_index(offsets, buckets):
    middle = buckets // 2
    limit = 2 * buckets
    magnitude = np.abs(offsets)
    inside = (offsets < middle) & (offsets > -middle)
    clipped = np.where(inside, middle - 1, magnitude)
    logged = (
        np.ceil(np.log(clipped / middle) / np.log((limit - 1) / middle) * (middle - 1)) + middle
    )
    bucket = np.where(magnitude <= middle, offsets, (logged * np.sign(offsets)).astype(np.int32))
    return np.clip(bucket + buckets, 0, 2 * buckets - 1).astype(np.int32)


def dot(a,b,dims=NN): return lax.dot_general(a,b,dims,preferred_element_type=f4)
def al(x,m): return pl.multiple_of(x,m)
def iotas():
    r=lax.broadcasted_iota(jnp.int32,(TILE,TILE),0); c=lax.broadcasted_iota(jnp.int32,(TILE,TILE),1)
    return r,c


def fwd_kernel(
    b_ref, qa_ref, ka_ref, rk_ref, rq_ref, qb_ref, kb_ref, v_ref, segr_ref,
    att_ref, inv_ref, p_ref,
    xs0, xs1, ys0, ys1, sc0, sc1, mx0, mx1, top, sm, acc, segb,
):
    r, c = iotas()
    eye = (r == c).astype(f4).astype(bf)
    rev = (r + c == TILE - 1).astype(f4).astype(bf)
    early = (r + c) < TILE
    lane = lax.broadcasted_iota(jnp.int32, (CH, TILE), 1)
    left = lane < 64
    lane_t = lax.broadcasted_iota(jnp.int32, (TILE, TILE), 1)
    left_t = lane_t < 64
    step = pl.program_id(0)
    last = pl.num_programs(0) - 1
    fac = SCALE * math.log2(math.e)

    def head(x, h, mask):
        zero = jnp.zeros(x.shape, bf)
        return jnp.where(mask, x, zero) if h == 0 else jnp.where(mask, zero, x)

    def product(ic, slot, xs, ys):
        rows = pl.ds(al(ic * CH, CH), CH)
        w = pl.ds(al((jnp.clip(slot + 3 - ic, 1, NEAR) - 1) * CH, CH), CH)
        out = pl.ds(al(slot * CH, CH), CH)
        q = qa_ref[rows, :]
        k = ka_ref[rows, :]
        for h in range(2):
            xs[h, rows, out] = dot(head(q, h, left), rk_ref[w, :], NT).astype(bf)
            ys[h, rows, out] = dot(head(k, h, left), rq_ref[w, :], NT).astype(bf)

    def skewed(ref, h, row, spot):
        rr = pl.ds(al(row * TILE, TILE), TILE)
        a = ref[h, rr, pl.ds(al((spot + 2) * TILE, TILE), TILE)]
        b = ref[h, rr, pl.ds(al((spot + 1) * TILE, TILE), TILE)]
        return pltpu.roll(jnp.where(early, a, b), 0, 1, stride=1, stride_axis=0)

    def score(ic, jc, s, xs, ys, sc, mx):
        cols = pl.ds(al(jc * CH, CH), CH)
        segc = segr_ref[:, cols].astype(f4)
        keys = kb_ref[cols, :]
        i = 2 * ic + s
        rows = pl.ds(al(i * TILE, TILE), TILE)
        srow = segb[rows, :]
        q = qb_ref[rows, :]
        for h in range(2):
            turned = [skewed(ys, h, 2 * jc + t, i - t) for t in range(2)]
            lhs = jnp.concatenate([head(q, h, left_t), eye], axis=1)
            rhs = jnp.concatenate([keys, jnp.concatenate(turned, axis=0)], axis=1)
            content = dot(lhs, rhs, NT)
            best = mx[h, rows, :]
            for t in range(2):
                along = skewed(xs, h, i, 2 * jc + t - s).astype(f4)
                ok = srow == segc[:, t * TILE : (t + 1) * TILE]
                val = jnp.where(ok, content[:, t * TILE : (t + 1) * TILE] + along, MASKED)
                sc[h, rows, pl.ds(al(jc * CH + t * TILE, TILE), TILE)] = val
                best = jnp.maximum(best, val)
            mx[h, rows, :] = best

    def mix(ic, jc, h, sc):
        rows = pl.ds(al(ic * CH, CH), CH)
        tot = sm[h]
        peak = top[h]
        for t in range(2):
            cols = pl.ds(al(jc * CH + t * TILE, TILE), TILE)
            e = jnp.exp2((sc[h, rows, cols] - peak) * fac)
            tot = tot + e
            rhs = jnp.concatenate([head(v_ref[cols, :], h, left_t), rev], axis=1)
            res = dot(e.astype(bf), rhs)
            acc[...] += res[:, :TILE]
            p_ref[h, rows, cols] = res[:, TILE:].astype(bf)
        sm[h] = tot

    def open_scores(ic, mx):
        rows = pl.ds(al(ic * CH, CH), CH)
        for h in range(2):
            mx[h, rows, :] = jnp.full((CH, TILE), MASKED, f4)

    def open_mix(ic, mx):
        rows = pl.ds(al(ic * CH, CH), CH)
        for h in range(2):
            peak = jnp.max(mx[h, rows, :], axis=1, keepdims=True)
            top[h] = jnp.broadcast_to(peak, (CH, TILE))
            sm[h] = jnp.zeros((CH, TILE), f4)
        acc[...] = jnp.zeros((CH, TILE), f4)

    def close_mix(ic):
        rows = pl.ds(al(ic * CH, CH), CH)
        inv = [1.0 / jnp.sum(sm[h], axis=1, keepdims=True) for h in range(2)]
        pair = jnp.where(
            left, jnp.broadcast_to(inv[0], (CH, TILE)), jnp.broadcast_to(inv[1], (CH, TILE))
        )
        inv_ref[rows, :] = pair
        att_ref[rows, :] = acc[...] * pair

    def sweep(before, body, after):
        def chunk(ic, _):
            lo = b_ref[ic]
            hi = b_ref[NCH + ic]
            before(ic, lo)

            def block(jc, _):
                body(ic, jc)
                return 0

            lax.fori_loop(lo, hi, block, 0)
            after(ic)
            return 0

        lax.fori_loop(0, NCH, chunk, 0)

    def fused(xs_new, ys_new, xs, ys, sc_new, mx_new, sc, mx):
        def before(ic, lo):
            close_mix(jnp.maximum(ic - 1, 0))
            product(ic, lo, xs_new, ys_new)
            open_scores(ic, mx_new)
            open_mix(ic, mx)

        def body(ic, jc):
            product(ic, jc + 1, xs_new, ys_new)
            for part in range(2):
                mix(ic, jc, part, sc)
                score(ic, jc, part, xs, ys, sc_new, mx_new)

        sweep(before, body, lambda ic: None)
        close_mix(jnp.int32(NCH - 1))

    @pl.when(step == 0)
    def _():
        for t in range(LEN // TILE):
            cols = slice(t * TILE, (t + 1) * TILE)
            row = jnp.broadcast_to(segr_ref[:, cols].astype(f4), (TILE, TILE))
            segb[cols, :] = row.T
        sweep(
            lambda ic, lo: product(ic, lo, xs0, ys0),
            lambda ic, jc: product(ic, jc + 1, xs0, ys0),
            lambda ic: None,
        )

    @pl.when((step > 0) & (step < last) & (step % 2 == 1))
    def _():
        fused(xs1, ys1, xs0, ys0, sc1, mx1, sc0, mx0)

    @pl.when((step > 0) & (step < last) & (step % 2 == 0))
    def _():
        fused(xs0, ys0, xs1, ys1, sc0, mx0, sc1, mx1)

    @pl.when(step == last)
    def _():
        def body(ic, jc):
            mix(ic, jc, 0, sc0)
            mix(ic, jc, 1, sc0)

        sweep(lambda ic, lo: open_mix(ic, mx0), body, close_mix)


def attend_forward(bounds, both, v, spread, segr):
    pairs = v.shape[1] // TILE

    def col(n, lag, at=0, every=2):
        return pl.BlockSpec(
            (n, TILE), lambda s, *_: (0, at + every * jnp.clip(s - lag, 0, pairs - 1))
        )

    def wide(lag):
        return pl.BlockSpec((2, LEN, LEN), lambda s, *_: (jnp.clip(s - lag, 0, pairs - 1), 0, 0))

    window = pltpu.VMEM((2, LEN, LEN + CH), bf)
    return pl.pallas_call(
        fwd_kernel,
        grid_spec=pltpu.PrefetchScalarGridSpec(
            num_scalar_prefetch=1,
            grid=(pairs + 2,),
            in_specs=[
                col(LEN, 0),
                col(LEN, 0, 1),
                col(NEAR * CH, 0, 1),
                col(NEAR * CH, 0),
                col(LEN, 1),
                col(LEN, 1, 1),
                col(LEN, 2, 0, 1),
                pl.BlockSpec((1, LEN), lambda s, *_: (0, 0)),
            ],
            out_specs=[col(LEN, 2, 0, 1), col(LEN, 2, 0, 1), wide(2)],
            scratch_shapes=[window] * 4
            + [pltpu.VMEM((2, LEN, LEN), f4)] * 2
            + [pltpu.VMEM((2, LEN, TILE), f4)] * 2
            + [pltpu.VMEM((2, CH, TILE), f4)] * 2
            + [pltpu.VMEM((CH, TILE), f4)]
            + [pltpu.VMEM((LEN, TILE), f4)],
        ),
        out_shape=[
            jax.ShapeDtypeStruct(v.shape, f4),
            jax.ShapeDtypeStruct(v.shape, f4),
            jax.ShapeDtypeStruct((2 * pairs, LEN, LEN), bf),
        ],
        compiler_params=pltpu.CompilerParams(vmem_limit_bytes=60 << 20),
        name="attend_forward",
    )(bounds, both, both, spread, spread, both, both, v, segr)


def bwd_kernel(
    b_ref, q_ref, k_ref, v_ref, da_ref, att_ref, inv_ref, p_ref, rk_ref, rq_ref,
    dqk_ref, dv_ref, g_ref,
    ws0, ws1, wt0, wt1, dq0, dq1, dkt0, dkt1, dvt0, dvt1, qt0, qt1, kt0, kt1,
    gk0, gk1, gq0, gq1, dat, vr, kr, rkr, dq2, dk2, corr, norm,
):
    r, c = iotas()
    rev = (r + c == TILE - 1).astype(f4).astype(bf)
    late = c >= r
    early = c <= r
    left = lax.broadcasted_iota(jnp.int32, (CH, TILE), 1) < 64
    upper = lax.broadcasted_iota(jnp.int32, (TILE, CH), 0) < 64
    step = pl.program_id(0)
    last = pl.num_programs(0) - 1

    def head(x, h):
        zero = jnp.zeros(x.shape, x.dtype)
        return jnp.where(left, x, zero) if h == 0 else jnp.where(left, zero, x)

    def chunk_of(i):
        return pl.ds(al(i * CH, CH), CH)

    def tile_of(i):
        return pl.ds(al(i * TILE, TILE), TILE)

    def clear(*refs):
        for ref in refs:
            ref[...] = jnp.zeros(ref.shape, ref.dtype)

    def prepare(qt, kt):
        da = (da_ref[...].astype(f4) * inv_ref[...]).astype(bf)
        for t in range(LEN // TILE):
            rows = slice(t * TILE, (t + 1) * TILE)
            vr[rows, :] = dot(rev, v_ref[rows, :]).astype(bf)
            turned = dot(rev, k_ref[rows, :]).astype(bf)
            kr[rows, :] = turned
            kt[:, rows] = turned.T
            qt[:, rows] = q_ref[rows, :].T
            dat[:, rows] = da[rows].T

    def turn_table():
        for t in range(NEAR * CH // TILE):
            rows = slice(t * TILE, (t + 1) * TILE)
            rkr[rows, :] = dot(rev, rk_ref[rows, :]).astype(bf)

    def pads(ic, lo, hi, ws, wt):
        zero = jnp.zeros((CH, CH), bf)
        for h in range(2):
            for ref in (ws, wt):
                ref[h, chunk_of(ic), chunk_of(lo)] = zero
                ref[h, chunk_of(ic), chunk_of(hi + 1)] = zero

    def open_grad(ic, dq):
        rows = chunk_of(ic)
        x = att_ref[rows, :] * da_ref[rows, :].astype(f4)
        pair = inv_ref[rows, :]
        turned = pltpu.roll(pair, 64, 1)
        for h in range(2):
            total = jnp.sum(head(x, h), axis=1, keepdims=True)
            corr[h] = jnp.broadcast_to(total, (CH, TILE))
            norm[h] = jnp.where(left, pair, turned) if h == 0 else jnp.where(left, turned, pair)
        dq[rows, :] = jnp.zeros((CH, TILE), f4)

    def both_heads(first, second):
        return jnp.where(left, first, second)

    def grad_start(ic, jc):
        rows, cols = chunk_of(ic), chunk_of(jc)
        da = da_ref[rows, :]
        values = vr[cols, :]
        return [dot(head(da, h), values, NT) for h in range(2)]

    def grad_scores(ic, jc, dps):
        rows, cols = chunk_of(ic), chunk_of(jc)
        parts = []
        for h in range(2):
            p = p_ref[h, rows, cols]
            d, iv = corr[h], norm[h]
            parts.append(
                [
                    (
                        p[:, t * TILE : (t + 1) * TILE].astype(f4)
                        * ((dps[h][:, t * TILE : (t + 1) * TILE] - d) * iv)
                    ).astype(bf)
                    for t in range(2)
                ]
            )
        return parts

    def grad_skew(ic, jc, parts, ws, wt):
        for h in range(2):
            for t in range(2):
                for s in range(2):
                    sr = slice(s * TILE, (s + 1) * TILE)
                    ws[h, tile_of(2 * ic + s), tile_of(2 * jc + 2 + t)] = pltpu.roll(
                        parts[h][t][sr], 0, 1, stride=1, stride_axis=0
                    )
                    wt[h, tile_of(2 * jc + t), tile_of(2 * ic + 2 + s)] = pltpu.roll(
                        parts[h][t][sr].T, 1, 1, stride=1, stride_axis=0
                    )

    def grad_values(ic, jc, dvt):
        rows, cols = chunk_of(ic), chunk_of(jc)
        for h in range(2):
            half = slice(h * 64, (h + 1) * 64)
            dvt[half, cols] += dot(dat[half, rows], p_ref[h, rows, cols])

    def grad_out(ic, jc, parts, dq, dkt, qt):
        rows, cols = chunk_of(ic), chunk_of(jc)
        keys = kr[cols, :]
        whole = [jnp.concatenate(parts[h], axis=1) for h in range(2)]
        dq[rows, :] += both_heads(dot(whole[0], keys), dot(whole[1], keys))
        for h in range(2):
            half = slice(h * 64, (h + 1) * 64)
            dkt[half, cols] += dot(qt[half, rows], whole[h])

    def fold(ic, slot, first, ws, wt, qt, kt, gk, gq):
        rows = chunk_of(ic)
        w = chunk_of(jnp.clip(slot + 3 - ic, 1, NEAR) - 1)
        for ref, mask, table, out, turned, g in (
            (ws, late, rkr, dq2, qt, gk),
            (wt, early, rq_ref, dk2, kt, gq),
        ):
            rels = table[w, :]
            outs = []
            for h in range(2):
                band = []
                for s in range(2):
                    line = []
                    for b in range(2):
                        spot = 2 * slot + s + b
                        x = ref[h, tile_of(2 * ic + s), tile_of(spot)]
                        y = ref[h, tile_of(2 * ic + s), tile_of(spot + 1)]
                        line.append(jnp.where(mask, x, y))
                    band.append(jnp.concatenate(line, axis=1))
                band = jnp.concatenate(band, axis=0)
                outs.append(dot(band, rels))
                half = slice(h * 64, (h + 1) * 64)
                g[half, w] += dot(turned[half, rows], band)
            if first:
                out[rows, :] = both_heads(*outs)
            else:
                out[rows, :] += both_heads(*outs)

    def close(ic, dq, dkt, dvt):
        rows = chunk_of(ic)
        dqk_ref[rows, :TILE] = ((dq[rows, :] + dq2[rows, :]) * SCALE).astype(bf)
        for t in range(2):
            tr = tile_of(2 * ic + t)
            x = ((dkt[:, tr].T + dk2[tr, :]) * SCALE).astype(bf)
            dqk_ref[tr, TILE:] = dot(rev, x).astype(bf)
            dv_ref[tr, :] = dot(rev, dvt[:, tr].T.astype(bf)).astype(bf)
        dkt[:, rows] = jnp.zeros((TILE, CH), f4)
        dvt[:, rows] = jnp.zeros((TILE, CH), f4)

    def flush(gk, gq):
        g_ref[:TILE, :] = (gq[...] * SCALE).astype(bf)
        for t in range(NEAR * CH // TILE):
            cols = slice(t * TILE, (t + 1) * TILE)
            g_ref[TILE:, cols] = dot((gk[:, cols] * SCALE).astype(bf), rev).astype(bf)

    def sweep(before, body, idle):
        def chunk(ic, _):
            lo = b_ref[2 * NCH + ic]
            hi = b_ref[3 * NCH + ic]

            @pl.when(hi > lo)
            def _():
                before(ic, lo, hi)

            @pl.when(hi <= lo)
            def _():
                idle(ic)

            def block(jc, _):
                body(ic, jc)
                return 0

            lax.fori_loop(lo, hi, block, 0)
            return 0

        lax.fori_loop(0, NCH, chunk, 0)

    def no_fold(ic):
        dq2[chunk_of(ic), :] = jnp.zeros((CH, TILE), f4)
        dk2[chunk_of(ic), :] = jnp.zeros((CH, TILE), f4)

    def no_grad(ic, dq):
        dq[chunk_of(ic), :] = jnp.zeros((CH, TILE), f4)

    def fused(new, old):
        ws, wt, dq, dkt, dvt, qt, kt, gk_next, gq_next = new
        ws_, wt_, dq_, dkt_, dvt_, qt_, kt_, gk, gq = old
        prepare(qt, kt)
        turn_table()

        def before(ic, lo, hi):
            @pl.when(step < 2)
            def _():
                pads(ic, lo, hi, ws, wt)

            fold(ic, lo, True, ws_, wt_, qt_, kt_, gk, gq)
            open_grad(ic, dq)

        def body(ic, jc):
            dps = grad_start(ic, jc)
            fold(ic, jc + 1, False, ws_, wt_, qt_, kt_, gk, gq)
            grad_values(ic, jc, dvt)
            parts = grad_scores(ic, jc, dps)
            grad_skew(ic, jc, parts, ws, wt)
            grad_out(ic, jc, parts, dq, dkt, qt)

        def idle(ic):
            no_fold(ic)
            no_grad(ic, dq)

        sweep(before, body, idle)

        def finish(ic, _):
            close(ic, dq_, dkt_, dvt_)
            return 0

        lax.fori_loop(0, NCH, finish, 0)
        flush(gk, gq)
        clear(gk, gq)

    set0 = (ws0, wt0, dq0, dkt0, dvt0, qt0, kt0, gk0, gq0)
    set1 = (ws1, wt1, dq1, dkt1, dvt1, qt1, kt1, gk1, gq1)

    @pl.when(step == 0)
    def _():
        clear(dkt0, dkt1, dvt0, dvt1, gk0, gk1, gq0, gq1)
        prepare(qt0, kt0)

        def before(ic, lo, hi):
            pads(ic, lo, hi, ws0, wt0)
            open_grad(ic, dq0)

        def body(ic, jc):
            parts = grad_scores(ic, jc, grad_start(ic, jc))
            grad_values(ic, jc, dvt0)
            grad_skew(ic, jc, parts, ws0, wt0)
            grad_out(ic, jc, parts, dq0, dkt0, qt0)

        sweep(before, body, lambda ic: no_grad(ic, dq0))

    @pl.when((step > 0) & (step < last) & (step % 2 == 1))
    def _():
        fused(set1, set0)

    @pl.when((step > 0) & (step < last) & (step % 2 == 0))
    def _():
        fused(set0, set1)

    @pl.when(step == last)
    def _():
        turn_table()
        sweep(
            lambda ic, lo, hi: fold(ic, lo, True, ws1, wt1, qt1, kt1, gk1, gq1),
            lambda ic, jc: fold(ic, jc + 1, False, ws1, wt1, qt1, kt1, gk1, gq1),
            no_fold,
        )

        def finish(ic, _):
            close(ic, dq1, dkt1, dvt1)
            return 0

        lax.fori_loop(0, NCH, finish, 0)
        flush(gk1, gq1)


def attend_backward(bounds, both, v, da, att, inv, spread, p):
    pairs = v.shape[1] // TILE

    def col(n, lag, at=0, every=1):
        return pl.BlockSpec(
            (n, TILE), lambda s, *_: (0, at + every * jnp.clip(s - lag, 0, pairs - 1))
        )

    def out(at):
        return lambda s, *_: (jnp.clip(s - 1, 0, pairs - 1), 0)[:: 1 - 2 * at]

    def twice(shape, dtype):
        return [pltpu.VMEM(shape, dtype)] * 2

    return pl.pallas_call(
        bwd_kernel,
        grid_spec=pltpu.PrefetchScalarGridSpec(
            num_scalar_prefetch=1,
            grid=(pairs + 1,),
            in_specs=[
                col(LEN, 0, 0, 2),
                col(LEN, 0, 1, 2),
                col(LEN, 0),
                col(LEN, 0),
                col(LEN, 0),
                col(LEN, 0),
                pl.BlockSpec((2, LEN, LEN), lambda s, *_: (jnp.minimum(s, pairs - 1), 0, 0)),
                col(NEAR * CH, 1, 1, 2),
                col(NEAR * CH, 1, 0, 2),
            ],
            out_specs=[
                pl.BlockSpec((LEN, 2 * TILE), out(1)),
                col(LEN, 1),
                pl.BlockSpec((2 * TILE, NEAR * CH), out(0)),
            ],
            scratch_shapes=twice((2, LEN, LEN + 2 * CH), bf)
            + twice((2, LEN, LEN + 2 * CH), bf)
            + twice((LEN, TILE), f4)
            + twice((TILE, LEN), f4)
            + twice((TILE, LEN), f4)
            + twice((TILE, LEN), bf)
            + twice((TILE, LEN), bf)
            + twice((TILE, NEAR * CH), f4)
            + twice((TILE, NEAR * CH), f4)
            + [pltpu.VMEM((TILE, LEN), bf)]
            + [pltpu.VMEM((LEN, TILE), bf)] * 2
            + [pltpu.VMEM((NEAR * CH, TILE), bf)]
            + [pltpu.VMEM((LEN, TILE), f4)] * 2
            + [pltpu.VMEM((2, CH, TILE), f4)] * 2,
        ),
        out_shape=[
            jax.ShapeDtypeStruct(both.shape, bf),
            jax.ShapeDtypeStruct(v.shape, bf),
            jax.ShapeDtypeStruct((both.shape[1], NEAR * CH), bf),
        ],
        compiler_params=pltpu.CompilerParams(vmem_limit_bytes=60 << 20),
        name="attend_backward",
    )(bounds, both, both, v, da, att, inv, p, spread, spread)


def gelu_pair(u):
    size = jnp.abs(u)
    bell = jnp.exp2(u * u * (-0.5 * math.log2(math.e)))
    t = 1.0 / (1.0 + (0.3275911 / math.sqrt(2.0)) * size)
    poly = 0.5 * 1.061405429
    for c in (-1.453152027, 1.421413741, -0.284496736, 0.254829592):
        poly = poly * t + 0.5 * c
    tail = poly * t * bell
    phi = jnp.where(u < 0.0, tail, 1.0 - tail)
    return u * phi, phi + u * bell * (1.0 / math.sqrt(2.0 * math.pi))


def middle_kernel(
    hid_ref, att_ref, wo_ref, we_ref, wc_ref, vec_ref, mask_ref, cot_ref,
    out_ref, dfirst_ref, datt_ref, grad_ref,
    pre, slope, acc, norm_, act, dexp, low, dtwo, dbranch, attended, turned, sums,
):
    step = pl.program_id(0)
    blocks = act.shape[0] // TOK
    parts = act.shape[1] // low.shape[1]

    @pl.when(step < blocks)
    def _():
        rows = pl.ds(al(step * TOK, TOK), TOK)
        views = [ref.at[rows] for ref in (act, dexp, low, dtwo, dbranch, attended)]
        token_block(
            step, hid_ref, att_ref, wo_ref, we_ref, wc_ref, vec_ref, mask_ref, cot_ref,
            out_ref, dfirst_ref, datt_ref, pre, slope, acc, norm_, sums, *views,
        )

    @pl.when(step >= blocks)
    def _():
        weight_block(
            step - blocks, parts, act, dexp, low, dtwo, dbranch, attended, turned, sums, grad_ref
        )


def token_block(
    step, hid_ref, att_ref, wo_ref, we_ref, wc_ref, vec_ref, mask_ref, cot_ref,
    out_ref, dfirst_ref, datt_ref, pre, slope, acc, norm_, sums,
    act_ref, dexp_ref, low_ref, dtwo_ref, dbranch_ref, attb_ref,
):
    width = hid_ref.shape[1]
    chunks = we_ref.shape[1] // FCH
    vectors = vec_ref[...].astype(f4).T
    gain_one = vectors[0:1, :]
    shift_one = vectors[1:2, :]
    gain_two = vectors[2:3, :]
    shift_two = vectors[3:4, :]
    inv = 1.0 / width
    attb_ref[...] = att_ref[...].astype(bf)
    first = hid_ref[...].astype(f4) + dot(attb_ref[...], wo_ref[...])
    cen = first - jnp.sum(first, axis=1, keepdims=True) * inv
    rstd_one = lax.rsqrt(jnp.sum(cen * cen, axis=1, keepdims=True) * inv + NORM_EPS)
    n_one = cen * rstd_one
    norm_[...] = n_one
    normed = n_one * gain_one + shift_one
    low_ref[...] = normed.astype(bf)
    acc[...] = jnp.zeros(acc.shape, f4)

    def cols(c):
        return slice(c * FCH, (c + 1) * FCH)

    def expand(c):
        pre[c % 2] = dot(low_ref[...], we_ref[:, cols(c)])

    def bend(c):
        value, grad = gelu_pair(pre[c % 2])
        act_ref[:, cols(c)] = value.astype(bf)
        slope[:, cols(c)] = grad.astype(bf)

    def contract(c):
        acc[...] += dot(act_ref[:, cols(c)], wc_ref[:, cols(c)])

    expand(0)
    expand(1)
    bend(0)

    def steady(c, _):
        expand(c + 1)
        bend(c)
        contract(c - 1)
        return 0

    for c in range(1, chunks - 1):
        steady(c, 0)
    bend(chunks - 1)
    contract(chunks - 2)
    contract(chunks - 1)
    branch = acc[...]
    turned = [
        jnp.broadcast_to(mask_ref[:, t : t + TILE].astype(f4), (TILE, TILE)).T
        for t in range(0, TOK, TILE)
    ]
    mask = jnp.concatenate(turned, axis=0)[:, 0:1]
    normed = norm_[...] * gain_one + shift_one
    second = normed + branch
    row_res = jnp.sum(mask * second * second, axis=0, keepdims=True)
    row_sub = jnp.sum(mask * branch * branch, axis=0, keepdims=True)
    cen = second - jnp.sum(second, axis=1, keepdims=True) * inv
    rstd = lax.rsqrt(jnp.sum(cen * cen, axis=1, keepdims=True) * inv + NORM_EPS)
    n_two = cen * rstd
    out_ref[...] = (n_two * gain_two + shift_two).astype(bf)
    up = cot_ref[...].astype(f4) * mask
    row_g2 = jnp.sum(up * n_two, axis=0, keepdims=True)
    row_s2 = jnp.sum(up, axis=0, keepdims=True)
    g = up * gain_two
    d_second = (
        g
        - jnp.sum(g, axis=1, keepdims=True) * inv
        - n_two * (jnp.sum(g * n_two, axis=1, keepdims=True) * inv)
    ) * rstd
    dtwo_ref[...] = d_second.astype(bf)
    acc[...] = d_second

    def back(c):
        grad = dot(dtwo_ref[...], wc_ref[:, cols(c)], NT) * slope[:, cols(c)].astype(f4)
        dexp_ref[:, cols(c)] = grad.astype(bf)

    def into(c):
        acc[...] += dot(dexp_ref[:, cols(c)], we_ref[:, cols(c)], NT)

    back(0)

    def steady_back(c, _):
        back(c)
        into(c - 1)
        return 0

    for c in range(1, chunks):
        steady_back(c, 0)
    into(chunks - 1)
    up = acc[...]
    n_one = norm_[...]
    row_g1 = jnp.sum(up * n_one, axis=0, keepdims=True)
    row_s1 = jnp.sum(up, axis=0, keepdims=True)
    g = up * gain_one
    d_first = (
        g
        - jnp.sum(g, axis=1, keepdims=True) * inv
        - n_one * (jnp.sum(g * n_one, axis=1, keepdims=True) * inv)
    ) * rstd_one
    dfirst_ref[...] = d_first
    low = d_first.astype(bf)
    dbranch_ref[...] = low
    datt_ref[...] = dot(low, wo_ref[...], NT).astype(bf)
    rows = jnp.concatenate(
        [row_g1, row_s1, row_g2, row_s2, row_res, row_sub, jnp.zeros((2, width), f4)], axis=0
    )

    @pl.when(step == 0)
    def _():
        sums[...] = rows

    @pl.when(step > 0)
    def _():
        sums[...] += rows


def weight_block(
    step, parts, act, dexp, low, dtwo, dbranch, attended, turned, sums, out_ref
):
    width = low.shape[1]

    @pl.when(step == 0)
    def _():
        turned[...] = low[...].T

    @pl.when(step < parts)
    def _():
        cols = pl.ds(al(step * width, width), width)
        out_ref[...] = dot(turned[...], dexp[:, cols]).astype(bf)

    @pl.when((step >= parts) & (step < 2 * parts))
    def _():
        cols = pl.ds(al((step - parts) * width, width), width)
        out_ref[...] = dot(act[:, cols].T, dtwo[...]).astype(bf)

    @pl.when(step == 2 * parts)
    def _():
        out_ref[...] = dot(attended[...].T, dbranch[...]).astype(bf)

    @pl.when(step == 2 * parts + 1)
    def _():
        rows = sums[...]
        total = jnp.broadcast_to(jnp.sum(rows[4:6], axis=1, keepdims=True), (2, width))
        full = jnp.concatenate([rows[:4], total, jnp.zeros((TILE - 6, width), f4)], axis=0)
        out_ref[:, :TILE] = full.T.astype(bf)


def middle(hidden, attended, weights, wide, mask, cotangent):
    tokens, width = hidden.shape
    blocks = tokens // TOK
    parts = wide // width
    tok = lambda n: pl.BlockSpec((TOK, n), lambda i: (jnp.minimum(i, blocks - 1), 0))
    once = lambda n, at: pl.BlockSpec(
        (width, n), lambda i: (0, at // n), pipeline_mode=pl.Buffered(1)
    )
    shape = lambda n, dtype: jax.ShapeDtypeStruct((tokens, n), dtype)
    whole = lambda n: pltpu.VMEM((tokens, n), bf)
    return pl.pallas_call(
        middle_kernel,
        grid=(blocks + 2 * parts + 2,),
        in_specs=[
            tok(width),
            tok(width),
            once(width, 2 * wide),
            once(wide, 0),
            once(wide, wide),
            once(TILE, 2 * wide + width),
            pl.BlockSpec((1, TOK), lambda i: (0, jnp.minimum(i, blocks - 1))),
            tok(width),
        ],
        out_specs=[
            tok(width),
            tok(width),
            tok(width),
            pl.BlockSpec((width, width), lambda i: (0, jnp.maximum(i - blocks, 0))),
        ],
        out_shape=[
            shape(width, bf),
            shape(width, f4),
            shape(width, bf),
            jax.ShapeDtypeStruct((width, 2 * wide + width + TILE), bf),
        ],
        scratch_shapes=[
            pltpu.VMEM((2, TOK, FCH), f4),
            pltpu.VMEM((TOK, wide), bf),
            pltpu.VMEM((TOK, width), f4),
            pltpu.VMEM((TOK, width), f4),
            whole(wide),
            whole(wide),
            whole(width),
            whole(width),
            whole(width),
            whole(width),
            pltpu.VMEM((width, tokens), bf),
            pltpu.VMEM((8, width), f4),
        ],
        compiler_params=pltpu.CompilerParams(vmem_limit_bytes=60 << 20),
        name="middle",
    )(hidden, attended, weights, weights, weights, weights, mask, cotangent)


def lane_pieces(size, count, parts, per, forward):
    found = [[] for _ in range(size // TILE)]
    for device in range(count):
        for part in range(parts):
            source = (device * parts + part) * per
            target = part * count * per + device * per
            if not forward:
                source, target = target, source
            done = 0
            while done < per:
                at, to = source + done, target + done
                span = min(per - done, TILE - at % TILE, TILE - to % TILE)
                found[to // TILE].append((at // TILE, at % TILE, to % TILE, span))
                done += span
    return found


def permute_lanes(load, store, rows, pieces):
    lane = lax.broadcasted_iota(jnp.int32, (rows, TILE), 1)
    for block, group in enumerate(pieces):
        total = jnp.zeros((rows, TILE), f4)
        for at, offset, spot, span in group:
            moved = load(at)
            if spot != offset:
                moved = pltpu.roll(moved, (spot - offset) % TILE, 1)
            total = jnp.where((lane >= spot) & (lane < spot + span), moved, total)
        store(block, total)


def lanes(block):
    return slice(block * TILE, (block + 1) * TILE)


def pack_kernel(
    count, query_ref, key_ref, table_ref, expand_ref, contract_ref, output_ref,
    small_ref, first_ref, out_ref,
):
    per, wide = expand_ref.shape
    width = output_ref.shape[1]
    parts = wide // width
    half = table_ref.shape[0] // 2
    table = table_ref[...].astype(f4)
    table = jnp.concatenate([table[:half], table[half:]], axis=1)
    for block in range(width // TILE):
        for spot, ref in enumerate((query_ref, key_ref)):
            at = lanes(2 * block + spot)
            rows = jnp.concatenate([ref[:, lanes(block)].astype(f4), table[:, at]], axis=0)
            first_ref[:, at] = rows.astype(bf)

    def store(block, value):
        out_ref[:, lanes(block)] = value.astype(bf)

    permute_lanes(
        lambda at: expand_ref[:, lanes(at)].astype(f4),
        store,
        per,
        lane_pieces(wide, count, parts, per, True),
    )
    rows = contract_ref[...].astype(f4)
    for part in range(parts):
        at = wide + part * width
        out_ref[:, at : at + width] = rows[part * per : (part + 1) * per].astype(bf)
    out_ref[:, 2 * wide : 2 * wide + width] = output_ref[...]
    out_ref[:, 2 * wide + width :] = small_ref[...]


def pack_weights(count, query, key, table, expand, contract, output, small):
    per, wide = expand.shape
    width = output.shape[1]
    shape = lambda a, b: jax.ShapeDtypeStruct((a, b), bf)
    return pl.pallas_call(
        partial(pack_kernel, count),
        out_shape=[
            shape(per + table.shape[0] // 2, 2 * width),
            shape(per, 2 * wide + width + TILE),
        ],
        name="pack_weights",
    )(query, key, table, expand, contract, output, small)


def finish_kernel(count, cells, own_ref, expand_ref, contract_ref, output_ref, *rest):
    per, wide = expand_ref.shape
    width = output_ref.shape[1]
    parts = wide // width

    def store(block, value):
        expand_ref[:, lanes(block)] = value

    permute_lanes(
        lambda at: own_ref[:, lanes(at)].astype(f4),
        store,
        per,
        lane_pieces(wide, count, parts, per, False),
    )
    for part in range(parts):
        at = wide + part * width
        contract_ref[part * per : (part + 1) * per, :] = own_ref[:, at : at + width].astype(f4)
    output_ref[...] = own_ref[:, 2 * wide : 2 * wide + width].astype(f4)
    turned = own_ref[:, 2 * wide + width :].astype(f4).T
    for number, ref in enumerate(rest[:4]):
        ref[...] = turned[number : number + 1, :]
    for number, ref in enumerate(rest[4:]):
        ref[...] = jnp.sqrt(turned[4 + number : 5 + number, :1] * (1.0 / cells))


def finish_grads(count, cells, own, wide, width):
    per = own.shape[0]
    shape = lambda a, b: jax.ShapeDtypeStruct((a, b), f4)
    return pl.pallas_call(
        partial(finish_kernel, count, cells),
        out_shape=[
            shape(per, wide),
            shape(per * (wide // width), width),
            shape(per, width),
            *[shape(1, per)] * 4,
            *[shape(1, 1)] * 2,
        ],
        name="finish_grads",
    )(own)


def digits(count):
    found = [(1, 2)]
    stride = 2
    while stride < count:
        radix = 4 if count // stride >= 4 else 2
        found.append((stride, radix))
        stride *= radix
    return found


def place(relative, count):
    spot = relative * 0
    for stride, radix in digits(count):
        spot = spot * radix + ((relative >> (stride.bit_length() - 1)) & (radix - 1))
    return spot


def mixing(size, count, me):
    per = size // count
    row = np.arange(size)
    target = place(jnp.asarray(row // per, jnp.int32) ^ me, count) * per + (row % per)
    spots = lax.broadcasted_iota(jnp.int32, (size, size), 1)
    return (target[:, None] == spots).astype(bf)


def near_index():
    index = bucket_index(LEN - np.arange(2 * LEN), BUCKETS).reshape(-1, CH)
    assert (index[:2] == index[0, 0]).all() and (index[-2:] == index[-1, -1]).all()
    return index[1:-1].reshape(-1)


def offset_rows(count, me):
    index = near_index()
    size = 2 * BUCKETS
    per = size // count
    target = place(jnp.asarray(index // per, jnp.int32) ^ me, count) * per + (index % per)
    spots = lax.broadcasted_iota(jnp.int32, (index.shape[0], size), 1)
    return (target[:, None] == spots).astype(bf)


def swap(value, offset, count):
    return lax.ppermute(value, "fsdp", [(i, i ^ offset) for i in range(count)])


def together(values):
    return list(lax.optimization_barrier(tuple(values)))


def gather_pair(first, second, count, beside, work):
    middle = digits(count)[1:]
    one, two = first[None], second[None]
    later = None
    for (stride_a, radix_a), (stride_b, radix_b) in zip(middle[::-1], middle):
        got_a = [one]
        got_b = [two]
        for step in range(1, max(radix_a, radix_b)):
            if step < radix_a:
                got_a.append(swap(one, step * stride_a, count))
            if step < radix_b:
                got_b.append(swap(two, step * stride_b, count))
        one, two, *beside = together(
            [jnp.concatenate(got_a, axis=0), jnp.concatenate(got_b, axis=0), *beside]
        )
        if later is None:
            later, beside = beside[0], work(beside[1])
    radices = [radix for _, radix in middle[::-1]]
    two = two.reshape(*radices, *second.shape)
    turn = tuple(range(len(middle)))[::-1]
    two = two.transpose(turn + (len(middle), len(middle) + 1)).reshape(-1, *second.shape)
    return (one, swap(one, 1, count)), (two, swap(two, 1, count)), later, beside


def scatter_pair(first, second, count, beside):
    middle = digits(count)[1:]
    radices = [radix for _, radix in middle]
    shape_a, shape_b = first.shape[1:], second.shape[1:]
    half_a = first.reshape(2, -1, *shape_a)
    half_b = second.reshape(2, -1, *shape_b)
    one, two = together(
        [
            half_a[0].astype(f4) + swap(half_a[1], 1, count).astype(f4),
            half_b[0].astype(f4) + swap(half_b[1], 1, count).astype(f4),
        ]
    )
    one = one.astype(bf).reshape(*radices, *shape_a)
    two = two.astype(bf).reshape(*radices, *shape_b)
    for step, ((stride_a, radix_a), (stride_b, radix_b)) in enumerate(zip(middle, middle[::-1])):
        last = two.ndim - 3
        got_a = []
        got_b = []
        for hop in range(1, max(radix_a, radix_b)):
            if hop < radix_a:
                got_a.append(swap(one[hop], hop * stride_a, count))
            if hop < radix_b:
                got_b.append(
                    swap(lax.index_in_dim(two, hop, last, keepdims=False), hop * stride_b, count)
                )
        sum_a = one[0].astype(f4)
        sum_b = lax.index_in_dim(two, 0, last, keepdims=False).astype(f4)
        if step == 0:
            *got, beside = together(got_a + got_b + [beside])
        else:
            got = together(got_a + got_b)
        for piece in got[: len(got_a)]:
            sum_a = sum_a + piece.astype(f4)
        for piece in got[len(got_a) :]:
            sum_b = sum_b + piece.astype(f4)
        if step == len(middle) - 1:
            return sum_a, sum_b, beside
        one, two = sum_a.astype(bf), sum_b.astype(bf)


def active_chunks(segment, valid):
    rows = segment.reshape(NCH, CH)
    ok = valid.reshape(NCH, CH) > 0
    first = rows[:, 0]
    last = rows[:, -1]
    over = (first[None, :] <= last[:, None]) & (last[None, :] >= first[:, None])
    real = jnp.max(jnp.where(ok, rows, -1), axis=1)
    back = (first[None, :] <= real[:, None]) & (last[None, :] >= first[:, None])
    back = back | back.T
    place_ = jnp.arange(NCH)[None, :]

    def limits(mask):
        lo = jnp.min(jnp.where(mask, place_, NCH), axis=1)
        hi = jnp.max(jnp.where(mask, place_ + 1, 0), axis=1)
        return jnp.where(hi > 0, lo, 0), hi

    return jnp.concatenate(limits(over) + limits(back)).astype(jnp.int32)


def mm(left, right, dims=NN):
    return lax.dot_general(left, right, dims, preferred_element_type=f4)


def shards(
    hidden,
    query_weight,
    key_weight,
    value_weight,
    output_weight,
    relative_table,
    first_gain,
    first_shift,
    expand_weight,
    contract_weight,
    second_gain,
    second_shift,
    segment_ids,
    valid,
    cotangent,
):
    count = lax.axis_size("fsdp")
    me = lax.axis_index("fsdp")
    width = hidden.shape[1]
    wide = expand_weight.shape[1]
    per = query_weight.shape[0]
    per_t = relative_table.shape[0]
    per_c = contract_weight.shape[0]
    parts = wide // width

    small = jnp.stack([first_gain, first_shift, second_gain, second_shift], axis=1)
    small = jnp.pad(small, ((0, 0), (0, TILE - 4)))
    first, rest = pack_weights(
        count,
        query_weight,
        key_weight,
        relative_table,
        expand_weight,
        contract_weight,
        output_weight,
        small,
    )

    def aside(number):
        mix = mixing(width, count, number)
        return [
            mix,
            mm(hidden, mix).astype(bf),
            offset_rows(count, number),
            active_chunks(segment_ids, valid),
        ]

    pair_a, pair_b, rest, (mix, hidden_mixed, onehot, bounds) = gather_pair(
        first, value_weight, count, [rest, me], aside
    )
    query_key = jnp.concatenate([x[:, :per] for x in pair_a], axis=0)
    query_key = query_key.reshape(count * per, 2 * width)
    value_full = jnp.concatenate(pair_b, axis=0).reshape(count * per, width)
    table = [
        jnp.concatenate([x[:, per:, :width], x[:, per:, width:]], axis=1) for x in pair_a
    ]
    table = jnp.concatenate(table, axis=0).reshape(count * per_t, width)
    weights = lax.all_gather(rest, "fsdp", axis=0, tiled=True)

    table_mixed = mm(table, mix).astype(bf)
    both_rows = mm(hidden_mixed, query_key).astype(bf)
    value_rows = mm(hidden_mixed, value_full).astype(bf)
    (position,) = together([mm(table_mixed, query_key).astype(bf)])
    spread_rows = mm(onehot, position).astype(bf)
    attended_wide, inverse, probs = attend_forward(
        bounds, both_rows, value_rows, spread_rows, segment_ids[None, :]
    )
    result, d_first, attended_gradient, grads = middle(
        hidden, attended_wide, weights, wide, valid[None, :], cotangent
    )
    owned = lax.psum_scatter(grads, "fsdp", scatter_dimension=0, tiled=True)
    both_low, value_low, offset_grad = attend_backward(
        bounds,
        both_rows,
        value_rows,
        attended_gradient,
        attended_wide,
        inverse,
        spread_rows,
        probs,
    )
    position_low = mm(offset_grad, onehot).astype(bf)
    grad_pack = mm(hidden_mixed, both_low, ROWS_FIRST) + mm(
        table_mixed, position_low, (((0,), (1,)), ((), ()))
    )
    grad_pack = grad_pack.astype(bf).reshape(count, per, 2 * width)
    grad_value = mm(hidden_mixed, value_low, ROWS_FIRST)
    grad_table = mm(position_low, query_key, (((0,), (1,)), ((), ())))
    grad_table = mm(grad_table.astype(bf), mix, NT).astype(bf)
    grad_value = jnp.concatenate(
        [
            grad_value.astype(bf).reshape(count, per, width),
            grad_table.reshape(count, per_t, width),
        ],
        axis=1,
    )
    d_input = mm(both_low, query_key, NT) + mm(value_low, value_full, NT)
    own_pack, own_value, d_input = scatter_pair(grad_pack, grad_value, count, d_input.astype(bf))
    d_input = d_first + mm(d_input, mix, NT)
    cells = float(hidden.shape[0] * count * width)
    expand_owned, contract_owned, output_owned, *last = finish_grads(
        count, cells, owned, wide, width
    )
    own_pack = own_pack.reshape(per, -1, 2, TILE)
    return (
        result,
        d_input.astype(bf),
        own_pack[:, :, 0].reshape(per, width),
        own_pack[:, :, 1].reshape(per, width),
        own_value[:per],
        output_owned,
        own_value[per:],
        last[0].reshape(per),
        last[1].reshape(per),
        expand_owned,
        contract_owned,
        last[2].reshape(per),
        last[3].reshape(per),
        last[4].reshape(()),
        last[5].reshape(()),
    )


def solution(mesh):
    in_specs = (
        P("fsdp", None),
        P("fsdp", None),
        P("fsdp", None),
        P("fsdp", None),
        P("fsdp", None),
        P("fsdp", None),
        P("fsdp"),
        P("fsdp"),
        P("fsdp", None),
        P("fsdp", None),
        P("fsdp"),
        P("fsdp"),
        P("fsdp"),
        P("fsdp"),
        P("fsdp", None),
    )
    out_specs = (
        P("fsdp", None),
        P("fsdp", None),
        P("fsdp", None),
        P("fsdp", None),
        P("fsdp", None),
        P("fsdp", None),
        P("fsdp", None),
        P("fsdp"),
        P("fsdp"),
        P("fsdp", None),
        P("fsdp", None),
        P("fsdp"),
        P("fsdp"),
        P(),
        P(),
    )
    return jax.shard_map(shards, mesh=mesh, in_specs=in_specs, out_specs=out_specs, check_vma=False)
```
